32 devices in a mesh: group: 2 (over y), node: 4 (over z), sample: 2 (over x), head: 2 (over core).
Axes of the slice: x: 2, y: 2, z: 4, core: 2. Of those that a mesh axis runs over, the one named last changes fastest.
Arguments:
- mesh_node_state: bfloat16 [4, 2048, 512], P(('group', 'sample'), 'node'), parts along dimension 0, may hold values from -6 to 6
- cotangent: bfloat16 [4, 2048, 512], P(('group', 'sample'), 'node', 'head'), parts along dimension 0, may hold values from -6 to 6
- query_weight: bfloat16 [512, 512], P('node', 'head'), may hold values from -8 to 8
- key_weight: bfloat16 [512, 512], P('node', 'head'), may hold values from -8 to 8
- value_weight: bfloat16 [512, 512], P('node', 'head'), may hold values from -0.25 to 0.25
- output_weight: bfloat16 [512, 512], P('head', 'node'), may hold values from -0.25 to 0.25
- adapter_down_weight: bfloat16 [3, 512, 16], replicated, may hold values from -0.25 to 0.25
- adapter_up_weight: bfloat16 [3, 16, 512], P(None, None, 'head'), may hold values from -1.5 to 1.5
- neighbour_key_blocks: int32 [16, 6], replicated, may hold values from 0 to 15, as said below
- block_node_order: int32 [2048], P('node'), may hold values from 0 to 2047, as said below
Outputs:
- mesh_out: bfloat16 [4, 2048, 512], P(('group', 'sample'), 'node', 'head'), parts along dimension 0
- lora_down_grad: float32 [6, 512, 16], P('group'), parts along dimension 0
- lora_up_grad: float32 [6, 16, 512], P('group', None, 'head'), parts along dimension 0
The draws below stay inside these ranges and needn't reach their ends.
There are 2 independent parts, one for each index of `group`. The reference program is written for one: setup_inputs(seed, part) draws one part's arguments, and reference() takes and returns one part's arrays. A program takes and returns all parts, laid end to end along the dimension named above; an argument that names none is the same for every part. Nothing has to cross between parts.
Inputs may be any that keep to these rules, and one draw needn't show every extreme that they name: `neighbour_key_blocks`: row b starts with b itself; every entry lies within 4 of b; entries may repeat. `block_node_order`: A permutation that maps each aligned range of 512 positions onto the same range of nodes.
All inputs are finite; a program needn't handle non-finite values.
Results may differ from the reference program's by a relative error of at most 0.011.
Values may be sent and summed in bfloat16 or wider, within the bound.
No kernel may reach another device: no remote copies, remote signals or barrier semaphores. Data moves between devices by JAX's collectives and lax.ppermute only.
A program may use at most 64 MiB of HBM per device.

```python
import math
import jax
import jax.numpy as jnp
from jax import lax

LATENT_WIDTH = 512
H = 4
DH = 128
ADAPTER_RANK = 16
BLK = 128
HB = 4
NBR = 6
NODE_DEV = 512
S = 2
NODES = 2048
NBLK = 16


def draw_query_weight(key, part):
    key = jax.random.fold_in(key, 11)
    values = jax.random.normal(key, (LATENT_WIDTH, LATENT_WIDTH), jnp.float32)
    return jnp.clip(values / math.sqrt(LATENT_WIDTH), -8.0, 8.0).astype(jnp.bfloat16)


def draw_key_weight(key, part):
    key = jax.random.fold_in(key, 13)
    fresh_noise = jax.random.normal(key, (LATENT_WIDTH, LATENT_WIDTH), jnp.float32)
    values = fresh_noise
    return jnp.clip(values / math.sqrt(LATENT_WIDTH), -8.0, 8.0).astype(jnp.bfloat16)


def draw_neighbour_key_blocks(key, part):
    key = jax.random.fold_in(key, 5)
    own_block = jnp.arange(NBLK, dtype=jnp.int32)[:, None]
    step_sizes = jax.random.randint(key, (NBLK, NBR - 1), -HB, HB + 1)
    nearby = jnp.clip(own_block + step_sizes, 0, NBLK - 1)
    return jnp.concatenate([own_block, nearby], axis=1).astype(jnp.int32)


def draw_block_node_order(key, part):
    key = jax.random.fold_in(key, 7)
    random_ranks = jax.random.randint(key, (NODES // NODE_DEV, NODE_DEV), 0, 16384)
    scores = random_ranks * NODE_DEV + jnp.arange(NODE_DEV, dtype=jnp.int32)[None, :]
    sorted_order = jnp.argsort(scores, axis=1, stable=True).astype(jnp.int32)
    offsets = (jnp.arange(NODES // NODE_DEV, dtype=jnp.int32) * NODE_DEV)[:, None]
    return (sorted_order + offsets).reshape(NODES).astype(jnp.int32)


def levels(key, extent, cuts, smallest, high):
    factor_of = 1.0
    for axis_at, blocks in cuts:
        draws = jax.random.uniform(jax.random.fold_in(jax.random.fold_in(key, 6), axis_at), (blocks,), jnp.float32, smallest / len(cuts), high / len(cuts))
        factor_of = factor_of * jnp.repeat(jnp.exp(draws), extent[axis_at] // blocks).reshape((-1,) + (1,) * (len(extent) - 1 - axis_at))
    return factor_of


def gaussian(key, extent, deviation, most, pieces=(), held_as=jnp.bfloat16):
    entries = jax.random.normal(key, extent, jnp.float32) * deviation
    if len(pieces) > 0:
        entries = levels(key, extent, pieces, -0.22, 0.18) * entries
    return jnp.clip(entries, min=-most, max=most).astype(held_as)


def setup_inputs(seed: int = 0, part: int = 0) -> dict:
    splits = jax.random.split(jax.random.key(seed), 11)
    part_keys = jax.random.split(jax.random.fold_in(splits[10], part), 11)
    mesh_node_state = gaussian(part_keys[0], (S, NODES, LATENT_WIDTH), 1.0, 6.0, ((0, 2), (1, 4)))
    cotangent = gaussian(part_keys[1], (S, NODES, LATENT_WIDTH), 1.0, 6.0, ((0, 2), (1, 4), (2, 2)))
    query_weight = draw_query_weight(jax.random.fold_in(splits[10], 71), part)
    key_weight = draw_key_weight(jax.random.fold_in(splits[10], 71), part)
    value_weight = gaussian(splits[4], (LATENT_WIDTH, LATENT_WIDTH), LATENT_WIDTH ** -0.5, 0.25, ((0, 4), (1, 2)))
    output_weight = gaussian(splits[5], (LATENT_WIDTH, LATENT_WIDTH), LATENT_WIDTH ** -0.5, 0.25, ((0, 2), (1, 4)))
    adapter_down_weight = gaussian(splits[6], (3, LATENT_WIDTH, ADAPTER_RANK), LATENT_WIDTH ** -0.5, 0.25)
    adapter_up_weight = gaussian(splits[7], (3, ADAPTER_RANK, LATENT_WIDTH), ADAPTER_RANK ** -0.5, 1.5, ((2, 2),))
    neighbour_key_blocks = draw_neighbour_key_blocks(jax.random.fold_in(splits[10], 71), part)
    block_node_order = draw_block_node_order(jax.random.fold_in(splits[10], 71), part)
    return {"mesh_node_state": mesh_node_state, "cotangent": cotangent, "query_weight": query_weight, "key_weight": key_weight, "value_weight": value_weight, "output_weight": output_weight, "adapter_down_weight": adapter_down_weight, "adapter_up_weight": adapter_up_weight, "neighbour_key_blocks": neighbour_key_blocks, "block_node_order": block_node_order}


adapter_scale = 0.5
masked_value = -1e+30

def settle(values):
    return lax.optimization_barrier(values.astype(jnp.bfloat16))

def norm_rows(values):
    widened = values.astype(jnp.float32)
    center = widened - lax.optimization_barrier(jnp.mean(widened, axis=-1, keepdims=True))
    spread = lax.optimization_barrier(jnp.mean(center * center, axis=-1, keepdims=True))
    return (center * lax.rsqrt(spread + 1e-05)).astype(jnp.bfloat16)

def block_allowed(table_rows):
    block_ids = jnp.arange(table_rows.shape[0], dtype=jnp.int32)
    targets = block_ids[:, None] + jnp.arange(2 * HB + 1, dtype=jnp.int32)[None, :] - HB
    return jnp.any(table_rows[:, :, None] == targets[:, None, :], axis=1)

def windows(blocks, block_count):
    padded = jnp.pad(blocks, ((HB, HB), (0, 0), (0, 0)))
    return jnp.stack([padded[offset:offset + block_count] for offset in range(2 * HB + 1)], axis=1)

def fold_windows(tiles, block_count):
    extended = jnp.zeros((block_count + 2 * HB,) + tiles.shape[2:], jnp.float32)
    for offset in range(2 * HB + 1):
        extended = extended.at[offset:offset + block_count].add(tiles[:, offset])
    return extended[HB:HB + block_count].astype(jnp.bfloat16)

def head_pass(query_tiles, key_tiles, value_tiles, grad_tiles, allowed):
    block_count = query_tiles.shape[0]
    inverse_root = 1.0 / math.sqrt(DH)
    query_wide = query_tiles.astype(jnp.float32)
    grad_wide = grad_tiles.astype(jnp.float32)
    key_window = windows(key_tiles, block_count).astype(jnp.float32)
    value_window = windows(value_tiles, block_count).astype(jnp.float32)
    scores = jnp.einsum('ibd,iokd->ibok', query_wide, key_window) * inverse_root
    scores = jnp.where(allowed[:, None, :, None], scores, masked_value)
    row_max = lax.optimization_barrier(jnp.max(scores, axis=(2, 3), keepdims=True))
    log_total = row_max + jnp.log(lax.optimization_barrier(jnp.sum(jnp.exp(scores - row_max), axis=(2, 3), keepdims=True)))
    prob_wide = jnp.exp(scores - log_total)
    prob_narrow = settle(prob_wide).astype(jnp.float32)
    attended = settle(jnp.einsum('ibok,iokd->ibd', prob_narrow, value_window))
    row_delta = lax.optimization_barrier(jnp.sum(grad_wide * attended.astype(jnp.float32), axis=-1))
    prob_grad = jnp.einsum('ibd,iokd->ibok', grad_wide, value_window)
    score_grad = settle(prob_wide * (prob_grad - row_delta[:, :, None, None]) * inverse_root).astype(jnp.float32)
    query_grad = jnp.einsum('ibok,iokd->ibd', score_grad, key_window).astype(jnp.bfloat16)
    key_part = jnp.einsum('ibok,ibd->iokd', score_grad, query_wide)
    value_part = jnp.einsum('ibok,ibd->iokd', prob_narrow, grad_wide)
    return (attended, query_grad, fold_windows(key_part, block_count), fold_windows(value_part, block_count))

def reference(mesh_node_state, cotangent, query_weight, key_weight, value_weight, output_weight, adapter_down_weight, adapter_up_weight, neighbour_key_blocks, block_node_order):
    ordered = mesh_node_state[:, block_node_order, :]
    normed = norm_rows(ordered)
    flattened_rows = normed.reshape(-1, LATENT_WIDTH)
    reduced_rank_term = []
    projected = []
    for member_block, weight_matrix in enumerate((query_weight, key_weight, value_weight)):
        reduced_portion = jnp.dot(flattened_rows, adapter_down_weight[member_block], preferred_element_type=jnp.float32).astype(jnp.bfloat16)
        summed_result = jnp.dot(flattened_rows, weight_matrix, preferred_element_type=jnp.float32) + adapter_scale * jnp.dot(reduced_portion, adapter_up_weight[member_block], preferred_element_type=jnp.float32)
        reduced_rank_term.append(reduced_portion)
        projected.append(summed_result.astype(jnp.bfloat16).reshape(S, NODES, LATENT_WIDTH))
    grad_rows = cotangent[:, block_node_order, :].reshape(-1, LATENT_WIDTH)
    att_grad = jnp.dot(grad_rows, output_weight.T, preferred_element_type=jnp.float32).astype(jnp.bfloat16).reshape(S, NODES, LATENT_WIDTH)
    allowed = block_allowed(neighbour_key_blocks)

    def one_head(position):
        sample = position // H
        head_index = position % H

        def head_cols(source):
            picked = lax.dynamic_index_in_dim(source, sample, 0, keepdims=False)
            return lax.dynamic_slice_in_dim(picked, head_index * DH, DH, 1).reshape(NBLK, BLK, DH)
        return head_pass(head_cols(projected[0]), head_cols(projected[1]), head_cols(projected[2]), head_cols(att_grad), allowed)
    results = lax.map(one_head, jnp.arange(S * H, dtype=jnp.int32))

    def join_heads(source):
        return source.reshape(S, H, NODES, DH).transpose(0, 2, 1, 3).reshape(S, NODES, LATENT_WIDTH)
    attended, query_grad, key_grad, value_grad = [join_heads(result) for result in results]
    mixed = jnp.dot(attended.reshape(-1, LATENT_WIDTH), output_weight, preferred_element_type=jnp.float32)
    ordered_out = (ordered.reshape(-1, LATENT_WIDTH).astype(jnp.float32) + mixed).astype(jnp.bfloat16).reshape(S, NODES, LATENT_WIDTH)
    mesh_out = jnp.zeros_like(mesh_node_state).at[:, block_node_order, :].set(ordered_out)
    flattened_wide = flattened_rows.astype(jnp.float32)
    down_gradient_list = []
    up_gradient_list = []
    for member_block, gradient in enumerate((query_grad, key_grad, value_grad)):
        gradient_flattened = gradient.reshape(-1, LATENT_WIDTH)
        backward_term = jnp.dot(gradient_flattened, adapter_up_weight[member_block].T, preferred_element_type=jnp.float32)
        down_gradient_list.append(adapter_scale * jnp.dot(flattened_wide.T, backward_term, precision=lax.Precision.HIGHEST))
        up_gradient_list.append(adapter_scale * jnp.dot(reduced_rank_term[member_block].T, gradient_flattened, preferred_element_type=jnp.float32))
    return (mesh_out, jnp.stack(down_gradient_list), jnp.stack(up_gradient_list))
```

```python
import functools
import math

import jax
import jax.numpy as jnp
from jax import lax
from jax.experimental import pallas as pl
from jax.experimental.pallas import tpu as pltpu
from jax.sharding import PartitionSpec as P

DH = 128
BLK = 128
HB = 4
RANK = 16
LOW = 128

adapter_scale = 0.5
masked_value = -1e30
F32 = jnp.float32
BF16 = jnp.bfloat16


def nn(a, b):
    return lax.dot_general(a, b, (((1,), (0,)), ((), ())), preferred_element_type=F32)


def nt(a, b):
    return lax.dot_general(a, b, (((1,), (1,)), ((), ())), preferred_element_type=F32)


def tn(a, b):
    return lax.dot_general(a, b, (((0,), (0,)), ((), ())), preferred_element_type=F32)


def scatter_matrix(order_ref, rows):
    local = order_ref[...] - lax.axis_index("node") * rows
    nodes = lax.broadcasted_iota(jnp.int32, (rows, rows), 0)
    return jnp.where(nodes == local, 1.0, 0.0).astype(BF16)


def prep_kernel(order_ref, x_ref, cot_ref, normed_ref, half_ref, cot_out_ref):
    rows = x_ref.shape[0]
    place = scatter_matrix(order_ref, rows)
    ordered = tn(place, x_ref[...])
    center = ordered - jnp.mean(ordered, axis=-1, keepdims=True)
    spread = jnp.mean(center * center, axis=-1, keepdims=True)
    normed_ref[...] = (center * lax.rsqrt(spread + 1e-05)).astype(BF16)
    cot_out_ref[...] = tn(place, cot_ref[...]).astype(BF16)
    start = pl.multiple_of(lax.axis_index("head") * (rows // 2), rows // 2)
    half_ref[...] = normed_ref[pl.ds(start, rows // 2), :]


def main_kernel(
    piece_rows,
    table_ref,
    order_ref,
    x_ref,
    normed_ref,
    a_own_ref,
    a_sib_ref,
    b_own_ref,
    b_sib_ref,
    cot_own_ref,
    cot_sib_ref,
    down_ref,
    up_ref,
    *rest,
):
    pieces, outs, scratch = rest[:-14], rest[-14:-11], rest[-11:]
    base_ref, other_ref, lora_ref = outs
    w_ref, kv_ref, low_ref, q_ref, do_ref, dq_ref, att_ref, tk_ref, tv_ref, bk_ref, bv_ref = scratch
    rows, width = normed_ref.shape
    cols = w_ref.shape[1]
    heads = cols // DH
    blocks = rows // BLK
    half = rows // 2
    node, head = lax.axis_index("node"), lax.axis_index("head")
    first = node * blocks
    inverse_root = 1.0 / math.sqrt(DH)

    for piece, (matrix, row) in zip(pieces, piece_rows(node)):
        start = pl.multiple_of(matrix * width + row, piece.shape[0])
        w_ref[pl.ds(start, piece.shape[0]), :] = piece[...]
    wq = w_ref[0:width, :]
    wk = w_ref[width : 2 * width, :]
    wv = w_ref[2 * width : 3 * width, :]

    def out_rows(which):
        start = pl.multiple_of(3 * width + which * (width // 2), width // 2)
        return w_ref[pl.ds(start, width // 2), :]

    mine, theirs = head * half, (1 - head) * half
    segments = [
        (normed_ref, 0),
        (a_own_ref, rows + mine),
        (a_sib_ref, rows + theirs),
        (b_own_ref, 2 * rows + mine),
        (b_sib_ref, 2 * rows + theirs),
    ]
    segments = [(r, s if isinstance(s, int) else pl.multiple_of(s, half)) for r, s in segments]
    for member, start in segments:
        value = member[...]
        low = nn(value, down_ref[...]).astype(BF16)
        span = pl.ds(start, value.shape[0])
        low_ref[span, :] = low
        kv_ref[span, :cols] = (nn(value, wk) + nn(low, up_ref[:, cols : 2 * cols])).astype(BF16)
        kv_ref[span, cols:] = (nn(value, wv) + nn(low, up_ref[:, 2 * cols :])).astype(BF16)
    low_own = low_ref[0:rows, :]
    q_ref[...] = (nn(normed_ref[...], wq) + nn(low_own, up_ref[:, :cols])).astype(BF16)
    do_ref[...] = (
        nn(cot_own_ref[...], out_rows(head)) + nn(cot_sib_ref[...], out_rows(1 - head))
    ).astype(BF16)
    bk_ref[...] = jnp.zeros_like(bk_ref)
    bv_ref[...] = jnp.zeros_like(bv_ref)

    odd = lax.rem(node, 2)
    left, right = 2 - odd, 1 + odd
    for i in range(blocks):
        named = [table_ref[first + i, e] for e in range(table_ref.shape[1])]
        starts, valid = [], []
        for e, c in enumerate(named):
            rel = c - first
            block = jnp.where(
                rel < 0,
                left * blocks + rel + blocks,
                jnp.where(rel >= blocks, (right - 1) * blocks + rel, rel),
            )
            starts.append(pl.multiple_of(block * BLK, BLK))
            fresh = c >= 0
            for before in named[:e]:
                fresh = jnp.logical_and(fresh, c != before)
            valid.append(fresh)
        own = slice(i * BLK, (i + 1) * BLK)
        low_sel = jnp.concatenate([low_ref[pl.ds(s, BLK), :] for s in starts], axis=0)
        for g in range(heads):
            lanes = slice(g * DH, (g + 1) * DH)
            vlanes = slice(cols + g * DH, cols + (g + 1) * DH)
            keys = jnp.concatenate([kv_ref[pl.ds(s, BLK), lanes] for s in starts], axis=0)
            values = jnp.concatenate([kv_ref[pl.ds(s, BLK), vlanes] for s in starts], axis=0)
            query, grad = q_ref[own, lanes], do_ref[own, lanes]
            scores = nt(query, keys) * inverse_root
            scores = jnp.concatenate(
                [
                    jnp.where(ok, scores[:, e * BLK : (e + 1) * BLK], masked_value)
                    for e, ok in enumerate(valid)
                ],
                axis=1,
            )
            row_max = jnp.max(scores, axis=-1, keepdims=True)
            weights = jnp.exp(scores - row_max)
            prob = weights * (1.0 / jnp.sum(weights, axis=-1, keepdims=True))
            prob_b = prob.astype(BF16)
            mixed = nn(prob_b, jnp.concatenate([values, low_sel], axis=1))
            attended = mixed[:, :DH].astype(BF16)
            att_ref[own, lanes] = attended
            tv_ref[own, g * LOW : (g + 1) * LOW] = mixed[:, DH:].astype(BF16)
            delta = jnp.sum(grad.astype(F32) * attended.astype(F32), axis=-1, keepdims=True)
            score_grad = (prob * (nt(grad, values) - delta) * inverse_root).astype(BF16)
            mixed = nn(score_grad, jnp.concatenate([keys, low_sel], axis=1))
            dq_ref[own, lanes] = mixed[:, :DH].astype(BF16)
            tk_ref[own, g * LOW : (g + 1) * LOW] = mixed[:, DH:].astype(BF16)
            up_k = up_ref[RANK : 2 * RANK, cols + g * DH : cols + (g + 1) * DH]
            up_v = up_ref[2 * RANK : 3 * RANK, 2 * cols + g * DH : 2 * cols + (g + 1) * DH]
            back_k = nn(nt(up_k, query).astype(BF16), score_grad)
            back_v = nn(nt(up_v, grad).astype(BF16), prob_b)
            for e, s in enumerate(starts):
                bk_ref[:, pl.ds(s, BLK)] += back_k[:, e * BLK : (e + 1) * BLK]
                bv_ref[:, pl.ds(s, BLK)] += back_v[:, e * BLK : (e + 1) * BLK]

    back_q = nt(up_ref[0:RANK, 0:cols], dq_ref[...])
    lhs = jnp.concatenate([back_q, bk_ref[:, 0:rows], bv_ref[:, 0:rows]], axis=0).astype(BF16)
    down = nn(lhs, normed_ref[...])
    halo = jnp.zeros((2 * RANK, width), F32)
    for member, start in segments[1:]:
        span = pl.ds(start, half)
        lhs = jnp.concatenate([bk_ref[:, span], bv_ref[:, span]], axis=0).astype(BF16)
        halo += nn(lhs, member[...])
    lora_ref[:, :width] = (
        down + jnp.concatenate([jnp.zeros((RANK, width), F32), halo], axis=0)
    ).astype(lora_ref.dtype)
    for g in range(heads):
        lanes = slice(g * DH, (g + 1) * DH)
        tlanes = slice(g * LOW, (g + 1) * LOW)
        grads = jnp.concatenate(
            [
                tn(low_own, dq_ref[:, lanes])[0:RANK],
                tn(tk_ref[:, tlanes], q_ref[:, lanes])[RANK : 2 * RANK],
                tn(tv_ref[:, tlanes], do_ref[:, lanes])[2 * RANK : 3 * RANK],
            ],
            axis=0,
        )
        lora_ref[:, width + g * DH : width + (g + 1) * DH] = (adapter_scale * grads).astype(
            lora_ref.dtype
        )

    place = scatter_matrix(order_ref, rows)
    attended = att_ref[...]
    own_cols = pl.ds(pl.multiple_of(head * cols, cols), cols)
    own_part = nn(place, nt(attended, out_rows(head)).astype(BF16))
    base_ref[...] = x_ref[:, own_cols].astype(F32) + own_part
    other_ref[...] = nn(place, nt(attended, out_rows(1 - head)).astype(BF16)).astype(BF16)


VMEM = pl.BlockSpec(memory_space=pltpu.VMEM)
SMEM = pl.BlockSpec(memory_space=pltpu.SMEM)


def swap(value, axis, step):
    size = lax.axis_size(axis)
    return lax.ppermute(value, axis, [(i, i ^ step) for i in range(size)])


def chain_pairs(size):
    pairs = {0: 0, size - 1: size - 1}
    for i in range(1, size - 1, 2):
        pairs[i], pairs[i + 1] = i + 1, i
    return sorted(pairs.items())


def gather_weights(matrices):
    count = lax.axis_size("node")
    depth = matrices[0].shape[0]
    if count > 4:
        whole = [lax.all_gather(m, "node", axis=0, tiled=True) for m in matrices]
        return whole, lambda node: [(m, 0) for m in range(4)]
    packed = jnp.concatenate(matrices, axis=1)
    pieces = [packed] + [swap(packed, "node", k) for k in range(1, count)]
    cols = matrices[0].shape[1]
    cut = [p[:, m * cols : (m + 1) * cols] for p in pieces for m in range(4)]
    return cut, lambda node: [
        (m, jnp.bitwise_xor(node, k) * depth) for k in range(count) for m in range(4)
    ]


def shards(
    mesh_node_state,
    cotangent,
    query_weight,
    key_weight,
    value_weight,
    output_weight,
    adapter_down_weight,
    adapter_up_weight,
    neighbour_key_blocks,
    block_node_order,
):
    _, rows, width = mesh_node_state.shape
    cols = query_weight.shape[1]
    state = mesh_node_state[0]
    order = block_node_order.reshape(1, rows)

    pieces, piece_rows = gather_weights(
        [query_weight, key_weight, value_weight, output_weight.T]
    )
    down = jnp.concatenate(list(adapter_down_weight), axis=1)
    down = jnp.pad(down, ((0, 0), (0, LOW - 3 * RANK)))
    up = jnp.concatenate(
        [
            jnp.pad(adapter_scale * adapter_up_weight[j], ((j * RANK, LOW - (j + 1) * RANK), (0, 0)))
            for j in range(3)
        ],
        axis=1,
    )
    normed, half, cot_own = pl.pallas_call(
        prep_kernel,
        out_shape=(
            jax.ShapeDtypeStruct((rows, width), BF16),
            jax.ShapeDtypeStruct((rows // 2, width), BF16),
            jax.ShapeDtypeStruct((rows, cols), BF16),
        ),
        in_specs=[VMEM] * 3,
        out_specs=(VMEM,) * 3,
        compiler_params=pltpu.CompilerParams(vmem_limit_bytes=24 * 2**20),
    )(order, state, cotangent[0])
    cot_sib = swap(cot_own, "head", 1)
    a_own = swap(half, "node", 1)
    b_own = lax.ppermute(half, "node", chain_pairs(lax.axis_size("node")))
    a_sib = swap(a_own, "head", 1)
    b_sib = swap(b_own, "head", 1)

    base, other, lora = pl.pallas_call(
        functools.partial(main_kernel, piece_rows),
        out_shape=(
            jax.ShapeDtypeStruct((rows, cols), F32),
            jax.ShapeDtypeStruct((rows, cols), BF16),
            jax.ShapeDtypeStruct((3 * RANK, width + cols), BF16),
        ),
        in_specs=[SMEM] + [VMEM] * (11 + len(pieces)),
        out_specs=(VMEM,) * 3,
        scratch_shapes=[
            pltpu.VMEM((4 * width, cols), BF16),
            pltpu.VMEM((3 * rows, 2 * cols), BF16),
            pltpu.VMEM((3 * rows, LOW), BF16),
            pltpu.VMEM((rows, cols), BF16),
            pltpu.VMEM((rows, cols), BF16),
            pltpu.VMEM((rows, cols), BF16),
            pltpu.VMEM((rows, cols), BF16),
            pltpu.VMEM((rows, cols // DH * LOW), BF16),
            pltpu.VMEM((rows, cols // DH * LOW), BF16),
            pltpu.VMEM((RANK, 3 * rows), F32),
            pltpu.VMEM((RANK, 3 * rows), F32),
        ],
        compiler_params=pltpu.CompilerParams(vmem_limit_bytes=40 * 2**20),
    )(
        neighbour_key_blocks,
        order,
        state,
        normed,
        a_own,
        a_sib,
        b_own,
        b_sib,
        cot_own,
        cot_sib,
        down,
        up,
        *pieces,
    )
    mesh_out = (base + swap(other, "head", 1).astype(F32)).astype(BF16)[None]

    total = lora.astype(F32)
    for axis in ("sample", "node"):
        step = 1
        while step < lax.axis_size(axis):
            sent = total.astype(BF16)
            total = sent.astype(F32) + swap(sent, axis, step).astype(F32)
            step *= 2
    sent = total[:, :width].astype(BF16)
    down_total = sent.astype(F32) + swap(sent, "head", 1).astype(F32)
    down_total = down_total.reshape(3, RANK, width).transpose(0, 2, 1)
    up_total = total[:, width:].reshape(3, RANK, cols)
    return (mesh_out, down_total, up_total)


def solution(mesh):
    in_specs = (
        P(("group", "sample"), "node", None),
        P(("group", "sample"), "node", "head"),
        P("node", "head"),
        P("node", "head"),
        P("node", "head"),
        P("head", "node"),
        P(),
        P(None, None, "head"),
        P(),
        P("node"),
    )
    out_specs = (
        P(("group", "sample"), "node", "head"),
        P("group", None, None),
        P("group", None, "head"),
    )
    return jax.shard_map(shards, mesh=mesh, in_specs=in_specs, out_specs=out_specs, check_vma=False)
```

```python
import functools
import math

import jax
import jax.numpy as jnp
from jax import lax
from jax.experimental import pallas as pl
from jax.experimental.pallas import tpu as pltpu
from jax.sharding import PartitionSpec as P

DH = 128
BLK = 128
RANK = 16
LOW = 128

adapter_scale = 0.5
masked_value = -1e30
F32 = jnp.float32
BF16 = jnp.bfloat16


def nn(a, b):
    return lax.dot_general(a, b, (((1,), (0,)), ((), ())), preferred_element_type=F32)


def nt(a, b):
    return lax.dot_general(a, b, (((1,), (1,)), ((), ())), preferred_element_type=F32)


def tn(a, b):
    return lax.dot_general(a, b, (((0,), (0,)), ((), ())), preferred_element_type=F32)


def scatter_matrix(order_ref, rows):
    local = order_ref[...] - lax.axis_index("node") * rows
    nodes = lax.broadcasted_iota(jnp.int32, (rows, rows), 0)
    return jnp.where(nodes == local, 1.0, 0.0).astype(BF16)


def head_at(split, which):
    if not split:
        return which
    return jnp.bitwise_xor(lax.rem(lax.axis_index("sample"), 2), which)


def lanes_at(index):
    if isinstance(index, int):
        return pl.ds(index * DH, DH)
    return pl.ds(pl.multiple_of(index * DH, DH), DH)


def pack_kernel(split, wq_ref, wk_ref, wv_ref, wo_ref, *outs):
    for which, out in enumerate(outs):
        lanes = lanes_at(head_at(split, which))
        for j, member in enumerate((wq_ref, wk_ref, wv_ref)):
            out[:, j * DH : (j + 1) * DH] = member[:, lanes]
        out[:, 3 * DH :] = wo_ref[lanes, :].T


def prep_kernel(order_ref, x_ref, cot_ref, normed_ref, half_ref, cot_out_ref):
    rows = x_ref.shape[0]
    place = scatter_matrix(order_ref, rows)
    ordered = tn(place, x_ref[...])
    center = ordered - jnp.mean(ordered, axis=-1, keepdims=True)
    spread = jnp.mean(center * center, axis=-1, keepdims=True)
    normed_ref[...] = (center * lax.rsqrt(spread + 1e-05)).astype(BF16)
    cot_out_ref[...] = tn(place, cot_ref[...]).astype(BF16)
    start = pl.multiple_of(lax.axis_index("head") * (rows // 2), rows // 2)
    half_ref[...] = normed_ref[pl.ds(start, rows // 2), :]


def head_kernel(split, which, piece_rows, *refs):
    (
        table_ref,
        normed_ref,
        a_own_ref,
        a_sib_ref,
        b_own_ref,
        b_sib_ref,
        cot_own_ref,
        cot_sib_ref,
        down_ref,
        up_ref,
    ) = refs[:10]
    rest = refs[10:]
    scratch = rest[-12:]
    if which == 0:
        pieces, (att_ref, wo_ref, down_out, up_out) = rest[:-16], rest[-16:-12]
    else:
        pieces, (down_in, up_in, att_ref, wo_ref, lora_ref) = rest[:-17], rest[-17:-12]
    w_ref, u_ref, kv_ref, low_ref, q_ref, do_ref, dq_ref, tk_ref, tv_ref, bk_ref, bv_ref, sum_ref = (
        scratch
    )
    rows, width = normed_ref.shape
    blocks = rows // BLK
    half = rows // 2
    node, core = lax.axis_index("node"), lax.axis_index("head")
    head = head_at(split, which)
    first = node * blocks
    inverse_root = 1.0 / math.sqrt(DH)

    for piece, row in zip(pieces, piece_rows(node)):
        if isinstance(row, int):
            w_ref[pl.ds(row, piece.shape[0]), :] = piece[...]
        else:
            w_ref[pl.ds(pl.multiple_of(row, piece.shape[0]), piece.shape[0]), :] = piece[...]
    wo_ref[...] = w_ref[:, 3 * DH :]
    u_ref[...] = jnp.zeros_like(u_ref)
    for j in range(3):
        u_ref[j * RANK : (j + 1) * RANK, j * DH : (j + 1) * DH] = (
            adapter_scale * up_ref[j * RANK : (j + 1) * RANK, lanes_at(head)]
        )

    mine, theirs = core * half, (1 - core) * half
    segments = [
        (normed_ref, 0),
        (a_own_ref, pl.multiple_of(rows + mine, half)),
        (a_sib_ref, pl.multiple_of(rows + theirs, half)),
        (b_own_ref, pl.multiple_of(2 * rows + mine, half)),
        (b_sib_ref, pl.multiple_of(2 * rows + theirs, half)),
    ]
    low_ref[...] = jnp.zeros_like(low_ref)
    for j, (member, start) in enumerate(segments):
        value = member[...]
        span = pl.ds(start, value.shape[0])
        low_ref[span, : 3 * RANK] = nt(value, down_ref[...]).astype(BF16)
        low = low_ref[span, :]
        skip = DH if j else 0
        projected = (nn(value, w_ref[:, skip : 3 * DH]) + nn(low, u_ref[:, skip:])).astype(BF16)
        if j == 0:
            q_ref[...] = projected[:, :DH]
        kv_ref[span, :] = projected[:, DH - skip :]
    low_own = low_ref[0:rows, :]

    def out_rows(side):
        return w_ref[pl.ds(pl.multiple_of(side * (width // 2), width // 2), width // 2), 3 * DH :]

    do_ref[...] = (
        nn(cot_own_ref[...], out_rows(core)) + nn(cot_sib_ref[...], out_rows(1 - core))
    ).astype(BF16)
    bk_ref[...] = jnp.zeros_like(bk_ref)
    bv_ref[...] = jnp.zeros_like(bv_ref)

    odd = lax.rem(node, 2)
    left, right = 2 - odd, 1 + odd
    for i in range(blocks):
        named = [table_ref[first + i, e] for e in range(table_ref.shape[1])]
        starts, valid = [], []
        for e, c in enumerate(named):
            rel = c - first
            block = jnp.where(
                rel < 0,
                left * blocks + rel + blocks,
                jnp.where(rel >= blocks, (right - 1) * blocks + rel, rel),
            )
            starts.append(pl.multiple_of(block * BLK, BLK))
            fresh = c >= 0
            for before in named[:e]:
                fresh = jnp.logical_and(fresh, c != before)
            valid.append(fresh)
        own = slice(i * BLK, (i + 1) * BLK)
        low_sel = jnp.concatenate([low_ref[pl.ds(s, BLK), :] for s in starts], axis=0)
        keys = jnp.concatenate([kv_ref[pl.ds(s, BLK), :DH] for s in starts], axis=0)
        values = jnp.concatenate([kv_ref[pl.ds(s, BLK), DH:] for s in starts], axis=0)
        query, grad = q_ref[own, :], do_ref[own, :]
        scores = nt(query, keys) * inverse_root
        scores = jnp.concatenate(
            [
                jnp.where(ok, scores[:, e * BLK : (e + 1) * BLK], masked_value)
                for e, ok in enumerate(valid)
            ],
            axis=1,
        )
        row_max = jnp.max(scores, axis=-1, keepdims=True)
        weights = jnp.exp(scores - row_max)
        prob = weights * (1.0 / jnp.sum(weights, axis=-1, keepdims=True))
        prob_b = prob.astype(BF16)
        mixed = nn(prob_b, jnp.concatenate([values, low_sel], axis=1))
        attended = mixed[:, :DH].astype(BF16)
        att_ref[own, :] = attended
        tv_ref[own, :] = mixed[:, DH:].astype(BF16)
        delta = jnp.sum(grad.astype(F32) * attended.astype(F32), axis=-1, keepdims=True)
        score_grad = (prob * (nt(grad, values) - delta) * inverse_root).astype(BF16)
        mixed = nn(score_grad, jnp.concatenate([keys, low_sel], axis=1))
        dq_ref[own, :] = mixed[:, :DH].astype(BF16)
        tk_ref[own, :] = mixed[:, DH:].astype(BF16)
        up_k = u_ref[RANK : 2 * RANK, DH : 2 * DH]
        up_v = u_ref[2 * RANK : 3 * RANK, 2 * DH :]
        back_k = nn(nt(up_k, query).astype(BF16), score_grad)
        back_v = nn(nt(up_v, grad).astype(BF16), prob_b)
        for e, s in enumerate(starts):
            bk_ref[:, pl.ds(s, BLK)] += back_k[:, e * BLK : (e + 1) * BLK]
            bv_ref[:, pl.ds(s, BLK)] += back_v[:, e * BLK : (e + 1) * BLK]

    back_q = nt(u_ref[0:RANK, 0:DH], dq_ref[...])
    lhs = jnp.concatenate([back_q, bk_ref[:, 0:rows], bv_ref[:, 0:rows]], axis=0).astype(BF16)
    sum_ref[...] = nn(lhs, normed_ref[...])
    for member, start in segments[1:]:
        span = pl.ds(start, half)
        lhs = jnp.concatenate([bk_ref[:, span], bv_ref[:, span]], axis=0).astype(BF16)
        sum_ref[RANK:, :] += nn(lhs, member[...])
    up_grad = adapter_scale * jnp.concatenate(
        [
            tn(low_own, dq_ref[...])[0:RANK],
            tn(tk_ref[...], q_ref[...])[RANK : 2 * RANK],
            tn(tv_ref[...], do_ref[...])[2 * RANK : 3 * RANK],
        ],
        axis=0,
    )
    if which == 0:
        down_out[...] = sum_ref[...]
        up_out[...] = up_grad
        return
    lora_ref[:, :width] = (sum_ref[...] + down_in[...]).astype(BF16)
    up_at = [pl.multiple_of(width + g * DH, DH) for g in (head, 1 - head)]
    lora_ref[:, pl.ds(up_at[0], DH)] = up_grad.astype(BF16)
    lora_ref[:, pl.ds(up_at[1], DH)] = up_in[...].astype(BF16)


def out_kernel(order_ref, x_ref, att1_ref, att2_ref, wo1_ref, wo2_ref, base_ref, other_ref):
    rows, width = x_ref.shape
    cols = width // 2
    core = lax.axis_index("head")
    place = scatter_matrix(order_ref, rows)

    def part(side):
        span = pl.ds(pl.multiple_of(side * cols, cols), cols)
        terms = nt(att1_ref[...], wo1_ref[span, :]) + nt(att2_ref[...], wo2_ref[span, :])
        return nn(place, terms.astype(BF16))

    other_ref[...] = part(1 - core).astype(BF16)
    own = pl.ds(pl.multiple_of(core * cols, cols), cols)
    base_ref[...] = x_ref[:, own].astype(F32) + part(core)


VMEM = pl.BlockSpec(memory_space=pltpu.VMEM)
SMEM = pl.BlockSpec(memory_space=pltpu.SMEM)


def shape(dims, dtype=BF16):
    return jax.ShapeDtypeStruct(dims, dtype)


def call(kernel, outs, ins, scratch=(), smem=0, flops=0, limit=32):
    return pl.pallas_call(
        kernel,
        out_shape=outs,
        in_specs=[SMEM] * smem + [VMEM] * (len(ins) - smem),
        out_specs=(VMEM,) * len(outs),
        scratch_shapes=list(scratch),
        cost_estimate=pl.CostEstimate(flops=flops, bytes_accessed=1 << 20, transcendentals=0),
        compiler_params=pltpu.CompilerParams(vmem_limit_bytes=limit * 2**20),
    )(*ins)


def swap(value, axis, step=1):
    size = lax.axis_size(axis)
    return lax.ppermute(value, axis, [(i, i ^ step) for i in range(size)])


def chain_pairs(size):
    pairs = {0: 0, size - 1: size - 1}
    for i in range(1, size - 1, 2):
        pairs[i], pairs[i + 1] = i + 1, i
    return sorted(pairs.items())


def gather_weights(first, second):
    count, depth = lax.axis_size("node"), first.shape[0]
    if not split_weights():
        whole = [lax.all_gather(m, "node", axis=0, tiled=True) for m in (first, second)]
        return [[whole[0]], [whole[1]]], [lambda node: [0]] * 2
    near = swap(first, "node", 1)
    far_pairs = [(g * 4 + n, g * 4 + (n ^ (2 + g))) for g in range(2) for n in range(4)]
    far = lax.ppermute(first, ("group", "node"), far_pairs)
    other_far = swap(far, "group")

    def places(node, steps):
        return [jnp.bitwise_xor(node, k) * depth for k in steps]

    def piece_rows(node):
        group = lax.axis_index("group")
        return places(node, (0, 1, 2 + group, 3 - group))

    own = [first, near, far, other_far]
    return [own, [second] + [swap(p, "sample") for p in own[1:]]], [piece_rows] * 2


def split_weights():
    return lax.axis_size("node") == 4 and lax.axis_size("group") == 2 and lax.axis_size("sample") == 2


def shards(
    mesh_node_state,
    cotangent,
    query_weight,
    key_weight,
    value_weight,
    output_weight,
    adapter_down_weight,
    adapter_up_weight,
    neighbour_key_blocks,
    block_node_order,
):
    _, rows, width = mesh_node_state.shape
    cols = query_weight.shape[1]
    depth = query_weight.shape[0]
    state = mesh_node_state[0]
    order = block_node_order.reshape(1, rows)
    split = split_weights()

    packed = call(
        functools.partial(pack_kernel, split),
        (shape((depth, 4 * DH)),) * 2,
        (query_weight, key_weight, value_weight, output_weight),
        limit=8,
    )
    pieces, piece_rows = gather_weights(*packed)
    down = adapter_down_weight.transpose(0, 2, 1).reshape(3 * RANK, width)
    up = adapter_up_weight.reshape(3 * RANK, cols)
    normed, half, cot_own = call(
        prep_kernel,
        (shape((rows, width)), shape((rows // 2, width)), shape((rows, cols))),
        (order, state, cotangent[0]),
        flops=2 * rows * rows * (width + cols),
        limit=16,
    )
    cot_sib = swap(cot_own, "head")
    a_own = swap(half, "node", 1)
    b_own = lax.ppermute(half, "node", chain_pairs(lax.axis_size("node")))
    a_sib = swap(a_own, "head")
    b_sib = swap(b_own, "head")

    shared = (
        neighbour_key_blocks,
        normed,
        a_own,
        a_sib,
        b_own,
        b_sib,
        cot_own,
        cot_sib,
        down,
        up,
    )
    scratch = [
        pltpu.VMEM((width, 4 * DH), BF16),
        pltpu.VMEM((LOW, 3 * DH), BF16),
        pltpu.VMEM((3 * rows, 2 * DH), BF16),
        pltpu.VMEM((3 * rows, LOW), BF16),
        pltpu.VMEM((rows, DH), BF16),
        pltpu.VMEM((rows, DH), BF16),
        pltpu.VMEM((rows, DH), BF16),
        pltpu.VMEM((rows, LOW), BF16),
        pltpu.VMEM((rows, LOW), BF16),
        pltpu.VMEM((RANK, 3 * rows), F32),
        pltpu.VMEM((RANK, 3 * rows), F32),
        pltpu.VMEM((3 * RANK, width), F32),
    ]
    att1, wo1, down1, up1 = call(
        functools.partial(head_kernel, split, 0, piece_rows[0]),
        (shape((rows, DH)), shape((width, DH)), shape((3 * RANK, width), F32), shape((3 * RANK, DH), F32)),
        shared + tuple(pieces[0]),
        scratch,
        smem=1,
        flops=4 * 10**9,
    )
    att2, wo2, lora = call(
        functools.partial(head_kernel, split, 1, piece_rows[1]),
        (shape((rows, DH)), shape((width, DH)), shape((3 * RANK, width + cols))),
        shared + tuple(pieces[1]) + (down1, up1),
        scratch,
        smem=1,
        flops=4 * 10**9,
    )
    base, other = call(
        out_kernel,
        (shape((rows, cols), F32), shape((rows, cols))),
        (order, state, att1, att2, wo1, wo2),
        flops=10**9,
    )
    mesh_out = (base + swap(other, "head").astype(F32)).astype(BF16)[None]

    total = lora.astype(F32)
    for axis in ("sample", "node"):
        step = 1
        while step < lax.axis_size(axis):
            sent = total.astype(BF16)
            total = sent.astype(F32) + swap(sent, axis, step).astype(F32)
            step *= 2
    sent = total[:, :width].astype(BF16)
    down_total = sent.astype(F32) + swap(sent, "head").astype(F32)
    down_total = down_total.reshape(3, RANK, width).transpose(0, 2, 1)
    up_total = total[:, width:].reshape(3, RANK, cols)
    return (mesh_out, down_total, up_total)


def solution(mesh):
    in_specs = (
        P(("group", "sample"), "node", None),
        P(("group", "sample"), "node", "head"),
        P("node", "head"),
        P("node", "head"),
        P("node", "head"),
        P("head", "node"),
        P(),
        P(None, None, "head"),
        P(),
        P("node"),
    )
    out_specs = (
        P(("group", "sample"), "node", "head"),
        P("group", None, None),
        P("group", None, "head"),
    )
    return jax.shard_map(shards, mesh=mesh, in_specs=in_specs, out_specs=out_specs, check_vma=False)
```

```python
import functools
import math

import jax
import jax.numpy as jnp
from jax import lax
from jax.experimental import pallas as pl
from jax.experimental.pallas import tpu as pltpu
from jax.sharding import PartitionSpec as P

DH = 128
BLK = 128
RANK = 16
LOW = 128

adapter_scale = 0.5
masked_value = -1e30
F32 = jnp.float32
BF16 = jnp.bfloat16


def nn(a, b):
    return lax.dot_general(a, b, (((1,), (0,)), ((), ())), preferred_element_type=F32)


def nt(a, b):
    return lax.dot_general(a, b, (((1,), (1,)), ((), ())), preferred_element_type=F32)


def tn(a, b):
    return lax.dot_general(a, b, (((0,), (0,)), ((), ())), preferred_element_type=F32)


def scatter_matrix(order_ref, rows):
    local = order_ref[...] - lax.axis_index("node") * rows
    nodes = lax.broadcasted_iota(jnp.int32, (rows, rows), 0)
    return jnp.where(nodes == local, 1.0, 0.0).astype(BF16)


def head_at(split, which):
    if not split:
        return which
    return jnp.bitwise_xor(lax.rem(lax.axis_index("sample"), 2), which)


def lanes_at(index):
    if isinstance(index, int):
        return pl.ds(index * DH, DH)
    return pl.ds(pl.multiple_of(index * DH, DH), DH)


def load_all(sources, buffers, sems):
    copies = [pltpu.make_async_copy(a, b, sems.at[i]) for i, (a, b) in enumerate(zip(sources, buffers))]
    for copy in copies:
        copy.start()
    return copies


def pack_kernel(split, *refs):
    sources, outs, buffers, sems = refs[:4], refs[4:6], refs[6:10], refs[10]
    for copy in load_all(sources, buffers, sems):
        copy.wait()
    wq_ref, wk_ref, wv_ref, wo_ref = buffers
    for which, out in enumerate(outs):
        lanes = lanes_at(head_at(split, which))
        for j, member in enumerate((wq_ref, wk_ref, wv_ref)):
            out[:, j * DH : (j + 1) * DH] = member[:, lanes]
        out[:, 3 * DH :] = wo_ref[lanes, :].T


def prep_kernel(
    order_hbm, x_hbm, cot_hbm, normed_ref, half_ref, cot_out_ref, order_ref, x_ref, cot_ref, sems
):
    rows = x_ref.shape[0]
    copies = load_all((order_hbm, x_hbm, cot_hbm), (order_ref, x_ref, cot_ref), sems)
    copies[0].wait()
    place = scatter_matrix(order_ref, rows)
    copies[1].wait()
    ordered = tn(place, x_ref[...])
    center = ordered - jnp.mean(ordered, axis=-1, keepdims=True)
    spread = jnp.mean(center * center, axis=-1, keepdims=True)
    normed_ref[...] = (center * lax.rsqrt(spread + 1e-05)).astype(BF16)
    copies[2].wait()
    cot_out_ref[...] = tn(place, cot_ref[...]).astype(BF16)
    start = pl.multiple_of(lax.axis_index("head") * (rows // 2), rows // 2)
    half_ref[...] = normed_ref[pl.ds(start, rows // 2), :]


def head_kernel(split, which, piece_rows, *refs):
    (
        table_ref,
        normed_ref,
        a_own_ref,
        a_sib_ref,
        b_own_ref,
        b_sib_ref,
        cot_own_ref,
        cot_sib_ref,
        down_ref,
        up_ref,
    ) = refs[:10]
    rest = refs[10:]
    scratch = rest[-12:]
    if which == 0:
        pieces, (att_ref, wo_ref, down_out, up_out) = rest[:-16], rest[-16:-12]
    else:
        pieces, (down_in, up_in, att_ref, wo_ref, down_out, up_out) = rest[:-18], rest[-18:-12]
    w_ref, u_ref, kv_ref, low_ref, q_ref, do_ref, dq_ref, tk_ref, tv_ref, bk_ref, bv_ref, sum_ref = (
        scratch
    )
    rows, width = normed_ref.shape
    blocks = rows // BLK
    half = rows // 2
    node, core = lax.axis_index("node"), lax.axis_index("head")
    head = head_at(split, which)
    first = node * blocks
    inverse_root = 1.0 / math.sqrt(DH)

    for piece, row in zip(pieces, piece_rows(node)):
        if isinstance(row, int):
            w_ref[pl.ds(row, piece.shape[0]), :] = piece[...]
        else:
            w_ref[pl.ds(pl.multiple_of(row, piece.shape[0]), piece.shape[0]), :] = piece[...]
    wo_ref[...] = w_ref[:, 3 * DH :]
    u_ref[...] = jnp.zeros_like(u_ref)
    for j in range(3):
        u_ref[j * RANK : (j + 1) * RANK, j * DH : (j + 1) * DH] = (
            adapter_scale * up_ref[j * RANK : (j + 1) * RANK, lanes_at(head)]
        )

    mine, theirs = core * half, (1 - core) * half
    segments = [
        (normed_ref, 0),
        (a_own_ref, pl.multiple_of(rows + mine, half)),
        (a_sib_ref, pl.multiple_of(rows + theirs, half)),
        (b_own_ref, pl.multiple_of(2 * rows + mine, half)),
        (b_sib_ref, pl.multiple_of(2 * rows + theirs, half)),
    ]
    low_ref[...] = jnp.zeros_like(low_ref)
    for j, (member, start) in enumerate(segments):
        value = member[...]
        span = pl.ds(start, value.shape[0])
        low_ref[span, : 3 * RANK] = nt(value, down_ref[...]).astype(BF16)
        low = low_ref[span, :]
        skip = DH if j else 0
        projected = (nn(value, w_ref[:, skip : 3 * DH]) + nn(low, u_ref[:, skip:])).astype(BF16)
        if j == 0:
            q_ref[...] = projected[:, :DH]
        kv_ref[span, :] = projected[:, DH - skip :]
    low_own = low_ref[0:rows, :]

    def out_rows(side):
        return w_ref[pl.ds(pl.multiple_of(side * (width // 2), width // 2), width // 2), 3 * DH :]

    do_ref[...] = (
        nn(cot_own_ref[...], out_rows(core)) + nn(cot_sib_ref[...], out_rows(1 - core))
    ).astype(BF16)
    bk_ref[...] = jnp.zeros_like(bk_ref)
    bv_ref[...] = jnp.zeros_like(bv_ref)

    odd = lax.rem(node, 2)
    left, right = 2 - odd, 1 + odd
    for i in range(blocks):
        named = [table_ref[first + i, e] for e in range(table_ref.shape[1])]
        starts, valid = [], []
        for e, c in enumerate(named):
            rel = c - first
            block = jnp.where(
                rel < 0,
                left * blocks + rel + blocks,
                jnp.where(rel >= blocks, (right - 1) * blocks + rel, rel),
            )
            starts.append(pl.multiple_of(block * BLK, BLK))
            fresh = c >= 0
            for before in named[:e]:
                fresh = jnp.logical_and(fresh, c != before)
            valid.append(fresh)
        own = slice(i * BLK, (i + 1) * BLK)
        low_sel = jnp.concatenate([low_ref[pl.ds(s, BLK), :] for s in starts], axis=0)
        keys = jnp.concatenate([kv_ref[pl.ds(s, BLK), :DH] for s in starts], axis=0)
        values = jnp.concatenate([kv_ref[pl.ds(s, BLK), DH:] for s in starts], axis=0)
        query, grad = q_ref[own, :], do_ref[own, :]
        scores = nt(query, keys) * inverse_root
        scores = jnp.concatenate(
            [
                jnp.where(ok, scores[:, e * BLK : (e + 1) * BLK], masked_value)
                for e, ok in enumerate(valid)
            ],
            axis=1,
        )
        row_max = jnp.max(scores, axis=-1, keepdims=True)
        weights = jnp.exp(scores - row_max)
        prob = weights * (1.0 / jnp.sum(weights, axis=-1, keepdims=True))
        prob_b = prob.astype(BF16)
        mixed = nn(prob_b, jnp.concatenate([values, low_sel], axis=1))
        attended = mixed[:, :DH].astype(BF16)
        att_ref[own, :] = attended
        tv_ref[own, :] = mixed[:, DH:].astype(BF16)
        delta = jnp.sum(grad.astype(F32) * attended.astype(F32), axis=-1, keepdims=True)
        score_grad = (prob * (nt(grad, values) - delta) * inverse_root).astype(BF16)
        mixed = nn(score_grad, jnp.concatenate([keys, low_sel], axis=1))
        dq_ref[own, :] = mixed[:, :DH].astype(BF16)
        tk_ref[own, :] = mixed[:, DH:].astype(BF16)
        up_k = u_ref[RANK : 2 * RANK, DH : 2 * DH]
        up_v = u_ref[2 * RANK : 3 * RANK, 2 * DH :]
        back_k = nn(nt(up_k, query).astype(BF16), score_grad)
        back_v = nn(nt(up_v, grad).astype(BF16), prob_b)
        for e, s in enumerate(starts):
            bk_ref[:, pl.ds(s, BLK)] += back_k[:, e * BLK : (e + 1) * BLK]
            bv_ref[:, pl.ds(s, BLK)] += back_v[:, e * BLK : (e + 1) * BLK]

    back_q = nt(u_ref[0:RANK, 0:DH], dq_ref[...])
    lhs = jnp.concatenate([back_q, bk_ref[:, 0:rows], bv_ref[:, 0:rows]], axis=0).astype(BF16)
    sum_ref[...] = nn(lhs, normed_ref[...])
    for member, start in segments[1:]:
        span = pl.ds(start, half)
        lhs = jnp.concatenate([bk_ref[:, span], bv_ref[:, span]], axis=0).astype(BF16)
        sum_ref[RANK:, :] += nn(lhs, member[...])
    up_grad = adapter_scale * jnp.concatenate(
        [
            tn(low_own, dq_ref[...])[0:RANK],
            tn(tk_ref[...], q_ref[...])[RANK : 2 * RANK],
            tn(tv_ref[...], do_ref[...])[2 * RANK : 3 * RANK],
        ],
        axis=0,
    )
    if which == 0:
        down_out[...] = sum_ref[...]
        up_out[...] = up_grad
        return
    down_out[...] = (sum_ref[...] + down_in[...]).astype(BF16)
    up_out[:, lanes_at(head)] = up_grad.astype(BF16)
    up_out[:, lanes_at(1 - head)] = up_in[...].astype(BF16)


def merge_kernel(down_ref, sibling_ref, up_ref, out_ref):
    width = down_ref.shape[1]
    out_ref[:, :width] = (down_ref[...].astype(F32) + sibling_ref[...].astype(F32)).astype(BF16)
    out_ref[:, width:] = up_ref[...]


def out_kernel(order_ref, x_ref, att1_ref, att2_ref, wo1_ref, wo2_ref, base_ref, other_ref):
    rows, width = x_ref.shape
    cols = width // 2
    core = lax.axis_index("head")
    place = scatter_matrix(order_ref, rows)

    def part(side):
        span = pl.ds(pl.multiple_of(side * cols, cols), cols)
        terms = nt(att1_ref[...], wo1_ref[span, :]) + nt(att2_ref[...], wo2_ref[span, :])
        return nn(place, terms.astype(BF16))

    other_ref[...] = part(1 - core).astype(BF16)
    own = pl.ds(pl.multiple_of(core * cols, cols), cols)
    base_ref[...] = x_ref[:, own].astype(F32) + part(core)


HBM = pl.BlockSpec(memory_space=pltpu.HBM)
VMEM = pl.BlockSpec(memory_space=pltpu.VMEM)
SMEM = pl.BlockSpec(memory_space=pltpu.SMEM)


def shape(dims, dtype=BF16):
    return jax.ShapeDtypeStruct(dims, dtype)


def call(kernel, outs, ins, scratch=(), smem=0, hbm=0, flops=0, limit=32):
    return pl.pallas_call(
        kernel,
        out_shape=outs,
        in_specs=[SMEM] * smem + [HBM] * hbm + [VMEM] * (len(ins) - smem - hbm),
        out_specs=(VMEM,) * len(outs),
        scratch_shapes=list(scratch),
        cost_estimate=pl.CostEstimate(flops=flops, bytes_accessed=1 << 20, transcendentals=0),
        compiler_params=pltpu.CompilerParams(vmem_limit_bytes=limit * 2**20),
    )(*ins)


def swap(value, axis, step=1):
    size = lax.axis_size(axis)
    return lax.ppermute(value, axis, [(i, i ^ step) for i in range(size)])


def chain_pairs(size):
    pairs = {0: 0, size - 1: size - 1}
    for i in range(1, size - 1, 2):
        pairs[i], pairs[i + 1] = i + 1, i
    return sorted(pairs.items())


def gather_weights(first, second):
    count, depth = lax.axis_size("node"), first.shape[0]
    if not split_weights():
        whole = [lax.all_gather(m, "node", axis=0, tiled=True) for m in (first, second)]
        return [[whole[0]], [whole[1]]], [lambda node: [0]] * 2
    near = swap(first, "node", 1)
    far_pairs = [(g * 4 + n, g * 4 + (n ^ (2 + g))) for g in range(2) for n in range(4)]
    far = lax.ppermute(first, ("group", "node"), far_pairs)
    other_far = swap(far, "group")

    def places(node, steps):
        return [jnp.bitwise_xor(node, k) * depth for k in steps]

    def piece_rows(node):
        group = lax.axis_index("group")
        return places(node, (0, 1, 2 + group, 3 - group))

    own = [first, near, far, other_far]
    return [own, [second] + [swap(p, "sample") for p in own[1:]]], [piece_rows] * 2


def split_weights():
    return lax.axis_size("node") == 4 and lax.axis_size("group") == 2 and lax.axis_size("sample") == 2


def shards(
    mesh_node_state,
    cotangent,
    query_weight,
    key_weight,
    value_weight,
    output_weight,
    adapter_down_weight,
    adapter_up_weight,
    neighbour_key_blocks,
    block_node_order,
):
    _, rows, width = mesh_node_state.shape
    cols = query_weight.shape[1]
    depth = query_weight.shape[0]
    state = mesh_node_state[0]
    order = block_node_order.reshape(1, rows)
    split = split_weights()

    packed = call(
        functools.partial(pack_kernel, split),
        (shape((depth, 4 * DH)),) * 2,
        (query_weight, key_weight, value_weight, output_weight),
        [pltpu.VMEM((depth, cols), BF16)] * 3
        + [pltpu.VMEM((cols, depth), BF16), pltpu.SemaphoreType.DMA((4,))],
        hbm=4,
        limit=8,
    )
    pieces, piece_rows = gather_weights(*packed)
    down = adapter_down_weight.transpose(0, 2, 1).reshape(3 * RANK, width)
    up = adapter_up_weight.reshape(3 * RANK, cols)
    order, _ = lax.optimization_barrier((order, packed[0]))
    normed, half, cot_own = call(
        prep_kernel,
        (shape((rows, width)), shape((rows // 2, width)), shape((rows, cols))),
        (order, state, cotangent[0]),
        [
            pltpu.VMEM((1, rows), jnp.int32),
            pltpu.VMEM((rows, width), BF16),
            pltpu.VMEM((rows, cols), BF16),
            pltpu.SemaphoreType.DMA((3,)),
        ],
        hbm=3,
        flops=2 * rows * rows * (width + cols),
        limit=16,
    )
    cot_sib = swap(cot_own, "head")
    half, _ = lax.optimization_barrier((half, pieces[0][min(1, len(pieces[0]) - 1)]))
    a_own = swap(half, "node", 1)
    b_own = lax.ppermute(half, "node", chain_pairs(lax.axis_size("node")))
    a_sib = swap(a_own, "head")
    b_sib = swap(b_own, "head")

    shared = (
        neighbour_key_blocks,
        normed,
        a_own,
        a_sib,
        b_own,
        b_sib,
        cot_own,
        cot_sib,
        down,
        up,
    )
    scratch = [
        pltpu.VMEM((width, 4 * DH), BF16),
        pltpu.VMEM((LOW, 3 * DH), BF16),
        pltpu.VMEM((3 * rows, 2 * DH), BF16),
        pltpu.VMEM((3 * rows, LOW), BF16),
        pltpu.VMEM((rows, DH), BF16),
        pltpu.VMEM((rows, DH), BF16),
        pltpu.VMEM((rows, DH), BF16),
        pltpu.VMEM((rows, LOW), BF16),
        pltpu.VMEM((rows, LOW), BF16),
        pltpu.VMEM((RANK, 3 * rows), F32),
        pltpu.VMEM((RANK, 3 * rows), F32),
        pltpu.VMEM((3 * RANK, width), F32),
    ]
    att1, wo1, down1, up1 = call(
        functools.partial(head_kernel, split, 0, piece_rows[0]),
        (shape((rows, DH)), shape((width, DH)), shape((3 * RANK, width), F32), shape((3 * RANK, DH), F32)),
        shared + tuple(pieces[0]),
        scratch,
        smem=1,
        flops=4 * 10**9,
    )
    att2, wo2, down2, up2 = call(
        functools.partial(head_kernel, split, 1, piece_rows[1]),
        (shape((rows, DH)), shape((width, DH)), shape((3 * RANK, width)), shape((3 * RANK, cols))),
        shared + tuple(pieces[1]) + (down1, up1),
        scratch,
        smem=1,
        flops=4 * 10**9,
    )
    down_sib = swap(down2, "head")
    base, other = call(
        out_kernel,
        (shape((rows, cols), F32), shape((rows, cols))),
        (order, state, att1, att2, wo1, wo2),
        flops=10**9,
    )
    lora = call(merge_kernel, (shape((3 * RANK, width + cols)),), (down2, down_sib, up2))[0]
    mesh_out = (base + swap(other, "head").astype(F32)).astype(BF16)[None]

    total = lora.astype(F32)
    for axis in ("sample", "node"):
        step = 1
        while step < lax.axis_size(axis):
            sent = total.astype(BF16)
            total = sent.astype(F32) + swap(sent, axis, step).astype(F32)
            step *= 2
    down_total = total[:, :width].reshape(3, RANK, width).transpose(0, 2, 1)
    up_total = total[:, width:].reshape(3, RANK, cols)
    return (mesh_out, down_total, up_total)


def solution(mesh):
    in_specs = (
        P(("group", "sample"), "node", None),
        P(("group", "sample"), "node", "head"),
        P("node", "head"),
        P("node", "head"),
        P("node", "head"),
        P("head", "node"),
        P(),
        P(None, None, "head"),
        P(),
        P("node"),
    )
    out_specs = (
        P(("group", "sample"), "node", "head"),
        P("group", None, None),
        P("group", None, "head"),
    )
    return jax.shard_map(shards, mesh=mesh, in_specs=in_specs, out_specs=out_specs, check_vma=False)
```

```python
import functools
import math

import jax
import jax.numpy as jnp
from jax import lax
from jax.experimental import pallas as pl
from jax.experimental.pallas import tpu as pltpu
from jax.sharding import PartitionSpec as P

DH = 128
BLK = 128
RANK = 16
LOW = 128

adapter_scale = 0.5
masked_value = -1e30
F32 = jnp.float32
BF16 = jnp.bfloat16


def nn(a, b):
    return lax.dot_general(a, b, (((1,), (0,)), ((), ())), preferred_element_type=F32)


def nt(a, b):
    return lax.dot_general(a, b, (((1,), (1,)), ((), ())), preferred_element_type=F32)


def tn(a, b):
    return lax.dot_general(a, b, (((0,), (0,)), ((), ())), preferred_element_type=F32)


def scatter_matrix(order_ref, rows):
    local = order_ref[...] - lax.axis_index("node") * rows
    nodes = lax.broadcasted_iota(jnp.int32, (rows, rows), 0)
    return jnp.where(nodes == local, 1.0, 0.0).astype(BF16)


def head_at(split, which):
    if not split:
        return which
    return jnp.bitwise_xor(lax.rem(lax.axis_index("sample"), 2), which)


def lanes_at(index):
    if isinstance(index, int):
        return pl.ds(index * DH, DH)
    return pl.ds(pl.multiple_of(index * DH, DH), DH)


def load_all(sources, buffers, sems):
    copies = [pltpu.make_async_copy(a, b, sems.at[i]) for i, (a, b) in enumerate(zip(sources, buffers))]
    for copy in copies:
        copy.start()
    return copies


def prep_kernel(split, *refs):
    sources, outs, buffers, sems = refs[:7], refs[7:-8], refs[-8:-1], refs[-1]
    copies = load_all(sources, buffers, sems)
    order_ref, x_ref, wq_ref, wk_ref, wv_ref, wo_ref, cot_ref = buffers
    normed_ref, half_ref, near_ref, cot_out_ref = outs[:4]
    rows = x_ref.shape[0]
    copies[0].wait()
    place = scatter_matrix(order_ref, rows)
    copies[1].wait()
    ordered = tn(place, x_ref[...])
    center = ordered - jnp.mean(ordered, axis=-1, keepdims=True)
    spread = jnp.mean(center * center, axis=-1, keepdims=True)
    normed_ref[...] = (center * lax.rsqrt(spread + 1e-05)).astype(BF16)
    for copy in copies[2:]:
        copy.wait()
    for which, out in enumerate(outs[4:]):
        lanes = lanes_at(head_at(split, which))
        for j, member in enumerate((wq_ref, wk_ref, wv_ref)):
            out[:, j * DH : (j + 1) * DH] = member[:, lanes]
        out[:, 3 * DH :] = wo_ref[lanes, :].T
    cot_out_ref[...] = tn(place, cot_ref[...]).astype(BF16)
    start = pl.multiple_of(lax.axis_index("head") * (rows // 2), rows // 2)
    half_ref[...] = normed_ref[pl.ds(start, rows // 2), :]
    skip = near_ref.shape[0] - rows // 2
    if skip:
        near_ref[:skip, :] = outs[4][...]
    near_ref[skip:, :] = half_ref[...]


def head_kernel(split, which, piece_rows, *refs):
    (
        table_ref,
        normed_ref,
        a_own_ref,
        a_sib_ref,
        b_own_ref,
        b_sib_ref,
        cot_own_ref,
        cot_sib_ref,
        down_ref,
        up_ref,
    ) = refs[:10]
    rest = refs[10:]
    scratch = rest[-12:]
    if which == 0:
        pieces, (att_ref, wo_ref, down_out, up_out) = rest[:-16], rest[-16:-12]
    else:
        pieces, (down_in, up_in, att_ref, wo_ref, down_out, up_out) = rest[:-18], rest[-18:-12]
    w_ref, u_ref, kv_ref, low_ref, q_ref, do_ref, dq_ref, tk_ref, tv_ref, bk_ref, bv_ref, sum_ref = (
        scratch
    )
    rows, width = normed_ref.shape
    blocks = rows // BLK
    half = rows // 2
    node, core = lax.axis_index("node"), lax.axis_index("head")
    head = head_at(split, which)
    first = node * blocks
    inverse_root = 1.0 / math.sqrt(DH)

    for piece, row in zip(pieces, piece_rows(node)):
        if isinstance(row, int):
            w_ref[pl.ds(row, piece.shape[0]), :] = piece[...]
        else:
            depth = rest[0].shape[0]
            w_ref[pl.ds(pl.multiple_of(row, depth), depth), :] = piece[:depth, :]
    wo_ref[...] = w_ref[:, 3 * DH :]
    u_ref[...] = jnp.zeros_like(u_ref)
    for j in range(3):
        u_ref[j * RANK : (j + 1) * RANK, j * DH : (j + 1) * DH] = (
            adapter_scale * up_ref[j * RANK : (j + 1) * RANK, lanes_at(head)]
        )

    mine, theirs = core * half, (1 - core) * half
    segments = [
        (normed_ref, 0),
        (a_own_ref.at[pl.ds(a_own_ref.shape[0] - half, half), :], pl.multiple_of(rows + mine, half)),
        (a_sib_ref, pl.multiple_of(rows + theirs, half)),
        (b_own_ref, pl.multiple_of(2 * rows + mine, half)),
        (b_sib_ref, pl.multiple_of(2 * rows + theirs, half)),
    ]
    low_ref[...] = jnp.zeros_like(low_ref)
    for j, (member, start) in enumerate(segments):
        value = member[...]
        span = pl.ds(start, value.shape[0])
        low_ref[span, : 3 * RANK] = nt(value, down_ref[...]).astype(BF16)
        low = low_ref[span, :]
        skip = DH if j else 0
        projected = (nn(value, w_ref[:, skip : 3 * DH]) + nn(low, u_ref[:, skip:])).astype(BF16)
        if j == 0:
            q_ref[...] = projected[:, :DH]
        kv_ref[span, :] = projected[:, DH - skip :]
    low_own = low_ref[0:rows, :]

    def out_rows(side):
        return w_ref[pl.ds(pl.multiple_of(side * (width // 2), width // 2), width // 2), 3 * DH :]

    do_ref[...] = (
        nn(cot_own_ref[...], out_rows(core)) + nn(cot_sib_ref[...], out_rows(1 - core))
    ).astype(BF16)
    bk_ref[...] = jnp.zeros_like(bk_ref)
    bv_ref[...] = jnp.zeros_like(bv_ref)

    odd = lax.rem(node, 2)
    left, right = 2 - odd, 1 + odd
    for i in range(blocks):
        named = [table_ref[first + i, e] for e in range(table_ref.shape[1])]
        starts, valid = [], []
        for e, c in enumerate(named):
            rel = c - first
            block = jnp.where(
                rel < 0,
                left * blocks + rel + blocks,
                jnp.where(rel >= blocks, (right - 1) * blocks + rel, rel),
            )
            starts.append(pl.multiple_of(block * BLK, BLK))
            fresh = c >= 0
            for before in named[:e]:
                fresh = jnp.logical_and(fresh, c != before)
            valid.append(fresh)
        own = slice(i * BLK, (i + 1) * BLK)
        low_sel = jnp.concatenate([low_ref[pl.ds(s, BLK), :] for s in starts], axis=0)
        keys = jnp.concatenate([kv_ref[pl.ds(s, BLK), :DH] for s in starts], axis=0)
        values = jnp.concatenate([kv_ref[pl.ds(s, BLK), DH:] for s in starts], axis=0)
        query, grad = q_ref[own, :], do_ref[own, :]
        scores = nt(query, keys) * inverse_root
        scores = jnp.concatenate(
            [
                jnp.where(ok, scores[:, e * BLK : (e + 1) * BLK], masked_value)
                for e, ok in enumerate(valid)
            ],
            axis=1,
        )
        row_max = jnp.max(scores, axis=-1, keepdims=True)
        weights = jnp.exp(scores - row_max)
        prob = weights * (1.0 / jnp.sum(weights, axis=-1, keepdims=True))
        prob_b = prob.astype(BF16)
        mixed = nn(prob_b, jnp.concatenate([values, low_sel], axis=1))
        attended = mixed[:, :DH].astype(BF16)
        att_ref[own, :] = attended
        tv_ref[own, :] = mixed[:, DH:].astype(BF16)
        delta = jnp.sum(grad.astype(F32) * attended.astype(F32), axis=-1, keepdims=True)
        score_grad = (prob * (nt(grad, values) - delta) * inverse_root).astype(BF16)
        mixed = nn(score_grad, jnp.concatenate([keys, low_sel], axis=1))
        dq_ref[own, :] = mixed[:, :DH].astype(BF16)
        tk_ref[own, :] = mixed[:, DH:].astype(BF16)
        up_k = u_ref[RANK : 2 * RANK, DH : 2 * DH]
        up_v = u_ref[2 * RANK : 3 * RANK, 2 * DH :]
        back_k = nn(nt(up_k, query).astype(BF16), score_grad)
        back_v = nn(nt(up_v, grad).astype(BF16), prob_b)
        for e, s in enumerate(starts):
            bk_ref[:, pl.ds(s, BLK)] += back_k[:, e * BLK : (e + 1) * BLK]
            bv_ref[:, pl.ds(s, BLK)] += back_v[:, e * BLK : (e + 1) * BLK]

    back_q = nt(u_ref[0:RANK, 0:DH], dq_ref[...])
    lhs = jnp.concatenate([back_q, bk_ref[:, 0:rows], bv_ref[:, 0:rows]], axis=0).astype(BF16)
    sum_ref[...] = nn(lhs, normed_ref[...])
    for member, start in segments[1:]:
        span = pl.ds(start, half)
        lhs = jnp.concatenate([bk_ref[:, span], bv_ref[:, span]], axis=0).astype(BF16)
        sum_ref[RANK:, :] += nn(lhs, member[...])
    up_grad = adapter_scale * jnp.concatenate(
        [
            tn(low_own, dq_ref[...])[0:RANK],
            tn(tk_ref[...], q_ref[...])[RANK : 2 * RANK],
            tn(tv_ref[...], do_ref[...])[2 * RANK : 3 * RANK],
        ],
        axis=0,
    )
    if which == 0:
        down_out[...] = sum_ref[...]
        up_out[...] = up_grad
        return
    down_out[...] = (sum_ref[...] + down_in[...]).astype(BF16)
    up_out[:, lanes_at(head)] = up_grad.astype(BF16)
    up_out[:, lanes_at(1 - head)] = up_in[...].astype(BF16)


def merge_kernel(down_ref, sibling_ref, up_ref, out_ref):
    width = down_ref.shape[1]
    out_ref[:, :width] = (down_ref[...].astype(F32) + sibling_ref[...].astype(F32)).astype(BF16)
    out_ref[:, width:] = up_ref[...]


def final_kernel(own_ref, recv_ref, down_ref, up_ref):
    width = down_ref.shape[1]
    total = own_ref[...].astype(F32) + recv_ref[...].astype(F32)
    down_ref[...] = total[:, :width]
    up_ref[...] = total[:, width:]


def out_kernel(order_ref, x_ref, att1_ref, att2_ref, wo1_ref, wo2_ref, base_ref, other_ref):
    rows, width = x_ref.shape
    cols = width // 2
    core = lax.axis_index("head")
    place = scatter_matrix(order_ref, rows)

    def part(side):
        span = pl.ds(pl.multiple_of(side * cols, cols), cols)
        terms = nt(att1_ref[...], wo1_ref[span, :]) + nt(att2_ref[...], wo2_ref[span, :])
        return nn(place, terms.astype(BF16))

    other_ref[...] = part(1 - core).astype(BF16)
    own = pl.ds(pl.multiple_of(core * cols, cols), cols)
    base_ref[...] = x_ref[:, own].astype(F32) + part(core)


HBM = pl.BlockSpec(memory_space=pltpu.HBM)
VMEM = pl.BlockSpec(memory_space=pltpu.VMEM)
SMEM = pl.BlockSpec(memory_space=pltpu.SMEM)


def shape(dims, dtype=BF16):
    return jax.ShapeDtypeStruct(dims, dtype)


def call(kernel, outs, ins, scratch=(), smem=0, hbm=0, flops=0, limit=None):
    return pl.pallas_call(
        kernel,
        out_shape=outs,
        in_specs=[SMEM] * smem + [HBM] * hbm + [VMEM] * (len(ins) - smem - hbm),
        out_specs=(VMEM,) * len(outs),
        scratch_shapes=list(scratch),
        cost_estimate=pl.CostEstimate(flops=flops, bytes_accessed=1 << 20, transcendentals=0),
        compiler_params=pltpu.CompilerParams(vmem_limit_bytes=limit and limit * 2**20),
    )(*ins)


def swap(value, axis, step=1):
    size = lax.axis_size(axis)
    return lax.ppermute(value, axis, [(i, i ^ step) for i in range(size)])


def chain_pairs(size):
    pairs = {0: 0, size - 1: size - 1}
    for i in range(1, size - 1, 2):
        pairs[i], pairs[i + 1] = i + 1, i
    return sorted(pairs.items())


def gather_weights(first, second, near):
    count, depth = lax.axis_size("node"), first.shape[0]
    if not split_weights():
        whole = [lax.all_gather(m, "node", axis=0, tiled=True) for m in (first, second)]
        return [[whole[0]], [whole[1]]], lambda node: [0]
    far_pairs = [(g * 4 + n, g * 4 + (n ^ (2 + g))) for g in range(2) for n in range(4)]
    far = lax.ppermute(first, ("group", "node"), far_pairs)
    other_far = swap(far, "group")
    diagonal = [(i, 3 - i) for i in range(4)]
    theirs = [
        second,
        swap(near[:depth], "sample"),
        swap(far, "sample"),
        lax.ppermute(far, ("group", "sample"), diagonal),
    ]

    def piece_rows(node):
        group = lax.axis_index("group")
        return [jnp.bitwise_xor(node, k) * depth for k in (0, 1, 2 + group, 3 - group)]

    return [[first, near, far, other_far], theirs], piece_rows


def split_weights():
    return lax.axis_size("node") == 4 and lax.axis_size("group") == 2 and lax.axis_size("sample") == 2


def shards(
    mesh_node_state,
    cotangent,
    query_weight,
    key_weight,
    value_weight,
    output_weight,
    adapter_down_weight,
    adapter_up_weight,
    neighbour_key_blocks,
    block_node_order,
):
    _, rows, width = mesh_node_state.shape
    cols = query_weight.shape[1]
    depth = query_weight.shape[0]
    state = mesh_node_state[0]
    order = block_node_order.reshape(1, rows)
    split = split_weights()

    down = adapter_down_weight.transpose(0, 2, 1).reshape(3 * RANK, width)
    up = adapter_up_weight.reshape(3 * RANK, cols)
    skip = depth if split else 0
    normed, half, near, cot_own, *packed = call(
        functools.partial(prep_kernel, split),
        (
            shape((rows, width)),
            shape((rows // 2, width)),
            shape((skip + rows // 2, width)),
            shape((rows, cols)),
            shape((depth, 4 * DH)),
            shape((depth, 4 * DH)),
        ),
        (order, state, query_weight, key_weight, value_weight, output_weight, cotangent[0]),
        [
            pltpu.VMEM((1, rows), jnp.int32),
            pltpu.VMEM((rows, width), BF16),
            pltpu.VMEM((depth, cols), BF16),
            pltpu.VMEM((depth, cols), BF16),
            pltpu.VMEM((depth, cols), BF16),
            pltpu.VMEM((cols, depth), BF16),
            pltpu.VMEM((rows, cols), BF16),
            pltpu.SemaphoreType.DMA((7,)),
        ],
        hbm=7,
        flops=2 * rows * rows * (width + cols),
    )
    a_own = swap(near, "node", 1)
    b_own = lax.ppermute(half, "node", chain_pairs(lax.axis_size("node")))
    pieces, piece_rows = gather_weights(*packed, a_own)
    cot_sib = swap(cot_own, "head")
    a_half, b_half, _ = lax.optimization_barrier((a_own[skip:], b_own, pieces[0][-1]))
    a_sib = swap(a_half, "head")
    b_sib = swap(b_half, "head")

    shared = (
        neighbour_key_blocks,
        normed,
        a_own,
        a_sib,
        b_own,
        b_sib,
        cot_own,
        cot_sib,
        down,
        up,
    )
    scratch = [
        pltpu.VMEM((width, 4 * DH), BF16),
        pltpu.VMEM((LOW, 3 * DH), BF16),
        pltpu.VMEM((3 * rows, 2 * DH), BF16),
        pltpu.VMEM((3 * rows, LOW), BF16),
        pltpu.VMEM((rows, DH), BF16),
        pltpu.VMEM((rows, DH), BF16),
        pltpu.VMEM((rows, DH), BF16),
        pltpu.VMEM((rows, LOW), BF16),
        pltpu.VMEM((rows, LOW), BF16),
        pltpu.VMEM((RANK, 3 * rows), F32),
        pltpu.VMEM((RANK, 3 * rows), F32),
        pltpu.VMEM((3 * RANK, width), F32),
    ]
    att1, wo1, down1, up1 = call(
        functools.partial(head_kernel, split, 0, piece_rows),
        (shape((rows, DH)), shape((width, DH)), shape((3 * RANK, width), F32), shape((3 * RANK, DH), F32)),
        shared + tuple(pieces[0]),
        scratch,
        smem=1,
        limit=32,
        flops=4 * 10**9,
    )
    att2, wo2, down2, up2 = call(
        functools.partial(head_kernel, split, 1, piece_rows),
        (shape((rows, DH)), shape((width, DH)), shape((3 * RANK, width)), shape((3 * RANK, cols))),
        shared + tuple(pieces[1]) + (down1, up1),
        scratch,
        smem=1,
        limit=32,
        flops=4 * 10**9,
    )
    down_sib = swap(down2, "head")
    base, other = call(
        out_kernel,
        (shape((rows, cols), F32), shape((rows, cols))),
        (order, state, att1, att2, wo1, wo2),
        flops=10**9,
    )
    lora = call(merge_kernel, (shape((3 * RANK, width + cols)),), (down2, down_sib, up2))[0]
    mesh_out = (base + swap(other, "head").astype(F32)).astype(BF16)[None]

    hops = [("sample", 1 << i) for i in range(lax.axis_size("sample").bit_length() - 1)]
    hops += [("node", 1 << i) for i in range(lax.axis_size("node").bit_length() - 1)]
    for axis, step in hops[:-1]:
        lora = (lora.astype(F32) + swap(lora, axis, step).astype(F32)).astype(BF16)
    down_total, up_total = call(
        final_kernel,
        (shape((3 * RANK, width), F32), shape((3 * RANK, cols), F32)),
        (lora, swap(lora, *hops[-1])),
    )
    down_total = down_total.reshape(3, RANK, width).transpose(0, 2, 1)
    up_total = up_total.reshape(3, RANK, cols)
    return (mesh_out, down_total, up_total)


def solution(mesh):
    in_specs = (
        P(("group", "sample"), "node", None),
        P(("group", "sample"), "node", "head"),
        P("node", "head"),
        P("node", "head"),
        P("node", "head"),
        P("head", "node"),
        P(),
        P(None, None, "head"),
        P(),
        P("node"),
    )
    out_specs = (
        P(("group", "sample"), "node", "head"),
        P("group", None, None),
        P("group", None, "head"),
    )
    return jax.shard_map(shards, mesh=mesh, in_specs=in_specs, out_specs=out_specs, check_vma=False)
```

```python
import functools
import math

import jax
import jax.numpy as jnp
from jax import lax
from jax.experimental import pallas as pl
from jax.experimental.pallas import tpu as pltpu
from jax.sharding import PartitionSpec as P

DH = 128
BLK = 128
RANK = 16
LOW = 128

adapter_scale = 0.5
masked_value = -1e30
F32 = jnp.float32
BF16 = jnp.bfloat16


def nn(a, b):
    return lax.dot_general(a, b, (((1,), (0,)), ((), ())), preferred_element_type=F32)


def nt(a, b):
    return lax.dot_general(a, b, (((1,), (1,)), ((), ())), preferred_element_type=F32)


def tn(a, b):
    return lax.dot_general(a, b, (((0,), (0,)), ((), ())), preferred_element_type=F32)


def scatter_matrix(order_ref, rows):
    local = order_ref[...] - lax.axis_index("node") * rows
    nodes = lax.broadcasted_iota(jnp.int32, (rows, rows), 0)
    return jnp.where(nodes == local, 1.0, 0.0).astype(BF16)


def head_at(split, which):
    if not split:
        return which
    return jnp.bitwise_xor(lax.rem(lax.axis_index("sample"), 2), which)


def lanes_at(index):
    if isinstance(index, int):
        return pl.ds(index * DH, DH)
    return pl.ds(pl.multiple_of(index * DH, DH), DH)


def load_all(sources, buffers, sems):
    copies = [pltpu.make_async_copy(a, b, sems.at[i]) for i, (a, b) in enumerate(zip(sources, buffers))]
    for copy in copies:
        copy.start()
    return copies


def prep_kernel(split, *refs):
    sources, outs, buffers, sems = refs[:9], refs[9:-7], refs[-7:-1], refs[-1]
    order_ref, down_ref, up_ref, x_own_ref, normed_ref, half_ref, near_ref, cot_out_ref = outs[:8]
    copies = load_all(sources, (order_ref,) + tuple(buffers) + (down_ref, up_ref), sems)
    x_ref, wq_ref, wk_ref, wv_ref, wo_ref, cot_ref = buffers
    rows = x_ref.shape[0]
    copies[0].wait()
    place = scatter_matrix(order_ref, rows)
    copies[1].wait()
    ordered = tn(place, x_ref[...])
    center = ordered - jnp.mean(ordered, axis=-1, keepdims=True)
    spread = jnp.mean(center * center, axis=-1, keepdims=True)
    normed_ref[...] = (center * lax.rsqrt(spread + 1e-05)).astype(BF16)
    for copy in copies[2:]:
        copy.wait()
    for which, out in enumerate(outs[8:]):
        lanes = lanes_at(head_at(split, which))
        for j, member in enumerate((wq_ref, wk_ref, wv_ref)):
            out[:, j * DH : (j + 1) * DH] = member[:, lanes]
        out[:, 3 * DH :] = wo_ref[lanes, :].T
    cot_out_ref[...] = tn(place, cot_ref[...]).astype(BF16)
    cols = x_own_ref.shape[1]
    x_own_ref[...] = x_ref[:, pl.ds(pl.multiple_of(lax.axis_index("head") * cols, cols), cols)]
    start = pl.multiple_of(lax.axis_index("head") * (rows // 2), rows // 2)
    half_ref[...] = normed_ref[pl.ds(start, rows // 2), :]
    skip = near_ref.shape[0] - rows // 2
    if skip:
        near_ref[:skip, :] = outs[8][...]
    near_ref[skip:, :] = half_ref[...]


def head_kernel(split, which, piece_rows, *refs):
    (
        table_ref,
        normed_ref,
        a_own_ref,
        a_sib_ref,
        b_own_ref,
        b_sib_ref,
        cot_own_ref,
        cot_sib_ref,
        down_ref,
        up_ref,
    ) = refs[:10]
    rest = refs[10:]
    scratch = rest[-12:]
    if which == 0:
        pieces, (att_ref, wo_ref, down_out, up_out) = rest[:-16], rest[-16:-12]
    else:
        pieces, (down_in, up_in, att_ref, wo_ref, down_out, up_out) = rest[:-18], rest[-18:-12]
    w_ref, u_ref, kv_ref, low_ref, q_ref, do_ref, dq_ref, tk_ref, tv_ref, bk_ref, bv_ref, sum_ref = (
        scratch
    )
    rows, width = normed_ref.shape
    blocks = rows // BLK
    half = rows // 2
    node, core = lax.axis_index("node"), lax.axis_index("head")
    head = head_at(split, which)
    first = node * blocks
    inverse_root = 1.0 / math.sqrt(DH)

    for piece, row in zip(pieces, piece_rows(node)):
        if isinstance(row, int):
            w_ref[pl.ds(row, piece.shape[0]), :] = piece[...]
        else:
            depth = rest[0].shape[0]
            w_ref[pl.ds(pl.multiple_of(row, depth), depth), :] = piece[:depth, :]
    wo_ref[...] = w_ref[:, 3 * DH :]
    u_ref[...] = jnp.zeros_like(u_ref)
    for j in range(3):
        u_ref[j * RANK : (j + 1) * RANK, j * DH : (j + 1) * DH] = (
            adapter_scale * up_ref[j * RANK : (j + 1) * RANK, lanes_at(head)]
        )

    mine, theirs = core * half, (1 - core) * half
    segments = [
        (normed_ref, 0),
        (a_own_ref.at[pl.ds(a_own_ref.shape[0] - half, half), :], pl.multiple_of(rows + mine, half)),
        (a_sib_ref, pl.multiple_of(rows + theirs, half)),
        (b_own_ref, pl.multiple_of(2 * rows + mine, half)),
        (b_sib_ref, pl.multiple_of(2 * rows + theirs, half)),
    ]
    low_ref[...] = jnp.zeros_like(low_ref)
    for j, (member, start) in enumerate(segments):
        value = member[...]
        span = pl.ds(start, value.shape[0])
        low_ref[span, : 3 * RANK] = nt(value, down_ref[...]).astype(BF16)
        low = low_ref[span, :]
        skip = DH if j else 0
        projected = (nn(value, w_ref[:, skip : 3 * DH]) + nn(low, u_ref[:, skip:])).astype(BF16)
        if j == 0:
            q_ref[...] = projected[:, :DH]
        kv_ref[span, :] = projected[:, DH - skip :]
    low_own = low_ref[0:rows, :]

    def out_rows(side):
        return w_ref[pl.ds(pl.multiple_of(side * (width // 2), width // 2), width // 2), 3 * DH :]

    do_ref[...] = (
        nn(cot_own_ref[...], out_rows(core)) + nn(cot_sib_ref[...], out_rows(1 - core))
    ).astype(BF16)
    bk_ref[...] = jnp.zeros_like(bk_ref)
    bv_ref[...] = jnp.zeros_like(bv_ref)

    odd = lax.rem(node, 2)
    left, right = 2 - odd, 1 + odd
    for i in range(blocks):
        named = [table_ref[first + i, e] for e in range(table_ref.shape[1])]
        starts, valid = [], []
        for e, c in enumerate(named):
            rel = c - first
            block = jnp.where(
                rel < 0,
                left * blocks + rel + blocks,
                jnp.where(rel >= blocks, (right - 1) * blocks + rel, rel),
            )
            starts.append(pl.multiple_of(block * BLK, BLK))
            fresh = c >= 0
            for before in named[:e]:
                fresh = jnp.logical_and(fresh, c != before)
            valid.append(fresh)
        own = slice(i * BLK, (i + 1) * BLK)
        low_sel = jnp.concatenate([low_ref[pl.ds(s, BLK), :] for s in starts], axis=0)
        keys = jnp.concatenate([kv_ref[pl.ds(s, BLK), :DH] for s in starts], axis=0)
        values = jnp.concatenate([kv_ref[pl.ds(s, BLK), DH:] for s in starts], axis=0)
        query, grad = q_ref[own, :], do_ref[own, :]
        scores = nt(query, keys) * inverse_root
        scores = jnp.concatenate(
            [
                jnp.where(ok, scores[:, e * BLK : (e + 1) * BLK], masked_value)
                for e, ok in enumerate(valid)
            ],
            axis=1,
        )
        row_max = jnp.max(scores, axis=-1, keepdims=True)
        weights = jnp.exp(scores - row_max)
        prob = weights * (1.0 / jnp.sum(weights, axis=-1, keepdims=True))
        prob_b = prob.astype(BF16)
        mixed = nn(prob_b, jnp.concatenate([values, low_sel], axis=1))
        attended = mixed[:, :DH].astype(BF16)
        att_ref[own, :] = attended
        tv_ref[own, :] = mixed[:, DH:].astype(BF16)
        delta = jnp.sum(grad.astype(F32) * attended.astype(F32), axis=-1, keepdims=True)
        score_grad = (prob * (nt(grad, values) - delta) * inverse_root).astype(BF16)
        mixed = nn(score_grad, jnp.concatenate([keys, low_sel], axis=1))
        dq_ref[own, :] = mixed[:, :DH].astype(BF16)
        tk_ref[own, :] = mixed[:, DH:].astype(BF16)
        up_k = u_ref[RANK : 2 * RANK, DH : 2 * DH]
        up_v = u_ref[2 * RANK : 3 * RANK, 2 * DH :]
        back_k = nn(nt(up_k, query).astype(BF16), score_grad)
        back_v = nn(nt(up_v, grad).astype(BF16), prob_b)
        for e, s in enumerate(starts):
            bk_ref[:, pl.ds(s, BLK)] += back_k[:, e * BLK : (e + 1) * BLK]
            bv_ref[:, pl.ds(s, BLK)] += back_v[:, e * BLK : (e + 1) * BLK]

    back_q = nt(u_ref[0:RANK, 0:DH], dq_ref[...])
    lhs = jnp.concatenate([back_q, bk_ref[:, 0:rows], bv_ref[:, 0:rows]], axis=0).astype(BF16)
    sum_ref[...] = nn(lhs, normed_ref[...])
    for member, start in segments[1:]:
        span = pl.ds(start, half)
        lhs = jnp.concatenate([bk_ref[:, span], bv_ref[:, span]], axis=0).astype(BF16)
        sum_ref[RANK:, :] += nn(lhs, member[...])
    up_grad = adapter_scale * jnp.concatenate(
        [
            tn(low_own, dq_ref[...])[0:RANK],
            tn(tk_ref[...], q_ref[...])[RANK : 2 * RANK],
            tn(tv_ref[...], do_ref[...])[2 * RANK : 3 * RANK],
        ],
        axis=0,
    )
    if which == 0:
        down_out[...] = sum_ref[...]
        up_out[...] = up_grad
        return
    down_out[...] = (sum_ref[...] + down_in[...]).astype(BF16)
    up_out[:, lanes_at(head)] = up_grad.astype(BF16)
    up_out[:, lanes_at(1 - head)] = up_in[...].astype(BF16)


def merge_kernel(down_ref, sibling_ref, up_ref, out_ref):
    width = down_ref.shape[1]
    out_ref[:, :width] = (down_ref[...].astype(F32) + sibling_ref[...].astype(F32)).astype(BF16)
    out_ref[:, width:] = up_ref[...]


def final_kernel(own_ref, recv_ref, down_ref, up_ref):
    width = down_ref.shape[1]
    total = own_ref[...].astype(F32) + recv_ref[...].astype(F32)
    down_ref[...] = total[:, :width]
    up_ref[...] = total[:, width:]


def out_kernel(order_ref, x_ref, att1_ref, att2_ref, wo1_ref, wo2_ref, base_ref, other_ref):
    rows, cols = x_ref.shape
    core = lax.axis_index("head")
    place = scatter_matrix(order_ref, rows)

    def part(side):
        span = pl.ds(pl.multiple_of(side * cols, cols), cols)
        terms = nt(att1_ref[...], wo1_ref[span, :]) + nt(att2_ref[...], wo2_ref[span, :])
        return nn(place, terms.astype(BF16))

    other_ref[...] = part(1 - core).astype(BF16)
    base_ref[...] = x_ref[...].astype(F32) + part(core)


HBM = pl.BlockSpec(memory_space=pltpu.HBM)
VMEM = pl.BlockSpec(memory_space=pltpu.VMEM)
SMEM = pl.BlockSpec(memory_space=pltpu.SMEM)


def shape(dims, dtype=BF16):
    return jax.ShapeDtypeStruct(dims, dtype)


def call(kernel, outs, ins, scratch=(), smem=0, hbm=0, flops=0, limit=None):
    return pl.pallas_call(
        kernel,
        out_shape=outs,
        in_specs=[SMEM] * smem + [HBM] * hbm + [VMEM] * (len(ins) - smem - hbm),
        out_specs=(VMEM,) * len(outs),
        scratch_shapes=list(scratch),
        cost_estimate=pl.CostEstimate(flops=flops, bytes_accessed=1 << 20, transcendentals=0),
        compiler_params=pltpu.CompilerParams(vmem_limit_bytes=limit and limit * 2**20),
    )(*ins)


def swap(value, axis, step=1):
    size = lax.axis_size(axis)
    return lax.ppermute(value, axis, [(i, i ^ step) for i in range(size)])


def chain_pairs(size):
    pairs = {0: 0, size - 1: size - 1}
    for i in range(1, size - 1, 2):
        pairs[i], pairs[i + 1] = i + 1, i
    return sorted(pairs.items())


def gather_weights(first, second, near):
    count, depth = lax.axis_size("node"), first.shape[0]
    if not split_weights():
        whole = [lax.all_gather(m, "node", axis=0, tiled=True) for m in (first, second)]
        return [[whole[0]], [whole[1]]], lambda node: [0]
    far_pairs = [(g * 4 + n, g * 4 + (n ^ (2 + g))) for g in range(2) for n in range(4)]
    far = lax.ppermute(first, ("group", "node"), far_pairs)
    other_far = swap(far, "group")
    diagonal = [(i, 3 - i) for i in range(4)]
    theirs = [
        second,
        swap(near[:depth], "sample"),
        swap(far, "sample"),
        lax.ppermute(far, ("group", "sample"), diagonal),
    ]

    def piece_rows(node):
        group = lax.axis_index("group")
        return [jnp.bitwise_xor(node, k) * depth for k in (0, 1, 2 + group, 3 - group)]

    return [[first, near, far, other_far], theirs], piece_rows


def split_weights():
    return lax.axis_size("node") == 4 and lax.axis_size("group") == 2 and lax.axis_size("sample") == 2


def shards(
    mesh_node_state,
    cotangent,
    query_weight,
    key_weight,
    value_weight,
    output_weight,
    adapter_down_weight,
    adapter_up_weight,
    neighbour_key_blocks,
    block_node_order,
):
    _, rows, width = mesh_node_state.shape
    cols = query_weight.shape[1]
    depth = query_weight.shape[0]
    state = mesh_node_state[0]
    order = block_node_order.reshape(1, rows)
    split = split_weights()

    skip = depth if split else 0
    order, down, up, x_own, normed, half, near, cot_own, *packed = call(
        functools.partial(prep_kernel, split),
        (
            shape((1, rows), jnp.int32),
            shape((3 * RANK, width)),
            shape((3 * RANK, cols)),
            shape((rows, cols)),
            shape((rows, width)),
            shape((rows // 2, width)),
            shape((skip + rows // 2, width)),
            shape((rows, cols)),
            shape((depth, 4 * DH)),
            shape((depth, 4 * DH)),
        ),
        (
            order,
            state,
            query_weight,
            key_weight,
            value_weight,
            output_weight,
            cotangent[0],
            adapter_down_weight.transpose(0, 2, 1).reshape(3 * RANK, width),
            adapter_up_weight.reshape(3 * RANK, cols),
        ),
        [
            pltpu.VMEM((rows, width), BF16),
            pltpu.VMEM((depth, cols), BF16),
            pltpu.VMEM((depth, cols), BF16),
            pltpu.VMEM((depth, cols), BF16),
            pltpu.VMEM((cols, depth), BF16),
            pltpu.VMEM((rows, cols), BF16),
            pltpu.SemaphoreType.DMA((9,)),
        ],
        hbm=9,
        flops=2 * rows * rows * (width + cols),
    )
    a_own = swap(near, "node", 1)
    b_own = lax.ppermute(half, "node", chain_pairs(lax.axis_size("node")))
    pieces, piece_rows = gather_weights(*packed, a_own)
    cot_sib = swap(cot_own, "head")
    a_half, b_half, _ = lax.optimization_barrier((a_own[skip:], b_own, pieces[0][-1]))
    a_sib = swap(a_half, "head")
    b_sib = swap(b_half, "head")

    shared = (
        neighbour_key_blocks,
        normed,
        a_own,
        a_sib,
        b_own,
        b_sib,
        cot_own,
        cot_sib,
        down,
        up,
    )
    scratch = [
        pltpu.VMEM((width, 4 * DH), BF16),
        pltpu.VMEM((LOW, 3 * DH), BF16),
        pltpu.VMEM((3 * rows, 2 * DH), BF16),
        pltpu.VMEM((3 * rows, LOW), BF16),
        pltpu.VMEM((rows, DH), BF16),
        pltpu.VMEM((rows, DH), BF16),
        pltpu.VMEM((rows, DH), BF16),
        pltpu.VMEM((rows, LOW), BF16),
        pltpu.VMEM((rows, LOW), BF16),
        pltpu.VMEM((RANK, 3 * rows), F32),
        pltpu.VMEM((RANK, 3 * rows), F32),
        pltpu.VMEM((3 * RANK, width), F32),
    ]
    att1, wo1, down1, up1 = call(
        functools.partial(head_kernel, split, 0, piece_rows),
        (shape((rows, DH)), shape((width, DH)), shape((3 * RANK, width), F32), shape((3 * RANK, DH), F32)),
        shared + tuple(pieces[0]),
        scratch,
        smem=1,
        limit=32,
    )
    att2, wo2, down2, up2 = call(
        functools.partial(head_kernel, split, 1, piece_rows),
        (shape((rows, DH)), shape((width, DH)), shape((3 * RANK, width)), shape((3 * RANK, cols))),
        shared + tuple(pieces[1]) + (down1, up1),
        scratch,
        smem=1,
        limit=32,
        flops=4 * 10**9,
    )
    down_sib = swap(down2, "head")
    base, other = call(
        out_kernel,
        (shape((rows, cols), F32), shape((rows, cols))),
        (order, x_own, att1, att2, wo1, wo2),
        flops=10**9,
        limit=16,
    )
    lora = call(merge_kernel, (shape((3 * RANK, width + cols)),), (down2, down_sib, up2), limit=16)[0]
    mesh_out = (base + swap(other, "head").astype(F32)).astype(BF16)[None]

    hops = [("sample", 1 << i) for i in range(lax.axis_size("sample").bit_length() - 1)]
    hops += [("node", 1 << i) for i in range(lax.axis_size("node").bit_length() - 1)]
    for axis, step in hops[:-1]:
        lora = (lora.astype(F32) + swap(lora, axis, step).astype(F32)).astype(BF16)
    down_total, up_total = call(
        final_kernel,
        (shape((3 * RANK, width), F32), shape((3 * RANK, cols), F32)),
        (lora, swap(lora, *hops[-1])),
        limit=16,
    )
    down_total = down_total.reshape(3, RANK, width).transpose(0, 2, 1)
    up_total = up_total.reshape(3, RANK, cols)
    return (mesh_out, down_total, up_total)


def solution(mesh):
    in_specs = (
        P(("group", "sample"), "node", None),
        P(("group", "sample"), "node", "head"),
        P("node", "head"),
        P("node", "head"),
        P("node", "head"),
        P("head", "node"),
        P(),
        P(None, None, "head"),
        P(),
        P("node"),
    )
    out_specs = (
        P(("group", "sample"), "node", "head"),
        P("group", None, None),
        P("group", None, "head"),
    )
    return jax.shard_map(shards, mesh=mesh, in_specs=in_specs, out_specs=out_specs, check_vma=False)
```

```python
import functools
import math

import jax
import jax.numpy as jnp
from jax import lax
from jax.experimental import pallas as pl
from jax.experimental.pallas import tpu as pltpu
from jax.sharding import PartitionSpec as P

DH = 128
BLK = 128
RANK = 16
LOW = 128

adapter_scale = 0.5
masked_value = -1e30
F32 = jnp.float32
BF16 = jnp.bfloat16


def nn(a, b):
    return lax.dot_general(a, b, (((1,), (0,)), ((), ())), preferred_element_type=F32)


def nt(a, b):
    return lax.dot_general(a, b, (((1,), (1,)), ((), ())), preferred_element_type=F32)


def tn(a, b):
    return lax.dot_general(a, b, (((0,), (0,)), ((), ())), preferred_element_type=F32)


def scatter_matrix(order_ref, rows):
    local = order_ref[...] - lax.axis_index("node") * rows
    nodes = lax.broadcasted_iota(jnp.int32, (rows, rows), 0)
    return jnp.where(nodes == local, 1.0, 0.0).astype(BF16)


def head_at(split, which):
    if not split:
        return which
    return jnp.bitwise_xor(lax.rem(lax.axis_index("sample"), 2), which)


def lanes_at(index):
    if isinstance(index, int):
        return pl.ds(index * DH, DH)
    return pl.ds(pl.multiple_of(index * DH, DH), DH)


def load_all(sources, buffers, sems):
    copies = [pltpu.make_async_copy(a, b, sems.at[i]) for i, (a, b) in enumerate(zip(sources, buffers))]
    for copy in copies:
        copy.start()
    return copies


def pack_kernel(split, *refs):
    sources, outs, buffers, sems = refs[:4], refs[4:6], refs[6:-1], refs[-1]
    for copy in load_all(sources, buffers, sems):
        copy.wait()
    for which, out in enumerate(outs):
        lanes = lanes_at(head_at(split, which))
        for j, member in enumerate(buffers[:3]):
            out[:, j * DH : (j + 1) * DH] = member[:, lanes]
        out[:, 3 * DH :] = buffers[3][lanes, :].T


def prep_kernel(*refs):
    sources, outs, buffers, sems = refs[:5], refs[5:-3], refs[-3:-1], refs[-1]
    order_ref, down_ref, up_ref, x_own_ref, normed_ref, half_ref, cot_out_ref = outs
    x_ref, cot_ref = buffers
    copies = load_all(sources, (order_ref, x_ref, cot_ref, down_ref, up_ref), sems)
    rows = x_ref.shape[0]
    copies[0].wait()
    place = scatter_matrix(order_ref, rows)
    copies[1].wait()
    ordered = tn(place, x_ref[...])
    center = ordered - jnp.mean(ordered, axis=-1, keepdims=True)
    spread = jnp.mean(center * center, axis=-1, keepdims=True)
    normed_ref[...] = (center * lax.rsqrt(spread + 1e-05)).astype(BF16)
    start = pl.multiple_of(lax.axis_index("head") * (rows // 2), rows // 2)
    half_ref[...] = normed_ref[pl.ds(start, rows // 2), :]
    for copy in copies[2:]:
        copy.wait()
    cot_out_ref[...] = tn(place, cot_ref[...]).astype(BF16)
    cols = x_own_ref.shape[1]
    x_own_ref[...] = x_ref[:, pl.ds(pl.multiple_of(lax.axis_index("head") * cols, cols), cols)]


def head_kernel(split, which, piece_rows, *refs):
    table_ref, normed_ref, a_own_ref, a_sib_ref, b_own_ref, b_sib_ref = refs[:6]
    cot_own_ref, cot_sib_ref, down_ref, up_ref = refs[6:10]
    rest, scratch = refs[10:-8], refs[-8:]
    if which == 0:
        pieces, (att_ref, wo_ref, low_ref, acc_ref, up_out) = rest[:-5], rest[-5:]
    else:
        low_ref, acc_in, up_in = rest[:3]
        pieces, (att_ref, wo_ref, down_out, up_out) = rest[3:-4], rest[-4:]
    w_ref, kv_ref, q_ref, do_ref, dq_ref, t_ref, back_ref = scratch[:7]
    if which:
        acc_ref = scratch[7]
    rows, width = normed_ref.shape
    blocks, half = rows // BLK, rows // 2
    node, core = lax.axis_index("node"), lax.axis_index("head")
    head = head_at(split, which)
    first = node * blocks
    inverse_root = 1.0 / math.sqrt(DH)

    for piece, row in zip(pieces, piece_rows(node)):
        start = row if isinstance(row, int) else pl.multiple_of(row, pieces[0].shape[0])
        w_ref[pl.ds(start, piece.shape[0]), :] = piece[...]
    wo_ref[...] = w_ref[:width, 3 * DH :]
    w_ref[width:, :] = jnp.zeros((LOW, 4 * DH), BF16)
    for j in range(3):
        span = slice(j * RANK, (j + 1) * RANK)
        w_ref[width + j * RANK : width + (j + 1) * RANK, j * DH : (j + 1) * DH] = (
            adapter_scale * up_ref[span, lanes_at(head)]
        )

    segments = [
        (normed_ref, 0),
        (a_own_ref, pl.multiple_of(rows + core * half, half)),
        (a_sib_ref, pl.multiple_of(rows + (1 - core) * half, half)),
        (b_own_ref, pl.multiple_of(2 * rows + core * half, half)),
        (b_sib_ref, pl.multiple_of(2 * rows + (1 - core) * half, half)),
    ]
    if which == 0:
        for member, start in segments:
            low = nt(member[...], down_ref[...]).astype(BF16)
            blank = jnp.zeros((low.shape[0], LOW - 3 * RANK), BF16)
            low_ref[pl.ds(start, low.shape[0]), :] = jnp.concatenate([low, blank], axis=1)
    for j, (member, start) in enumerate(segments):
        span = pl.ds(start, member.shape[0])
        value = jnp.concatenate([member[...], low_ref[span, :]], axis=1)
        projected = nn(value, w_ref[:, (DH if j else 0) : 3 * DH]).astype(BF16)
        if j == 0:
            q_ref[...] = projected[:, :DH]
        kv_ref[span, :] = projected[:, -2 * DH :]

    def out_rows(side):
        return w_ref[pl.ds(pl.multiple_of(side * (width // 2), width // 2), width // 2), 3 * DH :]

    do_ref[...] = (
        nn(cot_own_ref[...], out_rows(core)) + nn(cot_sib_ref[...], out_rows(1 - core))
    ).astype(BF16)
    up_q = w_ref[width : width + RANK, :DH]
    up_k = w_ref[width + RANK : width + 2 * RANK, DH : 2 * DH]
    up_v = w_ref[width + 2 * RANK : width + 3 * RANK, 2 * DH : 3 * DH]
    query_up = nt(up_k, q_ref[...]).astype(BF16)
    grad_up = nt(up_v, do_ref[...]).astype(BF16)

    odd = lax.rem(node, 2)
    left, right = 2 - odd, 1 + odd
    all_starts = []
    for i in range(blocks):
        named = [table_ref[first + i, e] for e in range(table_ref.shape[1])]
        starts, valid = [], []
        for e, c in enumerate(named):
            rel = c - first
            block = jnp.where(
                rel < 0,
                left * blocks + rel + blocks,
                jnp.where(rel >= blocks, (right - 1) * blocks + rel, rel),
            )
            starts.append(pl.multiple_of(block * BLK, BLK))
            fresh = c >= 0
            for before in named[:e]:
                fresh = jnp.logical_and(fresh, c != before)
            valid.append(fresh)
        all_starts.append(starts)
        own = slice(i * BLK, (i + 1) * BLK)
        low_sel = jnp.concatenate([low_ref[pl.ds(s, BLK), :] for s in starts], axis=0)
        keys = jnp.concatenate([kv_ref[pl.ds(s, BLK), :DH] for s in starts], axis=0)
        values = jnp.concatenate([kv_ref[pl.ds(s, BLK), DH:] for s in starts], axis=0)
        query, grad = q_ref[own, :], do_ref[own, :]
        scores = nt(query, keys) * inverse_root
        scores = jnp.concatenate(
            [
                jnp.where(ok, scores[:, e * BLK : (e + 1) * BLK], masked_value)
                for e, ok in enumerate(valid)
            ],
            axis=1,
        )
        row_max = jnp.max(scores, axis=-1, keepdims=True)
        weights = jnp.exp(scores - row_max)
        prob = weights * (1.0 / jnp.sum(weights, axis=-1, keepdims=True))
        prob_b = prob.astype(BF16)
        mixed = nn(prob_b, jnp.concatenate([values, low_sel], axis=1))
        attended = mixed[:, :DH].astype(BF16)
        att_ref[own, :] = attended
        t_ref[own, LOW:] = mixed[:, DH:].astype(BF16)
        delta = jnp.sum(grad.astype(F32) * attended.astype(F32), axis=-1, keepdims=True)
        score_grad = (prob * (nt(grad, values) - delta) * inverse_root).astype(BF16)
        mixed = nn(score_grad, jnp.concatenate([keys, low_sel], axis=1))
        dq_ref[own, :] = mixed[:, :DH].astype(BF16)
        t_ref[own, :LOW] = mixed[:, DH:].astype(BF16)
        back_ref[i, :RANK, :] = nn(query_up[:, own], score_grad)
        back_ref[i, RANK:, :] = nn(grad_up[:, own], prob_b)

    acc_ref[...] = acc_in[...] if which else jnp.zeros_like(acc_ref)
    acc_ref[:RANK, :rows] += nt(up_q, dq_ref[...])
    for i, starts in enumerate(all_starts):
        for e, s in enumerate(starts):
            acc_ref[RANK:, pl.ds(s, BLK)] += back_ref[i, :, e * BLK : (e + 1) * BLK]
    up_grad = adapter_scale * jnp.concatenate(
        [
            tn(low_ref[:rows, :], dq_ref[...])[0:RANK],
            tn(t_ref[:, :LOW], q_ref[...])[RANK : 2 * RANK],
            tn(t_ref[:, LOW:], do_ref[...])[2 * RANK : 3 * RANK],
        ],
        axis=0,
    )
    if which == 0:
        up_out[...] = up_grad
        return
    total = nn(acc_ref[:, :rows].astype(BF16), normed_ref[...])
    halo = jnp.zeros((2 * RANK, width), F32)
    for member, start in segments[1:]:
        halo += nn(acc_ref[RANK:, pl.ds(start, half)].astype(BF16), member[...])
    down_out[:RANK, :] = total[:RANK].astype(BF16)
    down_out[RANK:, :] = (total[RANK:] + halo).astype(BF16)
    up_out[:, lanes_at(head)] = up_grad.astype(BF16)
    up_out[:, lanes_at(1 - head)] = up_in[...].astype(BF16)


def merge_kernel(down_ref, sibling_ref, up_ref, out_ref):
    width = down_ref.shape[1]
    out_ref[:, :width] = (down_ref[...].astype(F32) + sibling_ref[...].astype(F32)).astype(BF16)
    out_ref[:, width:] = up_ref[...]


def final_kernel(own_ref, recv_ref, down_ref, up_ref):
    width = down_ref.shape[1]
    total = own_ref[...].astype(F32) + recv_ref[...].astype(F32)
    down_ref[...] = total[:, :width]
    up_ref[...] = total[:, width:]


def out_kernel(order_ref, x_ref, att1_ref, att2_ref, wo1_ref, wo2_ref, base_ref, other_ref):
    rows, cols = x_ref.shape
    core = lax.axis_index("head")
    place = scatter_matrix(order_ref, rows)

    def part(side):
        span = pl.ds(pl.multiple_of(side * cols, cols), cols)
        terms = nt(att1_ref[...], wo1_ref[span, :]) + nt(att2_ref[...], wo2_ref[span, :])
        return nn(place, terms.astype(BF16))

    other_ref[...] = part(1 - core).astype(BF16)
    base_ref[...] = x_ref[...].astype(F32) + part(core)


HBM = pl.BlockSpec(memory_space=pltpu.HBM)
VMEM = pl.BlockSpec(memory_space=pltpu.VMEM)
SMEM = pl.BlockSpec(memory_space=pltpu.SMEM)


def shape(dims, dtype=BF16):
    return jax.ShapeDtypeStruct(dims, dtype)


def call(kernel, outs, ins, scratch=(), smem=0, hbm=0, flops=0, limit=None):
    if hbm:
        ins = tuple(pltpu.with_memory_space_constraint(x, pltpu.HBM) for x in ins)
        outs = tuple(pltpu.VMEM(x.shape, x.dtype) for x in outs)
    return pl.pallas_call(
        kernel,
        out_shape=outs,
        in_specs=[SMEM] * smem + [HBM] * hbm + [VMEM] * (len(ins) - smem - hbm),
        out_specs=(VMEM,) * len(outs),
        scratch_shapes=list(scratch),
        cost_estimate=pl.CostEstimate(flops=flops, bytes_accessed=1 << 20, transcendentals=0),
        compiler_params=pltpu.CompilerParams(vmem_limit_bytes=limit and limit * 2**20),
    )(*ins)


def swap(value, axis, step=1):
    size = lax.axis_size(axis)
    return lax.ppermute(value, axis, [(i, i ^ step) for i in range(size)])


def chain_pairs(size):
    pairs = {0: 0, size - 1: size - 1}
    for i in range(1, size - 1, 2):
        pairs[i], pairs[i + 1] = i + 1, i
    return sorted(pairs.items())


def gather_weights(first, second, half):
    count, depth = lax.axis_size("node"), first.shape[0]
    if not split_weights():
        whole = [lax.all_gather(m, "node", axis=0, tiled=True) for m in (first, second)]
        return [whole[:1], whole[1:]], lambda node: [0], whole
    far_pairs = [(g * 4 + n, g * 4 + (n ^ (2 + g))) for g in range(2) for n in range(4)]
    far = lax.ppermute(first, ("group", "node"), far_pairs)
    near = swap(first, "node")
    far, near, _ = lax.optimization_barrier((far, near, half))
    diagonal = [(i, 3 - i) for i in range(4)]
    theirs = [
        second,
        swap(near, "sample"),
        swap(far, "sample"),
        lax.ppermute(far, ("group", "sample"), diagonal),
    ]

    def piece_rows(node):
        group = lax.axis_index("group")
        return [jnp.bitwise_xor(node, k) * depth for k in (0, 1, 2 + group, 3 - group)]

    ours = [first, near, far, swap(far, "group")]
    return [ours, theirs], piece_rows, (theirs[3], ours[3])


def split_weights():
    return lax.axis_size("node") == 4 and lax.axis_size("group") == 2 and lax.axis_size("sample") == 2


def shards(
    mesh_node_state,
    cotangent,
    query_weight,
    key_weight,
    value_weight,
    output_weight,
    adapter_down_weight,
    adapter_up_weight,
    neighbour_key_blocks,
    block_node_order,
):
    _, rows, width = mesh_node_state.shape
    cols = query_weight.shape[1]
    depth = query_weight.shape[0]
    state = mesh_node_state[0]
    order = block_node_order.reshape(1, rows)
    split = split_weights()

    packed = call(
        functools.partial(pack_kernel, split),
        (shape((depth, 4 * DH)),) * 2,
        (query_weight, key_weight, value_weight, output_weight),
        [pltpu.VMEM((depth, cols), BF16)] * 3
        + [pltpu.VMEM((cols, depth), BF16), pltpu.SemaphoreType.DMA((4,))],
        hbm=4,
        limit=16,
    )
    order, _ = lax.optimization_barrier((order, packed[0]))
    order, down, up, x_own, normed, half, cot_own = call(
        prep_kernel,
        (
            shape((1, rows), jnp.int32),
            shape((3 * RANK, width)),
            shape((3 * RANK, cols)),
            shape((rows, cols)),
            shape((rows, width)),
            shape((rows // 2, width)),
            shape((rows, cols)),
        ),
        (
            order,
            state,
            cotangent[0],
            adapter_down_weight.transpose(0, 2, 1).reshape(3 * RANK, width),
            adapter_up_weight.reshape(3 * RANK, cols),
        ),
        [
            pltpu.VMEM((rows, width), BF16),
            pltpu.VMEM((rows, cols), BF16),
            pltpu.SemaphoreType.DMA((5,)),
        ],
        hbm=5,
        flops=2 * rows * rows * (width + cols),
        limit=16,
    )
    pieces, piece_rows, late = gather_weights(*packed, half)
    a_own = swap(half, "node", 1)
    b_own = lax.ppermute(half, "node", chain_pairs(lax.axis_size("node")))
    cot_sib = swap(cot_own, "head")
    a_half, b_half, _ = lax.optimization_barrier((a_own, b_own, late))
    a_sib = swap(a_half, "head")
    b_sib = swap(b_half, "head")

    shared = (
        neighbour_key_blocks,
        normed,
        a_own,
        a_sib,
        b_own,
        b_sib,
        cot_own,
        cot_sib,
        down,
        up,
    )
    entries = neighbour_key_blocks.shape[1]
    scratch = [
        pltpu.VMEM((width + LOW, 4 * DH), BF16),
        pltpu.VMEM((3 * rows, 2 * DH), BF16),
        pltpu.VMEM((rows, DH), BF16),
        pltpu.VMEM((rows, DH), BF16),
        pltpu.VMEM((rows, DH), BF16),
        pltpu.VMEM((rows, 2 * LOW), BF16),
        pltpu.VMEM((rows // BLK, 2 * RANK, entries * BLK), F32),
        pltpu.VMEM((3 * RANK, 3 * rows), F32),
    ]
    att1, wo1, low, acc, up1 = call(
        functools.partial(head_kernel, split, 0, piece_rows),
        (
            shape((rows, DH)),
            shape((width, DH)),
            shape((3 * rows, LOW)),
            shape((3 * RANK, 3 * rows), F32),
            shape((3 * RANK, DH), F32),
        ),
        shared + tuple(pieces[0]),
        scratch,
        smem=1,
        limit=32,
    )
    att2, wo2, down2, up2 = call(
        functools.partial(head_kernel, split, 1, piece_rows),
        (shape((rows, DH)), shape((width, DH)), shape((3 * RANK, width)), shape((3 * RANK, cols))),
        shared + (low, acc, up1) + tuple(pieces[1]),
        scratch,
        smem=1,
        limit=32,
        flops=4 * 10**9,
    )
    down_sib = swap(down2, "head")
    base, other = call(
        out_kernel,
        (shape((rows, cols), F32), shape((rows, cols))),
        (order, x_own, att1, att2, wo1, wo2),
        flops=10**9,
        limit=16,
    )
    lora = call(merge_kernel, (shape((3 * RANK, width + cols)),), (down2, down_sib, up2), limit=16)[0]
    mesh_out = (base + swap(other, "head").astype(F32)).astype(BF16)[None]

    hops = [("sample", 1 << i) for i in range(lax.axis_size("sample").bit_length() - 1)]
    hops += [("node", 1 << i) for i in range(lax.axis_size("node").bit_length() - 1)]
    for axis, step in hops[:-1]:
        lora = (lora.astype(F32) + swap(lora, axis, step).astype(F32)).astype(BF16)
    down_total, up_total = call(
        final_kernel,
        (shape((3 * RANK, width), F32), shape((3 * RANK, cols), F32)),
        (lora, swap(lora, *hops[-1])),
        limit=16,
    )
    down_total = down_total.reshape(3, RANK, width).transpose(0, 2, 1)
    up_total = up_total.reshape(3, RANK, cols)
    return (mesh_out, down_total, up_total)


def solution(mesh):
    in_specs = (
        P(("group", "sample"), "node", None),
        P(("group", "sample"), "node", "head"),
        P("node", "head"),
        P("node", "head"),
        P("node", "head"),
        P("head", "node"),
        P(),
        P(None, None, "head"),
        P(),
        P("node"),
    )
    out_specs = (
        P(("group", "sample"), "node", "head"),
        P("group", None, None),
        P("group", None, "head"),
    )
    return jax.shard_map(shards, mesh=mesh, in_specs=in_specs, out_specs=out_specs, check_vma=False)
```

```python
import functools
import math

import jax
import jax.numpy as jnp
from jax import lax
from jax.experimental import pallas as pl
from jax.experimental.pallas import tpu as pltpu
from jax.sharding import PartitionSpec as P

DH = 128
BLK = 128
RANK = 16
LOW = 128

adapter_scale = 0.5
masked_value = -1e30
F32 = jnp.float32
BF16 = jnp.bfloat16


def nn(a, b):
    return lax.dot_general(a, b, (((1,), (0,)), ((), ())), preferred_element_type=F32)


def nt(a, b):
    return lax.dot_general(a, b, (((1,), (1,)), ((), ())), preferred_element_type=F32)


def tn(a, b):
    return lax.dot_general(a, b, (((0,), (0,)), ((), ())), preferred_element_type=F32)


def scatter_matrix(order_ref, rows):
    local = order_ref[...] - lax.axis_index("node") * rows
    nodes = lax.broadcasted_iota(jnp.int32, (rows, rows), 0)
    return jnp.where(nodes == local, 1.0, 0.0).astype(BF16)


def head_at(split, which):
    if not split:
        return which
    return jnp.bitwise_xor(lax.rem(lax.axis_index("sample"), 2), which)


def lanes_at(index):
    if isinstance(index, int):
        return pl.ds(index * DH, DH)
    return pl.ds(pl.multiple_of(index * DH, DH), DH)


def load_all(sources, buffers, sems):
    copies = [pltpu.make_async_copy(a, b, sems.at[i]) for i, (a, b) in enumerate(zip(sources, buffers))]
    for copy in copies:
        copy.start()
    return copies


def pack_kernel(split, *refs):
    sources, outs, buffers, sems = refs[:4], refs[4:6], refs[6:-1], refs[-1]
    for copy in load_all(sources, buffers, sems):
        copy.wait()
    for which, out in enumerate(outs):
        lanes = lanes_at(head_at(split, which))
        for j, member in enumerate(buffers[:3]):
            out[:, j * DH : (j + 1) * DH] = member[:, lanes]
        out[:, 3 * DH :] = buffers[3][lanes, :].T


def prep_kernel(*refs):
    sources, outs, buffers, sems = refs[:6], refs[6:-3], refs[-3:-1], refs[-1]
    order_ref, table_ref, down_ref, up_ref, x_own_ref, normed_ref, half_ref, cot_out_ref = outs
    x_ref, cot_ref = buffers
    copies = load_all(sources, (order_ref, x_ref, cot_ref, down_ref, up_ref, table_ref), sems)
    rows = x_ref.shape[0]
    copies[0].wait()
    place = scatter_matrix(order_ref, rows)
    copies[1].wait()
    ordered = tn(place, x_ref[...])
    center = ordered - jnp.mean(ordered, axis=-1, keepdims=True)
    spread = jnp.mean(center * center, axis=-1, keepdims=True)
    normed_ref[...] = (center * lax.rsqrt(spread + 1e-05)).astype(BF16)
    start = pl.multiple_of(lax.axis_index("head") * (rows // 2), rows // 2)
    half_ref[...] = normed_ref[pl.ds(start, rows // 2), :]
    for copy in copies[2:]:
        copy.wait()
    cot_out_ref[...] = tn(place, cot_ref[...]).astype(BF16)
    cols = x_own_ref.shape[1]
    x_own_ref[...] = x_ref[:, pl.ds(pl.multiple_of(lax.axis_index("head") * cols, cols), cols)]


def head_kernel(split, which, piece_rows, *refs):
    table_vmem, normed_ref, a_own_ref, a_sib_ref, b_own_ref, b_sib_ref = refs[:6]
    cot_own_ref, cot_sib_ref, down_ref, up_ref = refs[6:10]
    rest, scratch = refs[10:-11], refs[-11:]
    if which == 0:
        pieces, (att_ref, wo_ref, low_ref, acc_ref, up_out) = rest[:-5], rest[-5:]
    else:
        low_ref, acc_in, up_in = rest[:3]
        pieces, (att_ref, wo_ref, keep_ref, send_ref, up_out) = rest[3:-5], rest[-5:]
    w_ref, kv_ref, q_ref, do_ref, dq_ref, t_ref, back_ref = scratch[:7]
    table_ref, table_sem = scratch[8:10]
    if which:
        acc_ref = scratch[7]
    table_copy = pltpu.make_async_copy(table_vmem, table_ref, table_sem)
    table_copy.start()
    rows, width = normed_ref.shape
    blocks, half = rows // BLK, rows // 2
    node, core = lax.axis_index("node"), lax.axis_index("head")
    head = head_at(split, which)
    first = node * blocks
    inverse_root = 1.0 / math.sqrt(DH)

    places = piece_rows(node)
    step = width // len(places)
    for piece in pieces:
        for j in range(0, piece.shape[0], step):
            row, *places = places
            start = row if isinstance(row, int) else pl.multiple_of(row, step)
            w_ref[pl.ds(start, step), :] = piece[j : j + step, :]
    wo_ref[...] = w_ref[:width, 3 * DH :]
    w_ref[width:, :] = jnp.zeros((LOW, 4 * DH), BF16)
    for j in range(3):
        span = slice(j * RANK, (j + 1) * RANK)
        w_ref[width + j * RANK : width + (j + 1) * RANK, j * DH : (j + 1) * DH] = (
            adapter_scale * up_ref[span, lanes_at(head)]
        )

    segments = [
        (normed_ref, 0),
        (a_own_ref, pl.multiple_of(rows + core * half, half)),
        (a_sib_ref, pl.multiple_of(rows + (1 - core) * half, half)),
        (b_own_ref, pl.multiple_of(2 * rows + core * half, half)),
        (b_sib_ref, pl.multiple_of(2 * rows + (1 - core) * half, half)),
    ]
    if which == 0:
        for member, start in segments:
            low = nt(member[...], down_ref[...]).astype(BF16)
            blank = jnp.zeros((low.shape[0], LOW - 3 * RANK), BF16)
            low_ref[pl.ds(start, low.shape[0]), :] = jnp.concatenate([low, blank], axis=1)
    for j, (member, start) in enumerate(segments):
        span = pl.ds(start, member.shape[0])
        value = jnp.concatenate([member[...], low_ref[span, :]], axis=1)
        projected = nn(value, w_ref[:, (DH if j else 0) : 3 * DH]).astype(BF16)
        if j == 0:
            q_ref[...] = projected[:, :DH]
        kv_ref[span, :] = projected[:, -2 * DH :]

    def out_rows(side):
        return w_ref[pl.ds(pl.multiple_of(side * (width // 2), width // 2), width // 2), 3 * DH :]

    do_ref[...] = (
        nn(cot_own_ref[...], out_rows(core)) + nn(cot_sib_ref[...], out_rows(1 - core))
    ).astype(BF16)
    up_q = w_ref[width : width + RANK, :DH]
    up_k = w_ref[width + RANK : width + 2 * RANK, DH : 2 * DH]
    up_v = w_ref[width + 2 * RANK : width + 3 * RANK, 2 * DH : 3 * DH]
    query_up = nt(up_k, q_ref[...]).astype(BF16)
    grad_up = nt(up_v, do_ref[...]).astype(BF16)

    table_copy.wait()
    odd = lax.rem(node, 2)
    left, right = 2 - odd, 1 + odd
    all_starts = []
    for i in range(blocks):
        named = [table_ref[e, first + i] for e in range(table_ref.shape[0])]
        starts, valid = [], []
        for e, c in enumerate(named):
            rel = c - first
            block = jnp.where(
                rel < 0,
                left * blocks + rel + blocks,
                jnp.where(rel >= blocks, (right - 1) * blocks + rel, rel),
            )
            starts.append(pl.multiple_of(block * BLK, BLK))
            fresh = c >= 0
            for before in named[:e]:
                fresh = jnp.logical_and(fresh, c != before)
            valid.append(fresh)
        all_starts.append(starts)
        own = slice(i * BLK, (i + 1) * BLK)
        low_sel = jnp.concatenate([low_ref[pl.ds(s, BLK), :] for s in starts], axis=0)
        keys = jnp.concatenate([kv_ref[pl.ds(s, BLK), :DH] for s in starts], axis=0)
        values = jnp.concatenate([kv_ref[pl.ds(s, BLK), DH:] for s in starts], axis=0)
        query, grad = q_ref[own, :], do_ref[own, :]
        scores = nt(query, keys) * inverse_root
        scores = jnp.concatenate(
            [
                jnp.where(ok, scores[:, e * BLK : (e + 1) * BLK], masked_value)
                for e, ok in enumerate(valid)
            ],
            axis=1,
        )
        row_max = jnp.max(scores, axis=-1, keepdims=True)
        weights = jnp.exp(scores - row_max)
        prob = weights * (1.0 / jnp.sum(weights, axis=-1, keepdims=True))
        prob_b = prob.astype(BF16)
        mixed = nn(prob_b, jnp.concatenate([values, low_sel], axis=1))
        attended = mixed[:, :DH].astype(BF16)
        att_ref[own, :] = attended
        t_ref[own, LOW:] = mixed[:, DH:].astype(BF16)
        delta = jnp.sum(grad.astype(F32) * attended.astype(F32), axis=-1, keepdims=True)
        score_grad = (prob * (nt(grad, values) - delta) * inverse_root).astype(BF16)
        mixed = nn(score_grad, jnp.concatenate([keys, low_sel], axis=1))
        dq_ref[own, :] = mixed[:, :DH].astype(BF16)
        t_ref[own, :LOW] = mixed[:, DH:].astype(BF16)
        back_ref[i, :RANK, :] = nn(query_up[:, own], score_grad)
        back_ref[i, RANK:, :] = nn(grad_up[:, own], prob_b)

    acc_ref[...] = acc_in[...] if which else jnp.zeros_like(acc_ref)
    acc_ref[:RANK, :rows] += nt(up_q, dq_ref[...])
    for i, starts in enumerate(all_starts):
        for e, s in enumerate(starts):
            acc_ref[RANK:, pl.ds(s, BLK)] += back_ref[i, :, e * BLK : (e + 1) * BLK]
    up_grad = adapter_scale * jnp.concatenate(
        [
            tn(low_ref[:rows, :], dq_ref[...])[0:RANK],
            tn(t_ref[:, :LOW], q_ref[...])[RANK : 2 * RANK],
            tn(t_ref[:, LOW:], do_ref[...])[2 * RANK : 3 * RANK],
        ],
        axis=0,
    )
    if which == 0:
        up_out[...] = up_grad
        return
    total = nn(acc_ref[:, :rows].astype(BF16), normed_ref[...])
    halo = jnp.zeros((2 * RANK, width), F32)
    for member, start in segments[1:]:
        halo += nn(acc_ref[RANK:, pl.ds(start, half)].astype(BF16), member[...])
    sum_ref = scratch[10]
    sum_ref[:RANK, :] = total[:RANK]
    sum_ref[RANK:, :] = total[RANK:] + halo
    keep_ref[...] = sum_ref[:, half_lanes(core, width)].astype(BF16)
    send_ref[...] = sum_ref[:, half_lanes(1 - core, width)].astype(BF16)
    up_out[:, lanes_at(head)] = up_grad.astype(BF16)
    up_out[:, lanes_at(1 - head)] = up_in[...].astype(BF16)


def half_lanes(side, width):
    return pl.ds(pl.multiple_of(side * (width // 2), width // 2), width // 2)


def merge_kernel(down_ref, sibling_ref, up_ref, out_ref):
    width = down_ref.shape[1]
    out_ref[:, :width] = (down_ref[...].astype(F32) + sibling_ref[...].astype(F32)).astype(BF16)
    out_ref[:, width:] = up_ref[...]


def total_kernel(*refs):
    terms, (down_ref, up_ref) = [r[...].astype(F32) for r in refs[:-2]], refs[-2:]
    while len(terms) > 1:
        terms = [a + b for a, b in zip(terms[::2], terms[1::2])]
    width = down_ref.shape[1]
    down_ref[...] = terms[0][:, :width]
    up_ref[...] = terms[0][:, width:]


def final_kernel(own_ref, recv_ref, up_ref, out_ref, up_out):
    core, width = lax.axis_index("head"), out_ref.shape[1]
    up_out[...] = up_ref[...]
    out_ref[:, half_lanes(core, width)] = own_ref[...]
    out_ref[:, half_lanes(1 - core, width)] = recv_ref[...]


def out_kernel(order_ref, x_ref, att1_ref, att2_ref, wo1_ref, wo2_ref, base_ref, other_ref):
    rows, cols = x_ref.shape
    core = lax.axis_index("head")
    place = scatter_matrix(order_ref, rows)

    def part(side):
        span = pl.ds(pl.multiple_of(side * cols, cols), cols)
        terms = nt(att1_ref[...], wo1_ref[span, :]) + nt(att2_ref[...], wo2_ref[span, :])
        return nn(place, terms.astype(BF16))

    other_ref[...] = part(1 - core).astype(BF16)
    base_ref[...] = x_ref[...].astype(F32) + part(core)


HBM = pl.BlockSpec(memory_space=pltpu.HBM)
VMEM = pl.BlockSpec(memory_space=pltpu.VMEM)


def shape(dims, dtype=BF16):
    return jax.ShapeDtypeStruct(dims, dtype)


def call(kernel, outs, ins, scratch=(), hbm=0, flops=0, limit=None, pin=False):
    if hbm:
        ins = tuple(pltpu.with_memory_space_constraint(x, pltpu.HBM) for x in ins)
    if hbm or pin:
        outs = tuple(pltpu.VMEM(x.shape, x.dtype) for x in outs)
    return pl.pallas_call(
        kernel,
        out_shape=outs,
        in_specs=[HBM] * hbm + [VMEM] * (len(ins) - hbm),
        out_specs=(VMEM,) * len(outs),
        scratch_shapes=list(scratch),
        cost_estimate=pl.CostEstimate(flops=flops, bytes_accessed=1 << 20, transcendentals=0),
        compiler_params=pltpu.CompilerParams(vmem_limit_bytes=limit and limit * 2**20),
    )(*ins)


def swap(value, axis, step=1):
    size = lax.axis_size(axis)
    return lax.ppermute(value, axis, [(i, i ^ step) for i in range(size)])


def chain_pairs(size):
    pairs = {0: 0, size - 1: size - 1}
    for i in range(1, size - 1, 2):
        pairs[i], pairs[i + 1] = i + 1, i
    return sorted(pairs.items())


def pair_kernel(one_ref, two_ref, out_ref):
    depth = one_ref.shape[0]
    out_ref[:depth, :] = one_ref[...]
    out_ref[depth:, :] = two_ref[...]


def gather_weights(first, second, half):
    count, depth = lax.axis_size("node"), first.shape[0]
    if not split_weights():
        whole = [lax.all_gather(m, "node", axis=0, tiled=True) for m in (first, second)]
        return [whole[:1], whole[1:]], lambda node: [0], whole
    far_pairs = [(g * 4 + n, g * 4 + (n ^ (2 + g))) for g in range(2) for n in range(4)]
    far = lax.ppermute(first, ("group", "node"), far_pairs)
    near = swap(first, "node")
    far, near, _ = lax.optimization_barrier((far, near, half))
    other_far = swap(far, "group")
    near_theirs = swap(near, "sample")
    far_held, _ = lax.optimization_barrier((far, near_theirs))
    pair = call(pair_kernel, (shape((2 * depth, 4 * DH)),), (far_held, other_far), limit=16)[0]
    theirs = [second, near_theirs, swap(pair, "sample")]

    def piece_rows(node):
        group = lax.axis_index("group")
        return [jnp.bitwise_xor(node, k) * depth for k in (0, 1, 2 + group, 3 - group)]

    return [[first, near, far, other_far], theirs], piece_rows, other_far


def split_weights():
    return lax.axis_size("node") == 4 and lax.axis_size("group") == 2 and lax.axis_size("sample") == 2


def shards(
    mesh_node_state,
    cotangent,
    query_weight,
    key_weight,
    value_weight,
    output_weight,
    adapter_down_weight,
    adapter_up_weight,
    neighbour_key_blocks,
    block_node_order,
):
    _, rows, width = mesh_node_state.shape
    cols = query_weight.shape[1]
    depth = query_weight.shape[0]
    state = mesh_node_state[0]
    order = block_node_order.reshape(1, rows)
    split = split_weights()

    packed = call(
        functools.partial(pack_kernel, split),
        (shape((depth, 4 * DH)),) * 2,
        (query_weight, key_weight, value_weight, output_weight),
        [pltpu.VMEM((depth, cols), BF16)] * 3
        + [pltpu.VMEM((cols, depth), BF16), pltpu.SemaphoreType.DMA((4,))],
        hbm=4,
        limit=16,
    )
    order, _ = lax.optimization_barrier((order, packed[0]))
    order, table, down, up, x_own, normed, half, cot_own = call(
        prep_kernel,
        (
            shape((1, rows), jnp.int32),
            shape(neighbour_key_blocks.shape[::-1], jnp.int32),
            shape((3 * RANK, width)),
            shape((3 * RANK, cols)),
            shape((rows, cols)),
            shape((rows, width)),
            shape((rows // 2, width)),
            shape((rows, cols)),
        ),
        (
            order,
            state,
            cotangent[0],
            adapter_down_weight.transpose(0, 2, 1).reshape(3 * RANK, width),
            adapter_up_weight.reshape(3 * RANK, cols),
            neighbour_key_blocks.T,
        ),
        [
            pltpu.VMEM((rows, width), BF16),
            pltpu.VMEM((rows, cols), BF16),
            pltpu.SemaphoreType.DMA((6,)),
        ],
        hbm=6,
        flops=2 * rows * rows * (width + cols),
        limit=16,
    )
    pieces, piece_rows, late = gather_weights(*packed, half)
    a_own = swap(half, "node", 1)
    b_own = lax.ppermute(half, "node", chain_pairs(lax.axis_size("node")))
    cot_sib = swap(cot_own, "head")
    a_half, b_half, _ = lax.optimization_barrier((a_own, b_own, late))
    a_sib = swap(a_half, "head")
    b_sib = swap(b_half, "head")

    shared = (
        table,
        normed,
        a_own,
        a_sib,
        b_own,
        b_sib,
        cot_own,
        cot_sib,
        down,
        up,
    )
    entries = neighbour_key_blocks.shape[1]
    scratch = [
        pltpu.VMEM((width + LOW, 4 * DH), BF16),
        pltpu.VMEM((3 * rows, 2 * DH), BF16),
        pltpu.VMEM((rows, DH), BF16),
        pltpu.VMEM((rows, DH), BF16),
        pltpu.VMEM((rows, DH), BF16),
        pltpu.VMEM((rows, 2 * LOW), BF16),
        pltpu.VMEM((rows // BLK, 2 * RANK, entries * BLK), F32),
        pltpu.VMEM((3 * RANK, 3 * rows), F32),
        pltpu.SMEM(table.shape, jnp.int32),
        pltpu.SemaphoreType.DMA,
        pltpu.VMEM((3 * RANK, width), F32),
    ]
    att1, wo1, low, acc, up1 = call(
        functools.partial(head_kernel, split, 0, piece_rows),
        (
            shape((rows, DH)),
            shape((width, DH)),
            shape((3 * rows, LOW)),
            shape((3 * RANK, 3 * rows), F32),
            shape((3 * RANK, DH), F32),
        ),
        shared + tuple(pieces[0]),
        scratch,
        limit=32,
    )
    att2, wo2, keep, send, up2 = call(
        functools.partial(head_kernel, split, 1, piece_rows),
        (
            shape((rows, DH)),
            shape((width, DH)),
            shape((3 * RANK, width // 2)),
            shape((3 * RANK, width // 2)),
            shape((3 * RANK, cols)),
        ),
        shared + (low, acc, up1) + tuple(pieces[1]),
        scratch,
        limit=32,
        flops=4 * 10**9,
    )
    received = swap(send, "head")
    base, other = call(
        out_kernel,
        (shape((rows, cols), F32), shape((rows, cols))),
        (order, x_own, att1, att2, wo1, wo2),
        flops=10**9,
        limit=16,
    )
    mesh_out = (base + swap(other, "head").astype(F32)).astype(BF16)[None]
    size = (3 * RANK, width // 2 + cols)
    lora = call(merge_kernel, (shape(size),), (keep, received, up2), limit=16)[0]
    hops = [("sample", 1 << i) for i in range(lax.axis_size("sample").bit_length() - 1)]
    count = lax.axis_size("node")
    if count != 4:
        hops += [("node", 1 << i) for i in range(count.bit_length() - 2)]
    for axis, step in hops:
        lora = (lora.astype(F32) + swap(lora, axis, step).astype(F32)).astype(BF16)
    steps = (1, 2, 3) if count == 4 else (count // 2,)
    terms = (lora, *[swap(lora, "node", k) for k in steps])
    terms, mesh_out = lax.optimization_barrier((terms, mesh_out))
    down_half, up_total = call(
        total_kernel,
        (shape((3 * RANK, width // 2), F32), shape((3 * RANK, cols), F32)),
        terms,
        limit=16,
        pin=True,
    )
    down_total, up_total = call(
        final_kernel,
        (shape((3 * RANK, width), F32), shape((3 * RANK, cols), F32)),
        (down_half, swap(down_half, "head"), up_total),
        limit=16,
    )
    down_total = down_total.reshape(3, RANK, width).transpose(0, 2, 1)
    up_total = up_total.reshape(3, RANK, cols)
    return (mesh_out, down_total, up_total)


def solution(mesh):
    in_specs = (
        P(("group", "sample"), "node", None),
        P(("group", "sample"), "node", "head"),
        P("node", "head"),
        P("node", "head"),
        P("node", "head"),
        P("head", "node"),
        P(),
        P(None, None, "head"),
        P(),
        P("node"),
    )
    out_specs = (
        P(("group", "sample"), "node", "head"),
        P("group", None, None),
        P("group", None, "head"),
    )
    return jax.shard_map(shards, mesh=mesh, in_specs=in_specs, out_specs=out_specs, check_vma=False)
```

```python
import functools
import math

import jax
import jax.numpy as jnp
from jax import lax
from jax.experimental import pallas as pl
from jax.experimental.pallas import tpu as pltpu
from jax.sharding import PartitionSpec as P

DH = 128
BLK = 128
RANK = 16
LOW = 128

adapter_scale = 0.5
masked_value = -1e30
F32 = jnp.float32
BF16 = jnp.bfloat16


def nn(a, b):
    return lax.dot_general(a, b, (((1,), (0,)), ((), ())), preferred_element_type=F32)


def nt(a, b):
    return lax.dot_general(a, b, (((1,), (1,)), ((), ())), preferred_element_type=F32)


def tn(a, b):
    return lax.dot_general(a, b, (((0,), (0,)), ((), ())), preferred_element_type=F32)


def scatter_matrix(order_ref, rows):
    local = order_ref[...] - lax.axis_index("node") * rows
    nodes = lax.broadcasted_iota(jnp.int32, (rows, rows), 0)
    return jnp.where(nodes == local, 1.0, 0.0).astype(BF16)


def head_at(split, which):
    if not split:
        return which
    return jnp.bitwise_xor(lax.rem(lax.axis_index("sample"), 2), which)


def lanes_at(index):
    if isinstance(index, int):
        return pl.ds(index * DH, DH)
    return pl.ds(pl.multiple_of(index * DH, DH), DH)


def load_all(sources, buffers, sems):
    copies = [pltpu.make_async_copy(a, b, sems.at[i]) for i, (a, b) in enumerate(zip(sources, buffers))]
    for copy in copies:
        copy.start()
    return copies


def pack_kernel(split, *refs):
    sources, outs, buffers, sems = refs[:4], refs[4:6], refs[6:-1], refs[-1]
    for copy in load_all(sources, buffers, sems):
        copy.wait()
    for which, out in enumerate(outs):
        lanes = lanes_at(head_at(split, which))
        for j, member in enumerate(buffers[:3]):
            out[:, j * DH : (j + 1) * DH] = member[:, lanes]
        out[:, 3 * DH :] = buffers[3][lanes, :].T


def prep_kernel(*refs):
    sources, outs, buffers, sems = refs[:6], refs[6:-3], refs[-3:-1], refs[-1]
    order_ref, table_ref, down_ref, up_ref, x_own_ref, normed_ref, half_ref, cot_out_ref = outs
    x_ref, cot_ref = buffers
    copies = load_all(sources, (order_ref, x_ref, cot_ref, down_ref, up_ref, table_ref), sems)
    rows = x_ref.shape[0]
    copies[0].wait()
    place = scatter_matrix(order_ref, rows)
    copies[1].wait()
    ordered = tn(place, x_ref[...])
    center = ordered - jnp.mean(ordered, axis=-1, keepdims=True)
    spread = jnp.mean(center * center, axis=-1, keepdims=True)
    normed_ref[...] = (center * lax.rsqrt(spread + 1e-05)).astype(BF16)
    start = pl.multiple_of(lax.axis_index("head") * (rows // 2), rows // 2)
    half_ref[...] = normed_ref[pl.ds(start, rows // 2), :]
    for copy in copies[2:]:
        copy.wait()
    cot_out_ref[...] = tn(place, cot_ref[...]).astype(BF16)
    cols = x_own_ref.shape[1]
    x_own_ref[...] = x_ref[:, pl.ds(pl.multiple_of(lax.axis_index("head") * cols, cols), cols)]


def head_kernel(split, which, piece_rows, *refs):
    table_vmem, normed_ref, a_own_ref, a_sib_ref, b_own_ref, b_sib_ref = refs[:6]
    cot_own_ref, cot_sib_ref, down_ref, up_ref = refs[6:10]
    rest, scratch = refs[10:-11], refs[-11:]
    if which == 0:
        pieces, (att_ref, wo_ref, low_ref, acc_ref, up_out) = rest[:-5], rest[-5:]
    else:
        low_ref, acc_in, up_in = rest[:3]
        pieces, (att_ref, wo_ref, keep_ref, send_ref, up_out) = rest[3:-5], rest[-5:]
    w_ref, kv_ref, q_ref, do_ref, dq_ref, t_ref, back_ref = scratch[:7]
    table_ref, table_sem = scratch[8:10]
    if which:
        acc_ref = scratch[7]
    table_copy = pltpu.make_async_copy(table_vmem, table_ref, table_sem)
    table_copy.start()
    rows, width = normed_ref.shape
    blocks, half = rows // BLK, rows // 2
    node, core = lax.axis_index("node"), lax.axis_index("head")
    head = head_at(split, which)
    first = node * blocks
    inverse_root = 1.0 / math.sqrt(DH)

    places = piece_rows(node)
    step = width // len(places)
    for piece in pieces:
        for j in range(0, piece.shape[0], step):
            row, *places = places
            start = row if isinstance(row, int) else pl.multiple_of(row, step)
            w_ref[pl.ds(start, step), :] = piece[j : j + step, :]
    wo_ref[...] = w_ref[:width, 3 * DH :]
    w_ref[width:, :] = jnp.zeros((LOW, 4 * DH), BF16)
    for j in range(3):
        span = slice(j * RANK, (j + 1) * RANK)
        w_ref[width + j * RANK : width + (j + 1) * RANK, j * DH : (j + 1) * DH] = (
            adapter_scale * up_ref[span, lanes_at(head)]
        )

    segments = [
        (normed_ref, 0),
        (a_own_ref, pl.multiple_of(rows + core * half, half)),
        (a_sib_ref, pl.multiple_of(rows + (1 - core) * half, half)),
        (b_own_ref, pl.multiple_of(2 * rows + core * half, half)),
        (b_sib_ref, pl.multiple_of(2 * rows + (1 - core) * half, half)),
    ]
    if which == 0:
        for member, start in segments:
            low = nt(member[...], down_ref[...]).astype(BF16)
            blank = jnp.zeros((low.shape[0], LOW - 3 * RANK), BF16)
            low_ref[pl.ds(start, low.shape[0]), :] = jnp.concatenate([low, blank], axis=1)
    for j, (member, start) in enumerate(segments):
        span = pl.ds(start, member.shape[0])
        value = jnp.concatenate([member[...], low_ref[span, :]], axis=1)
        projected = nn(value, w_ref[:, (DH if j else 0) : 3 * DH]).astype(BF16)
        if j == 0:
            q_ref[...] = projected[:, :DH]
        kv_ref[span, :] = projected[:, -2 * DH :]

    def out_rows(side):
        return w_ref[pl.ds(pl.multiple_of(side * (width // 2), width // 2), width // 2), 3 * DH :]

    do_ref[...] = (
        nn(cot_own_ref[...], out_rows(core)) + nn(cot_sib_ref[...], out_rows(1 - core))
    ).astype(BF16)
    up_q = w_ref[width : width + RANK, :DH]
    up_k = w_ref[width + RANK : width + 2 * RANK, DH : 2 * DH]
    up_v = w_ref[width + 2 * RANK : width + 3 * RANK, 2 * DH : 3 * DH]
    query_up = nt(up_k, q_ref[...]).astype(BF16)
    grad_up = nt(up_v, do_ref[...]).astype(BF16)

    table_copy.wait()
    odd = lax.rem(node, 2)
    left, right = 2 - odd, 1 + odd
    all_starts, all_valid = [], []
    for i in range(blocks):
        named = [table_ref[e, first + i] for e in range(table_ref.shape[0])]
        starts, valid = [], []
        for e, c in enumerate(named):
            rel = c - first
            block = jnp.where(
                rel < 0,
                left * blocks + rel + blocks,
                jnp.where(rel >= blocks, (right - 1) * blocks + rel, rel),
            )
            starts.append(pl.multiple_of(block * BLK, BLK))
            fresh = c >= 0
            for before in named[:e]:
                fresh = jnp.logical_and(fresh, c != before)
            valid.append(fresh)
        all_starts.append(starts)
        all_valid.append(valid)

    def chosen(ref, i, lanes=slice(None)):
        return jnp.concatenate([ref[pl.ds(s, BLK), lanes] for s in all_starts[i]], axis=0)

    def masked(scores, i):
        return jnp.concatenate(
            [
                jnp.where(ok, scores[:, e * BLK : (e + 1) * BLK], masked_value)
                for e, ok in enumerate(all_valid[i])
            ],
            axis=1,
        )

    units = range(blocks)
    own = [slice(i * BLK, (i + 1) * BLK) for i in units]
    key_lanes, value_lanes = slice(0, DH), slice(DH, 2 * DH)
    for base in range(0, blocks, 4):
        some = range(base, base + 4)
        scores = [
            masked(nt(q_ref[own[i], :], chosen(kv_ref, i, key_lanes)) * inverse_root, i) for i in some
        ]
        prob_grads = [nt(do_ref[own[i], :], chosen(kv_ref, i, value_lanes)) for i in some]
        probs, probs_b, score_grads = [], [], []
        for score in scores:
            weights = jnp.exp(score - jnp.max(score, axis=-1, keepdims=True))
            prob = weights * (1.0 / jnp.sum(weights, axis=-1, keepdims=True))
            probs.append(prob)
            probs_b.append(prob.astype(BF16))
        for i, prob, prob_b, prob_grad in zip(some, probs, probs_b, prob_grads):
            rhs = jnp.concatenate([chosen(kv_ref, i, value_lanes), chosen(low_ref, i)], axis=1)
            mixed = nn(prob_b, rhs)
            attended = mixed[:, :DH].astype(BF16)
            att_ref[own[i], :] = attended
            t_ref[own[i], LOW:] = mixed[:, DH:].astype(BF16)
            terms = do_ref[own[i], :].astype(F32) * attended.astype(F32)
            delta = jnp.sum(terms, axis=-1, keepdims=True)
            score_grads.append((prob * (prob_grad - delta) * inverse_root).astype(BF16))
        for i, prob_b, score_grad in zip(some, probs_b, score_grads):
            rhs = jnp.concatenate([chosen(kv_ref, i, key_lanes), chosen(low_ref, i)], axis=1)
            mixed = nn(score_grad, rhs)
            dq_ref[own[i], :] = mixed[:, :DH].astype(BF16)
            t_ref[own[i], :LOW] = mixed[:, DH:].astype(BF16)
            back_ref[i, :RANK, :] = nn(query_up[:, own[i]], score_grad)
            back_ref[i, RANK:, :] = nn(grad_up[:, own[i]], prob_b)

    acc_ref[...] = acc_in[...] if which else jnp.zeros_like(acc_ref)
    acc_ref[:RANK, :rows] += nt(up_q, dq_ref[...])
    for i, starts in enumerate(all_starts):
        for e, s in enumerate(starts):
            acc_ref[RANK:, pl.ds(s, BLK)] += back_ref[i, :, e * BLK : (e + 1) * BLK]
    up_grad = adapter_scale * jnp.concatenate(
        [
            tn(low_ref[:rows, :], dq_ref[...])[0:RANK],
            tn(t_ref[:, :LOW], q_ref[...])[RANK : 2 * RANK],
            tn(t_ref[:, LOW:], do_ref[...])[2 * RANK : 3 * RANK],
        ],
        axis=0,
    )
    if which == 0:
        up_out[...] = up_grad
        return
    total = nn(acc_ref[:, :rows].astype(BF16), normed_ref[...])
    halo = jnp.zeros((2 * RANK, width), F32)
    for member, start in segments[1:]:
        halo += nn(acc_ref[RANK:, pl.ds(start, half)].astype(BF16), member[...])
    sum_ref = scratch[10]
    sum_ref[:RANK, :] = total[:RANK]
    sum_ref[RANK:, :] = total[RANK:] + halo
    keep_ref[...] = sum_ref[:, half_lanes(core, width)].astype(BF16)
    send_ref[...] = sum_ref[:, half_lanes(1 - core, width)].astype(BF16)
    up_out[:, lanes_at(head)] = up_grad.astype(BF16)
    up_out[:, lanes_at(1 - head)] = up_in[...].astype(BF16)


def half_lanes(side, width):
    return pl.ds(pl.multiple_of(side * (width // 2), width // 2), width // 2)


def merge_kernel(down_ref, sibling_ref, up_ref, out_ref):
    width = down_ref.shape[1]
    out_ref[:, :width] = (down_ref[...].astype(F32) + sibling_ref[...].astype(F32)).astype(BF16)
    out_ref[:, width:] = up_ref[...]


def total_kernel(*refs):
    terms, (down_ref, up_ref) = [r[...].astype(F32) for r in refs[:-2]], refs[-2:]
    while len(terms) > 1:
        terms = [a + b for a, b in zip(terms[::2], terms[1::2])]
    width = down_ref.shape[1]
    down_ref[...] = terms[0][:, :width]
    up_ref[...] = terms[0][:, width:]


def final_kernel(own_ref, recv_ref, up_ref, out_ref, up_out):
    core, width = lax.axis_index("head"), out_ref.shape[1]
    up_out[...] = up_ref[...]
    out_ref[:, half_lanes(core, width)] = own_ref[...]
    out_ref[:, half_lanes(1 - core, width)] = recv_ref[...]


def out_kernel(order_ref, x_ref, att1_ref, att2_ref, wo1_ref, wo2_ref, base_ref, other_ref):
    rows, cols = x_ref.shape
    core = lax.axis_index("head")
    place = scatter_matrix(order_ref, rows)

    def part(side):
        span = pl.ds(pl.multiple_of(side * cols, cols), cols)
        terms = nt(att1_ref[...], wo1_ref[span, :]) + nt(att2_ref[...], wo2_ref[span, :])
        return nn(place, terms.astype(BF16))

    other_ref[...] = part(1 - core).astype(BF16)
    base_ref[...] = x_ref[...].astype(F32) + part(core)


HBM = pl.BlockSpec(memory_space=pltpu.HBM)
VMEM = pl.BlockSpec(memory_space=pltpu.VMEM)


def shape(dims, dtype=BF16):
    return jax.ShapeDtypeStruct(dims, dtype)


def call(kernel, outs, ins, scratch=(), hbm=0, flops=0, limit=None, pin=False):
    if hbm:
        ins = tuple(pltpu.with_memory_space_constraint(x, pltpu.HBM) for x in ins)
    if hbm or pin:
        outs = tuple(pltpu.VMEM(x.shape, x.dtype) for x in outs)
    return pl.pallas_call(
        kernel,
        out_shape=outs,
        in_specs=[HBM] * hbm + [VMEM] * (len(ins) - hbm),
        out_specs=(VMEM,) * len(outs),
        scratch_shapes=list(scratch),
        cost_estimate=pl.CostEstimate(flops=flops, bytes_accessed=1 << 20, transcendentals=0),
        compiler_params=pltpu.CompilerParams(vmem_limit_bytes=limit and limit * 2**20),
    )(*ins)


def swap(value, axis, step=1):
    size = lax.axis_size(axis)
    return lax.ppermute(value, axis, [(i, i ^ step) for i in range(size)])


def chain_pairs(size):
    pairs = {0: 0, size - 1: size - 1}
    for i in range(1, size - 1, 2):
        pairs[i], pairs[i + 1] = i + 1, i
    return sorted(pairs.items())


def pair_kernel(one_ref, two_ref, out_ref):
    depth = one_ref.shape[0]
    out_ref[:depth, :] = one_ref[...]
    out_ref[depth:, :] = two_ref[...]


def gather_weights(first, second, half):
    count, depth = lax.axis_size("node"), first.shape[0]
    if not split_weights():
        whole = [lax.all_gather(m, "node", axis=0, tiled=True) for m in (first, second)]
        return [whole[:1], whole[1:]], lambda node: [0], whole
    far_pairs = [(g * 4 + n, g * 4 + (n ^ (2 + g))) for g in range(2) for n in range(4)]
    far = lax.ppermute(first, ("group", "node"), far_pairs)
    near = swap(first, "node")
    far, near, _ = lax.optimization_barrier((far, near, half))
    other_far = swap(far, "group")
    near_theirs = swap(near, "sample")
    far_held, _ = lax.optimization_barrier((far, near_theirs))
    pair = call(pair_kernel, (shape((2 * depth, 4 * DH)),), (far_held, other_far), limit=16)[0]
    theirs = [second, near_theirs, swap(pair, "sample")]

    def piece_rows(node):
        group = lax.axis_index("group")
        return [jnp.bitwise_xor(node, k) * depth for k in (0, 1, 2 + group, 3 - group)]

    return [[first, near, far, other_far], theirs], piece_rows, other_far


def split_weights():
    return lax.axis_size("node") == 4 and lax.axis_size("group") == 2 and lax.axis_size("sample") == 2


def shards(
    mesh_node_state,
    cotangent,
    query_weight,
    key_weight,
    value_weight,
    output_weight,
    adapter_down_weight,
    adapter_up_weight,
    neighbour_key_blocks,
    block_node_order,
):
    _, rows, width = mesh_node_state.shape
    cols = query_weight.shape[1]
    depth = query_weight.shape[0]
    state = mesh_node_state[0]
    order = block_node_order.reshape(1, rows)
    split = split_weights()

    packed = call(
        functools.partial(pack_kernel, split),
        (shape((depth, 4 * DH)),) * 2,
        (query_weight, key_weight, value_weight, output_weight),
        [pltpu.VMEM((depth, cols), BF16)] * 3
        + [pltpu.VMEM((cols, depth), BF16), pltpu.SemaphoreType.DMA((4,))],
        hbm=4,
        limit=16,
    )
    order, _ = lax.optimization_barrier((order, packed[0]))
    order, table, down, up, x_own, normed, half, cot_own = call(
        prep_kernel,
        (
            shape((1, rows), jnp.int32),
            shape(neighbour_key_blocks.shape[::-1], jnp.int32),
            shape((3 * RANK, width)),
            shape((3 * RANK, cols)),
            shape((rows, cols)),
            shape((rows, width)),
            shape((rows // 2, width)),
            shape((rows, cols)),
        ),
        (
            order,
            state,
            cotangent[0],
            adapter_down_weight.transpose(0, 2, 1).reshape(3 * RANK, width),
            adapter_up_weight.reshape(3 * RANK, cols),
            neighbour_key_blocks.T,
        ),
        [
            pltpu.VMEM((rows, width), BF16),
            pltpu.VMEM((rows, cols), BF16),
            pltpu.SemaphoreType.DMA((6,)),
        ],
        hbm=6,
        flops=2 * rows * rows * (width + cols),
        limit=16,
    )
    pieces, piece_rows, late = gather_weights(*packed, half)
    a_own = swap(half, "node", 1)
    b_own = lax.ppermute(half, "node", chain_pairs(lax.axis_size("node")))
    cot_sib = swap(cot_own, "head")
    a_half, b_half, _ = lax.optimization_barrier((a_own, b_own, late))
    a_sib = swap(a_half, "head")
    b_sib = swap(b_half, "head")

    shared = (
        table,
        normed,
        a_own,
        a_sib,
        b_own,
        b_sib,
        cot_own,
        cot_sib,
        down,
        up,
    )
    entries = neighbour_key_blocks.shape[1]
    scratch = [
        pltpu.VMEM((width + LOW, 4 * DH), BF16),
        pltpu.VMEM((3 * rows, 2 * DH), BF16),
        pltpu.VMEM((rows, DH), BF16),
        pltpu.VMEM((rows, DH), BF16),
        pltpu.VMEM((rows, DH), BF16),
        pltpu.VMEM((rows, 2 * LOW), BF16),
        pltpu.VMEM((rows // BLK, 2 * RANK, entries * BLK), F32),
        pltpu.VMEM((3 * RANK, 3 * rows), F32),
        pltpu.SMEM(table.shape, jnp.int32),
        pltpu.SemaphoreType.DMA,
        pltpu.VMEM((3 * RANK, width), F32),
    ]
    att1, wo1, low, acc, up1 = call(
        functools.partial(head_kernel, split, 0, piece_rows),
        (
            shape((rows, DH)),
            shape((width, DH)),
            shape((3 * rows, LOW)),
            shape((3 * RANK, 3 * rows), F32),
            shape((3 * RANK, DH), F32),
        ),
        shared + tuple(pieces[0]),
        scratch,
        limit=32,
    )
    att2, wo2, keep, send, up2 = call(
        functools.partial(head_kernel, split, 1, piece_rows),
        (
            shape((rows, DH)),
            shape((width, DH)),
            shape((3 * RANK, width // 2)),
            shape((3 * RANK, width // 2)),
            shape((3 * RANK, cols)),
        ),
        shared + (low, acc, up1) + tuple(pieces[1]),
        scratch,
        limit=32,
        flops=4 * 10**9,
    )
    received = swap(send, "head")
    base, other = call(
        out_kernel,
        (shape((rows, cols), F32), shape((rows, cols))),
        (order, x_own, att1, att2, wo1, wo2),
        flops=10**9,
        limit=16,
    )
    mesh_out = (base + swap(other, "head").astype(F32)).astype(BF16)[None]
    size = (3 * RANK, width // 2 + cols)
    lora = call(merge_kernel, (shape(size),), (keep, received, up2), limit=16)[0]
    hops = [("sample", 1 << i) for i in range(lax.axis_size("sample").bit_length() - 1)]
    count = lax.axis_size("node")
    if count != 4:
        hops += [("node", 1 << i) for i in range(count.bit_length() - 2)]
    for axis, step in hops:
        lora = (lora.astype(F32) + swap(lora, axis, step).astype(F32)).astype(BF16)
    steps = (1, 2, 3) if count == 4 else (count // 2,)
    terms = (lora, *[swap(lora, "node", k) for k in steps])
    terms, mesh_out = lax.optimization_barrier((terms, mesh_out))
    down_half, up_total = call(
        total_kernel,
        (shape((3 * RANK, width // 2), F32), shape((3 * RANK, cols), F32)),
        terms,
        limit=16,
        pin=True,
    )
    down_total, up_total = call(
        final_kernel,
        (shape((3 * RANK, width), F32), shape((3 * RANK, cols), F32)),
        (down_half, swap(down_half, "head"), up_total),
        limit=16,
    )
    down_total = down_total.reshape(3, RANK, width).transpose(0, 2, 1)
    up_total = up_total.reshape(3, RANK, cols)
    return (mesh_out, down_total, up_total)


def solution(mesh):
    in_specs = (
        P(("group", "sample"), "node", None),
        P(("group", "sample"), "node", "head"),
        P("node", "head"),
        P("node", "head"),
        P("node", "head"),
        P("head", "node"),
        P(),
        P(None, None, "head"),
        P(),
        P("node"),
    )
    out_specs = (
        P(("group", "sample"), "node", "head"),
        P("group", None, None),
        P("group", None, "head"),
    )
    return jax.shard_map(shards, mesh=mesh, in_specs=in_specs, out_specs=out_specs, check_vma=False)
```

```python
import functools
import math

import jax
import jax.numpy as jnp
from jax import lax
from jax.experimental import pallas as pl
from jax.experimental.pallas import tpu as pltpu
from jax.sharding import PartitionSpec as P

DH = 128
BLK = 128
RANK = 16
LOW = 128

adapter_scale = 0.5
masked_value = -1e30
F32 = jnp.float32
BF16 = jnp.bfloat16


def nn(a, b):
    return lax.dot_general(a, b, (((1,), (0,)), ((), ())), preferred_element_type=F32)


def nt(a, b):
    return lax.dot_general(a, b, (((1,), (1,)), ((), ())), preferred_element_type=F32)


def tn(a, b):
    return lax.dot_general(a, b, (((0,), (0,)), ((), ())), preferred_element_type=F32)


def scatter_matrix(order_ref, rows):
    local = order_ref[...] - lax.axis_index("node") * rows
    nodes = lax.broadcasted_iota(jnp.int32, (rows, rows), 0)
    return jnp.where(nodes == local, 1.0, 0.0).astype(BF16)


def head_at(split, which):
    if not split:
        return which
    return jnp.bitwise_xor(lax.rem(lax.axis_index("sample"), 2), which)


def lanes_at(index):
    if isinstance(index, int):
        return pl.ds(index * DH, DH)
    return pl.ds(pl.multiple_of(index * DH, DH), DH)


def load_all(sources, buffers, sems):
    copies = [pltpu.make_async_copy(a, b, sems.at[i]) for i, (a, b) in enumerate(zip(sources, buffers))]
    for copy in copies:
        copy.start()
    return copies


def pack_kernel(split, *refs):
    sources, outs, buffers, sems = refs[:4], refs[4:6], refs[6:-1], refs[-1]
    for copy in load_all(sources, buffers, sems):
        copy.wait()
    for which, out in enumerate(outs):
        lanes = lanes_at(head_at(split, which))
        for j, member in enumerate(buffers[:3]):
            out[:, j * DH : (j + 1) * DH] = member[:, lanes]
        out[:, 3 * DH :] = buffers[3][lanes, :].T


def prep_kernel(*refs):
    sources, outs, buffers, sems = refs[:6], refs[6:-3], refs[-3:-1], refs[-1]
    order_ref, table_ref, down_ref, up_ref, x_own_ref, normed_ref, half_ref, cot_out_ref = outs
    x_ref, cot_ref = buffers
    copies = load_all(sources, (order_ref, x_ref, cot_ref, down_ref, up_ref, table_ref), sems)
    rows = x_ref.shape[0]
    copies[0].wait()
    place = scatter_matrix(order_ref, rows)
    copies[1].wait()
    ordered = tn(place, x_ref[...])
    center = ordered - jnp.mean(ordered, axis=-1, keepdims=True)
    spread = jnp.mean(center * center, axis=-1, keepdims=True)
    normed_ref[...] = (center * lax.rsqrt(spread + 1e-05)).astype(BF16)
    start = pl.multiple_of(lax.axis_index("head") * (rows // 2), rows // 2)
    half_ref[...] = normed_ref[pl.ds(start, rows // 2), :]
    for copy in copies[2:]:
        copy.wait()
    cot_out_ref[...] = tn(place, cot_ref[...]).astype(BF16)
    cols = x_own_ref.shape[1]
    x_own_ref[...] = x_ref[:, pl.ds(pl.multiple_of(lax.axis_index("head") * cols, cols), cols)]


def head_kernel(split, which, piece_rows, *refs):
    table_vmem, normed_ref, a_own_ref, a_sib_ref, a_sib2_ref = refs[:5]
    b_own_ref, b_sib_ref, b_sib2_ref, cot_own_ref, cot_sib_ref, down_ref, up_ref = refs[5:12]
    rest, scratch = refs[12:-11], refs[-11:]
    if which == 0:
        pieces, (att_ref, wo_ref, low_ref, acc_ref, up_out) = rest[:-5], rest[-5:]
    else:
        low_ref, acc_in, up_in = rest[:3]
        pieces, (att_ref, wo_ref, keep_ref, send_ref, up_out) = rest[3:-5], rest[-5:]
    w_ref, kv_ref, q_ref, do_ref, dq_ref, t_ref, back_ref = scratch[:7]
    table_ref, table_sem = scratch[8:10]
    if which:
        acc_ref = scratch[7]
    table_copy = pltpu.make_async_copy(table_vmem, table_ref, table_sem)
    table_copy.start()
    rows, width = normed_ref.shape
    blocks, half = rows // BLK, rows // 2
    node, core = lax.axis_index("node"), lax.axis_index("head")
    head = head_at(split, which)
    first = node * blocks
    inverse_root = 1.0 / math.sqrt(DH)

    places = piece_rows(node)
    step = width // len(places)
    for piece in pieces:
        for j in range(0, piece.shape[0], step):
            row, *places = places
            start = row if isinstance(row, int) else pl.multiple_of(row, step)
            w_ref[pl.ds(start, step), :] = piece[j : j + step, :]
    wo_ref[...] = w_ref[:width, 3 * DH :]
    w_ref[width:, :] = jnp.zeros((LOW, 4 * DH), BF16)
    for j in range(3):
        span = slice(j * RANK, (j + 1) * RANK)
        w_ref[width + j * RANK : width + (j + 1) * RANK, j * DH : (j + 1) * DH] = (
            adapter_scale * up_ref[span, lanes_at(head)]
        )

    segments = [
        ((normed_ref,), 0),
        ((a_own_ref,), pl.multiple_of(rows + core * half, half)),
        ((a_sib_ref, a_sib2_ref), pl.multiple_of(rows + (1 - core) * half, half)),
        ((b_own_ref,), pl.multiple_of(2 * rows + core * half, half)),
        ((b_sib_ref, b_sib2_ref), pl.multiple_of(2 * rows + (1 - core) * half, half)),
    ]
    def rows_of(members):
        return jnp.concatenate([m[...] for m in members], axis=0)

    if which == 0:
        for members, start in segments:
            low = nt(rows_of(members), down_ref[...]).astype(BF16)
            blank = jnp.zeros((low.shape[0], LOW - 3 * RANK), BF16)
            low_ref[pl.ds(start, low.shape[0]), :] = jnp.concatenate([low, blank], axis=1)
    for j, (members, start) in enumerate(segments):
        span = pl.ds(start, half if j else rows)
        value = jnp.concatenate([rows_of(members), low_ref[span, :]], axis=1)
        projected = nn(value, w_ref[:, (DH if j else 0) : 3 * DH]).astype(BF16)
        if j == 0:
            q_ref[...] = projected[:, :DH]
        kv_ref[span, :] = projected[:, -2 * DH :]

    def out_rows(side):
        return w_ref[pl.ds(pl.multiple_of(side * (width // 2), width // 2), width // 2), 3 * DH :]

    do_ref[...] = (
        nn(cot_own_ref[...], out_rows(core)) + nn(cot_sib_ref[...], out_rows(1 - core))
    ).astype(BF16)
    up_q = w_ref[width : width + RANK, :DH]
    up_k = w_ref[width + RANK : width + 2 * RANK, DH : 2 * DH]
    up_v = w_ref[width + 2 * RANK : width + 3 * RANK, 2 * DH : 3 * DH]
    query_up = nt(up_k, q_ref[...]).astype(BF16)
    grad_up = nt(up_v, do_ref[...]).astype(BF16)

    table_copy.wait()
    odd = lax.rem(node, 2)
    left, right = 2 - odd, 1 + odd
    all_starts, all_valid = [], []
    for i in range(blocks):
        named = [table_ref[e, first + i] for e in range(table_ref.shape[0])]
        starts, valid = [], []
        for e, c in enumerate(named):
            rel = c - first
            block = jnp.where(
                rel < 0,
                left * blocks + rel + blocks,
                jnp.where(rel >= blocks, (right - 1) * blocks + rel, rel),
            )
            starts.append(pl.multiple_of(block * BLK, BLK))
            fresh = c >= 0
            for before in named[:e]:
                fresh = jnp.logical_and(fresh, c != before)
            valid.append(fresh)
        all_starts.append(starts)
        all_valid.append(valid)

    def chosen(ref, i, lanes=slice(None)):
        return jnp.concatenate([ref[pl.ds(s, BLK), lanes] for s in all_starts[i]], axis=0)

    def masked(scores, i):
        return jnp.concatenate(
            [
                jnp.where(ok, scores[:, e * BLK : (e + 1) * BLK], masked_value)
                for e, ok in enumerate(all_valid[i])
            ],
            axis=1,
        )

    units = range(blocks)
    own = [slice(i * BLK, (i + 1) * BLK) for i in units]
    key_lanes, value_lanes = slice(0, DH), slice(DH, 2 * DH)
    for base in range(0, blocks, 4):
        some = range(base, base + 4)
        scores = [
            masked(nt(q_ref[own[i], :], chosen(kv_ref, i, key_lanes)) * inverse_root, i) for i in some
        ]
        prob_grads = [nt(do_ref[own[i], :], chosen(kv_ref, i, value_lanes)) for i in some]
        probs, probs_b, score_grads = [], [], []
        for score in scores:
            weights = jnp.exp(score - jnp.max(score, axis=-1, keepdims=True))
            prob = weights * (1.0 / jnp.sum(weights, axis=-1, keepdims=True))
            probs.append(prob)
            probs_b.append(prob.astype(BF16))
        for i, prob, prob_b, prob_grad in zip(some, probs, probs_b, prob_grads):
            rhs = jnp.concatenate([chosen(kv_ref, i, value_lanes), chosen(low_ref, i)], axis=1)
            mixed = nn(prob_b, rhs)
            attended = mixed[:, :DH].astype(BF16)
            att_ref[own[i], :] = attended
            t_ref[own[i], LOW:] = mixed[:, DH:].astype(BF16)
            terms = do_ref[own[i], :].astype(F32) * attended.astype(F32)
            delta = jnp.sum(terms, axis=-1, keepdims=True)
            score_grads.append((prob * (prob_grad - delta) * inverse_root).astype(BF16))
        for i, prob_b, score_grad in zip(some, probs_b, score_grads):
            rhs = jnp.concatenate([chosen(kv_ref, i, key_lanes), chosen(low_ref, i)], axis=1)
            mixed = nn(score_grad, rhs)
            dq_ref[own[i], :] = mixed[:, :DH].astype(BF16)
            t_ref[own[i], :LOW] = mixed[:, DH:].astype(BF16)
            back_ref[i, :RANK, :] = nn(query_up[:, own[i]], score_grad)
            back_ref[i, RANK:, :] = nn(grad_up[:, own[i]], prob_b)

    acc_ref[...] = acc_in[...] if which else jnp.zeros_like(acc_ref)
    acc_ref[:RANK, :rows] += nt(up_q, dq_ref[...])
    for i, starts in enumerate(all_starts):
        for e, s in enumerate(starts):
            acc_ref[RANK:, pl.ds(s, BLK)] += back_ref[i, :, e * BLK : (e + 1) * BLK]
    up_grad = adapter_scale * jnp.concatenate(
        [
            tn(low_ref[:rows, :], dq_ref[...])[0:RANK],
            tn(t_ref[:, :LOW], q_ref[...])[RANK : 2 * RANK],
            tn(t_ref[:, LOW:], do_ref[...])[2 * RANK : 3 * RANK],
        ],
        axis=0,
    )
    if which == 0:
        up_out[...] = up_grad
        return
    total = nn(acc_ref[:, :rows].astype(BF16), normed_ref[...])
    halo = jnp.zeros((2 * RANK, width), F32)
    for members, start in segments[1:]:
        halo += nn(acc_ref[RANK:, pl.ds(start, half)].astype(BF16), rows_of(members))
    sum_ref = scratch[10]
    sum_ref[:RANK, :] = total[:RANK]
    sum_ref[RANK:, :] = total[RANK:] + halo
    keep_ref[...] = sum_ref[:, half_lanes(core, width)].astype(BF16)
    send_ref[...] = sum_ref[:, half_lanes(1 - core, width)].astype(BF16)
    up_out[:, lanes_at(head)] = up_grad.astype(BF16)
    up_out[:, lanes_at(1 - head)] = up_in[...].astype(BF16)


def half_lanes(side, width):
    return pl.ds(pl.multiple_of(side * (width // 2), width // 2), width // 2)


def merge_kernel(down_ref, sibling_ref, up_ref, out_ref):
    width = down_ref.shape[1]
    out_ref[:, :width] = (down_ref[...].astype(F32) + sibling_ref[...].astype(F32)).astype(BF16)
    out_ref[:, width:] = up_ref[...]


def total_kernel(*refs):
    terms, (down_ref, up_ref) = [r[...].astype(F32) for r in refs[:-2]], refs[-2:]
    while len(terms) > 1:
        terms = [a + b for a, b in zip(terms[::2], terms[1::2])]
    width = down_ref.shape[1]
    down_ref[...] = terms[0][:, :width]
    up_ref[...] = terms[0][:, width:]


def final_kernel(own_ref, recv_ref, up_ref, out_ref, up_out):
    core, width = lax.axis_index("head"), out_ref.shape[1]
    up_out[...] = up_ref[...]
    out_ref[:, half_lanes(core, width)] = own_ref[...]
    out_ref[:, half_lanes(1 - core, width)] = recv_ref[...]


def out_kernel(order_ref, x_ref, att1_ref, att2_ref, wo1_ref, wo2_ref, base_ref, other_ref):
    rows, cols = x_ref.shape
    core = lax.axis_index("head")
    place = scatter_matrix(order_ref, rows)

    def part(side):
        span = pl.ds(pl.multiple_of(side * cols, cols), cols)
        terms = nt(att1_ref[...], wo1_ref[span, :]) + nt(att2_ref[...], wo2_ref[span, :])
        return nn(place, terms.astype(BF16))

    other_ref[...] = part(1 - core).astype(BF16)
    base_ref[...] = x_ref[...].astype(F32) + part(core)


HBM = pl.BlockSpec(memory_space=pltpu.HBM)
VMEM = pl.BlockSpec(memory_space=pltpu.VMEM)


def shape(dims, dtype=BF16):
    return jax.ShapeDtypeStruct(dims, dtype)


def call(kernel, outs, ins, scratch=(), hbm=0, flops=0, limit=None, pin=False):
    if hbm:
        ins = tuple(pltpu.with_memory_space_constraint(x, pltpu.HBM) for x in ins)
    if hbm or pin:
        outs = tuple(pltpu.VMEM(x.shape, x.dtype) for x in outs)
    return pl.pallas_call(
        kernel,
        out_shape=outs,
        in_specs=[HBM] * hbm + [VMEM] * (len(ins) - hbm),
        out_specs=(VMEM,) * len(outs),
        scratch_shapes=list(scratch),
        cost_estimate=pl.CostEstimate(flops=flops, bytes_accessed=1 << 20, transcendentals=0),
        compiler_params=pltpu.CompilerParams(vmem_limit_bytes=limit and limit * 2**20),
    )(*ins)


def swap(value, axis, step=1):
    size = lax.axis_size(axis)
    return lax.ppermute(value, axis, [(i, i ^ step) for i in range(size)])


def chain_pairs(size):
    pairs = {0: 0, size - 1: size - 1}
    for i in range(1, size - 1, 2):
        pairs[i], pairs[i + 1] = i + 1, i
    return sorted(pairs.items())


def split_kernel(a_ref, b_ref, *outs):
    rows = outs[0].shape[0]
    for out, (ref, start) in zip(outs, ((a_ref, 0), (a_ref, rows), (b_ref, 0), (b_ref, rows))):
        out[...] = ref[start : start + rows, :]


def pair_kernel(one_ref, two_ref, out_ref):
    depth = one_ref.shape[0]
    out_ref[:depth, :] = one_ref[...]
    out_ref[depth:, :] = two_ref[...]


def gather_weights(first, second, half):
    count, depth = lax.axis_size("node"), first.shape[0]
    if not split_weights():
        whole = [lax.all_gather(m, "node", axis=0, tiled=True) for m in (first, second)]
        return [whole[:1], whole[1:]], lambda node: [0], whole
    far_pairs = [(g * 4 + n, g * 4 + (n ^ (2 + g))) for g in range(2) for n in range(4)]
    far = lax.ppermute(first, ("group", "node"), far_pairs)
    near = swap(first, "node")
    far, near, _ = lax.optimization_barrier((far, near, half))
    other_far = swap(far, "group")
    pair = call(pair_kernel, (shape((2 * depth, 4 * DH)),), (near, far), limit=16)[0]
    pair = swap(pair, "sample")
    theirs = [second, pair, swap(other_far, "sample")]

    def piece_rows(node):
        group = lax.axis_index("group")
        return [jnp.bitwise_xor(node, k) * depth for k in (0, 1, 2 + group, 3 - group)]

    return [[first, near, far, other_far], theirs], piece_rows, other_far


def split_weights():
    return lax.axis_size("node") == 4 and lax.axis_size("group") == 2 and lax.axis_size("sample") == 2


def shards(
    mesh_node_state,
    cotangent,
    query_weight,
    key_weight,
    value_weight,
    output_weight,
    adapter_down_weight,
    adapter_up_weight,
    neighbour_key_blocks,
    block_node_order,
):
    _, rows, width = mesh_node_state.shape
    cols = query_weight.shape[1]
    depth = query_weight.shape[0]
    state = mesh_node_state[0]
    order = block_node_order.reshape(1, rows)
    split = split_weights()

    packed = call(
        functools.partial(pack_kernel, split),
        (shape((depth, 4 * DH)),) * 2,
        (query_weight, key_weight, value_weight, output_weight),
        [pltpu.VMEM((depth, cols), BF16)] * 3
        + [pltpu.VMEM((cols, depth), BF16), pltpu.SemaphoreType.DMA((4,))],
        hbm=4,
        limit=16,
    )
    order, _ = lax.optimization_barrier((order, packed[0]))
    order, table, down, up, x_own, normed, half, cot_own = call(
        prep_kernel,
        (
            shape((1, rows), jnp.int32),
            shape(neighbour_key_blocks.shape[::-1], jnp.int32),
            shape((3 * RANK, width)),
            shape((3 * RANK, cols)),
            shape((rows, cols)),
            shape((rows, width)),
            shape((rows // 2, width)),
            shape((rows, cols)),
        ),
        (
            order,
            state,
            cotangent[0],
            adapter_down_weight.transpose(0, 2, 1).reshape(3 * RANK, width),
            adapter_up_weight.reshape(3 * RANK, cols),
            neighbour_key_blocks.T,
        ),
        [
            pltpu.VMEM((rows, width), BF16),
            pltpu.VMEM((rows, cols), BF16),
            pltpu.SemaphoreType.DMA((6,)),
        ],
        hbm=6,
        flops=2 * rows * rows * (width + cols),
        limit=16,
    )
    pieces, piece_rows, late = gather_weights(*packed, half)
    a_own = swap(half, "node", 1)
    b_own = lax.ppermute(half, "node", chain_pairs(lax.axis_size("node")))
    cot_sib = swap(cot_own, "head")
    a_half, b_half, _ = lax.optimization_barrier((a_own, b_own, late))
    quarters = call(split_kernel, (shape((rows // 4, width)),) * 4, (a_half, b_half), limit=16)
    a_sib, a_sib2, b_sib, b_sib2 = [swap(q, "head") for q in quarters]

    shared = (
        table,
        normed,
        a_own,
        a_sib,
        a_sib2,
        b_own,
        b_sib,
        b_sib2,
        cot_own,
        cot_sib,
        down,
        up,
    )
    entries = neighbour_key_blocks.shape[1]
    scratch = [
        pltpu.VMEM((width + LOW, 4 * DH), BF16),
        pltpu.VMEM((3 * rows, 2 * DH), BF16),
        pltpu.VMEM((rows, DH), BF16),
        pltpu.VMEM((rows, DH), BF16),
        pltpu.VMEM((rows, DH), BF16),
        pltpu.VMEM((rows, 2 * LOW), BF16),
        pltpu.VMEM((rows // BLK, 2 * RANK, entries * BLK), F32),
        pltpu.VMEM((3 * RANK, 3 * rows), F32),
        pltpu.SMEM(table.shape, jnp.int32),
        pltpu.SemaphoreType.DMA,
        pltpu.VMEM((3 * RANK, width), F32),
    ]
    att1, wo1, low, acc, up1 = call(
        functools.partial(head_kernel, split, 0, piece_rows),
        (
            shape((rows, DH)),
            shape((width, DH)),
            shape((3 * rows, LOW)),
            shape((3 * RANK, 3 * rows), F32),
            shape((3 * RANK, DH), F32),
        ),
        shared + tuple(pieces[0]),
        scratch,
        limit=32,
    )
    att2, wo2, keep, send, up2 = call(
        functools.partial(head_kernel, split, 1, piece_rows),
        (
            shape((rows, DH)),
            shape((width, DH)),
            shape((3 * RANK, width // 2)),
            shape((3 * RANK, width // 2)),
            shape((3 * RANK, cols)),
        ),
        shared + (low, acc, up1) + tuple(pieces[1]),
        scratch,
        limit=32,
        flops=4 * 10**9,
    )
    received = swap(send, "head")
    base, other = call(
        out_kernel,
        (shape((rows, cols), F32), shape((rows, cols))),
        (order, x_own, att1, att2, wo1, wo2),
        flops=10**9,
        limit=16,
    )
    mesh_out = (base + swap(other, "head").astype(F32)).astype(BF16)[None]
    size = (3 * RANK, width // 2 + cols)
    lora = call(merge_kernel, (shape(size),), (keep, received, up2), limit=16)[0]
    hops = [("sample", 1 << i) for i in range(lax.axis_size("sample").bit_length() - 1)]
    count = lax.axis_size("node")
    if count != 4:
        hops += [("node", 1 << i) for i in range(count.bit_length() - 2)]
    for axis, step in hops:
        lora = (lora.astype(F32) + swap(lora, axis, step).astype(F32)).astype(BF16)
    steps = (1, 2, 3) if count == 4 else (count // 2,)
    terms = (lora, *[swap(lora, "node", k) for k in steps])
    terms, mesh_out = lax.optimization_barrier((terms, mesh_out))
    down_half, up_total = call(
        total_kernel,
        (shape((3 * RANK, width // 2), F32), shape((3 * RANK, cols), F32)),
        terms,
        limit=16,
        pin=True,
    )
    down_total, up_total = call(
        final_kernel,
        (shape((3 * RANK, width), F32), shape((3 * RANK, cols), F32)),
        (down_half, swap(down_half, "head"), up_total),
        limit=16,
    )
    down_total = down_total.reshape(3, RANK, width).transpose(0, 2, 1)
    up_total = up_total.reshape(3, RANK, cols)
    return (mesh_out, down_total, up_total)


def solution(mesh):
    in_specs = (
        P(("group", "sample"), "node", None),
        P(("group", "sample"), "node", "head"),
        P("node", "head"),
        P("node", "head"),
        P("node", "head"),
        P("head", "node"),
        P(),
        P(None, None, "head"),
        P(),
        P("node"),
    )
    out_specs = (
        P(("group", "sample"), "node", "head"),
        P("group", None, None),
        P("group", None, "head"),
    )
    return jax.shard_map(shards, mesh=mesh, in_specs=in_specs, out_specs=out_specs, check_vma=False)
```

```python
import functools
import math

import jax
import jax.numpy as jnp
from jax import lax
from jax.experimental import pallas as pl
from jax.experimental.pallas import tpu as pltpu
from jax.sharding import PartitionSpec as P

DH = 128
BLK = 128
RANK = 16
LOW = 128

adapter_scale = 0.5
masked_value = -1e30
F32 = jnp.float32
BF16 = jnp.bfloat16


def nn(a, b):
    return lax.dot_general(a, b, (((1,), (0,)), ((), ())), preferred_element_type=F32)


def nt(a, b):
    return lax.dot_general(a, b, (((1,), (1,)), ((), ())), preferred_element_type=F32)


def tn(a, b):
    return lax.dot_general(a, b, (((0,), (0,)), ((), ())), preferred_element_type=F32)


def scatter_matrix(order_ref, rows):
    local = order_ref[...] - lax.axis_index("node") * rows
    nodes = lax.broadcasted_iota(jnp.int32, (rows, rows), 0)
    return jnp.where(nodes == local, 1.0, 0.0).astype(BF16)


def head_at(split, which):
    if not split:
        return which
    return jnp.bitwise_xor(lax.rem(lax.axis_index("sample"), 2), which)


def lanes_at(index):
    if isinstance(index, int):
        return pl.ds(index * DH, DH)
    return pl.ds(pl.multiple_of(index * DH, DH), DH)


def load_all(sources, buffers, sems):
    copies = [pltpu.make_async_copy(a, b, sems.at[i]) for i, (a, b) in enumerate(zip(sources, buffers))]
    for copy in copies:
        copy.start()
    return copies


def pack_kernel(split, *refs):
    sources, outs, buffers, sems = refs[:4], refs[4:6], refs[6:-1], refs[-1]
    for copy in load_all(sources, buffers, sems):
        copy.wait()
    for which, out in enumerate(outs):
        lanes = lanes_at(head_at(split, which))
        for j, member in enumerate(buffers[:3]):
            out[:, j * DH : (j + 1) * DH] = member[:, lanes]
        out[:, 3 * DH :] = buffers[3][lanes, :].T


def prep_kernel(*refs):
    sources, outs, buffers, sems = refs[:6], refs[6:-3], refs[-3:-1], refs[-1]
    order_ref, table_ref, down_ref, up_ref, x_own_ref, normed_ref, half_ref, cot_out_ref = outs
    x_ref, cot_ref = buffers
    copies = load_all(sources, (order_ref, x_ref, cot_ref, down_ref, up_ref, table_ref), sems)
    rows = x_ref.shape[0]
    copies[0].wait()
    place = scatter_matrix(order_ref, rows)
    copies[1].wait()
    ordered = tn(place, x_ref[...])
    center = ordered - jnp.mean(ordered, axis=-1, keepdims=True)
    spread = jnp.mean(center * center, axis=-1, keepdims=True)
    normed_ref[...] = (center * lax.rsqrt(spread + 1e-05)).astype(BF16)
    start = pl.multiple_of(lax.axis_index("head") * (rows // 2), rows // 2)
    half_ref[...] = normed_ref[pl.ds(start, rows // 2), :]
    for copy in copies[2:]:
        copy.wait()
    cot_out_ref[...] = tn(place, cot_ref[...]).astype(BF16)
    cols = x_own_ref.shape[1]
    x_own_ref[...] = x_ref[:, pl.ds(pl.multiple_of(lax.axis_index("head") * cols, cols), cols)]


def head_kernel(split, which, piece_rows, *refs):
    table_vmem, normed_ref, a_own_ref, a_sib_ref, a_sib2_ref = refs[:5]
    b_own_ref, b_sib_ref, b_sib2_ref, cot_own_ref, cot_sib_ref, down_ref, up_ref = refs[5:12]
    rest, scratch = refs[12:-11], refs[-11:]
    if which == 0:
        pieces, (att_ref, wo_ref, low_ref, acc_ref, up_out) = rest[:-5], rest[-5:]
    else:
        low_ref, acc_in, up_in = rest[:3]
        pieces, (att_ref, wo_ref, keep_ref, send_ref, up_out) = rest[3:-5], rest[-5:]
    w_ref, kv_ref, q_ref, do_ref, dq_ref, t_ref, back_ref = scratch[:7]
    table_ref, table_sem = scratch[8:10]
    if which:
        acc_ref = scratch[7]
    table_copy = pltpu.make_async_copy(table_vmem, table_ref, table_sem)
    table_copy.start()
    rows, width = normed_ref.shape
    blocks, half = rows // BLK, rows // 2
    node, core = lax.axis_index("node"), lax.axis_index("head")
    head = head_at(split, which)
    first = node * blocks
    inverse_root = 1.0 / math.sqrt(DH)

    places = piece_rows(node)
    step = width // len(places)
    for piece in pieces:
        for j in range(0, piece.shape[0], step):
            row, *places = places
            start = row if isinstance(row, int) else pl.multiple_of(row, step)
            w_ref[pl.ds(start, step), :] = piece[j : j + step, :]
    wo_ref[...] = w_ref[:width, 3 * DH :]
    w_ref[width:, :] = jnp.zeros((LOW, 4 * DH), BF16)
    for j in range(3):
        span = slice(j * RANK, (j + 1) * RANK)
        w_ref[width + j * RANK : width + (j + 1) * RANK, j * DH : (j + 1) * DH] = (
            adapter_scale * up_ref[span, lanes_at(head)]
        )

    segments = [
        ((normed_ref,), 0),
        ((a_own_ref,), pl.multiple_of(rows + core * half, half)),
        ((a_sib_ref, a_sib2_ref), pl.multiple_of(rows + (1 - core) * half, half)),
        ((b_own_ref,), pl.multiple_of(2 * rows + core * half, half)),
        ((b_sib_ref, b_sib2_ref), pl.multiple_of(2 * rows + (1 - core) * half, half)),
    ]
    def rows_of(members):
        return jnp.concatenate([m[...] for m in members], axis=0)

    if which == 0:
        for members, start in segments:
            low = nt(rows_of(members), down_ref[...]).astype(BF16)
            blank = jnp.zeros((low.shape[0], LOW - 3 * RANK), BF16)
            low_ref[pl.ds(start, low.shape[0]), :] = jnp.concatenate([low, blank], axis=1)
    for j, (members, start) in enumerate(segments):
        span = pl.ds(start, half if j else rows)
        value = jnp.concatenate([rows_of(members), low_ref[span, :]], axis=1)
        projected = nn(value, w_ref[:, (DH if j else 0) : 3 * DH]).astype(BF16)
        if j == 0:
            q_ref[...] = projected[:, :DH]
        kv_ref[span, :] = projected[:, -2 * DH :]

    def out_rows(side):
        return w_ref[pl.ds(pl.multiple_of(side * (width // 2), width // 2), width // 2), 3 * DH :]

    do_ref[...] = (
        nn(cot_own_ref[...], out_rows(core)) + nn(cot_sib_ref[...], out_rows(1 - core))
    ).astype(BF16)
    up_q = w_ref[width : width + RANK, :DH]
    up_k = w_ref[width + RANK : width + 2 * RANK, DH : 2 * DH]
    up_v = w_ref[width + 2 * RANK : width + 3 * RANK, 2 * DH : 3 * DH]
    query_up = nt(up_k, q_ref[...]).astype(BF16)
    grad_up = nt(up_v, do_ref[...]).astype(BF16)

    table_copy.wait()
    odd = lax.rem(node, 2)
    left, right = 2 - odd, 1 + odd
    all_starts, all_valid = [], []
    for i in range(blocks):
        named = [table_ref[e, first + i] for e in range(table_ref.shape[0])]
        starts, valid = [], []
        for e, c in enumerate(named):
            rel = c - first
            block = jnp.where(
                rel < 0,
                left * blocks + rel + blocks,
                jnp.where(rel >= blocks, (right - 1) * blocks + rel, rel),
            )
            starts.append(pl.multiple_of(block * BLK, BLK))
            fresh = c >= 0
            for before in named[:e]:
                fresh = jnp.logical_and(fresh, c != before)
            valid.append(fresh)
        all_starts.append(starts)
        all_valid.append(valid)

    def chosen(ref, i, lanes=slice(None)):
        return jnp.concatenate([ref[pl.ds(s, BLK), lanes] for s in all_starts[i]], axis=0)

    def masked(scores, i):
        return jnp.concatenate(
            [
                jnp.where(ok, scores[:, e * BLK : (e + 1) * BLK], masked_value)
                for e, ok in enumerate(all_valid[i])
            ],
            axis=1,
        )

    units = range(blocks)
    own = [slice(i * BLK, (i + 1) * BLK) for i in units]
    key_lanes, value_lanes = slice(0, DH), slice(DH, 2 * DH)
    for base in range(0, blocks, 4):
        some = range(base, base + 4)
        scores = [
            masked(nt(q_ref[own[i], :], chosen(kv_ref, i, key_lanes)) * inverse_root, i) for i in some
        ]
        prob_grads = [nt(do_ref[own[i], :], chosen(kv_ref, i, value_lanes)) for i in some]
        probs, probs_b, score_grads = [], [], []
        for score in scores:
            weights = jnp.exp(score - jnp.max(score, axis=-1, keepdims=True))
            prob = weights * (1.0 / jnp.sum(weights, axis=-1, keepdims=True))
            probs.append(prob)
            probs_b.append(prob.astype(BF16))
        for i, prob, prob_b, prob_grad in zip(some, probs, probs_b, prob_grads):
            rhs = jnp.concatenate([chosen(kv_ref, i, value_lanes), chosen(low_ref, i)], axis=1)
            mixed = nn(prob_b, rhs)
            attended = mixed[:, :DH].astype(BF16)
            att_ref[own[i], :] = attended
            t_ref[own[i], LOW:] = mixed[:, DH:].astype(BF16)
            terms = do_ref[own[i], :].astype(F32) * attended.astype(F32)
            delta = jnp.sum(terms, axis=-1, keepdims=True)
            score_grads.append((prob * (prob_grad - delta) * inverse_root).astype(BF16))
        for i, prob_b, score_grad in zip(some, probs_b, score_grads):
            rhs = jnp.concatenate([chosen(kv_ref, i, key_lanes), chosen(low_ref, i)], axis=1)
            mixed = nn(score_grad, rhs)
            dq_ref[own[i], :] = mixed[:, :DH].astype(BF16)
            t_ref[own[i], :LOW] = mixed[:, DH:].astype(BF16)
            back_ref[i, :RANK, :] = nn(query_up[:, own[i]], score_grad)
            back_ref[i, RANK:, :] = nn(grad_up[:, own[i]], prob_b)

    acc_ref[...] = acc_in[...] if which else jnp.zeros_like(acc_ref)
    acc_ref[:RANK, :rows] += nt(up_q, dq_ref[...])
    for i, starts in enumerate(all_starts):
        for e, s in enumerate(starts):
            acc_ref[RANK:, pl.ds(s, BLK)] += back_ref[i, :, e * BLK : (e + 1) * BLK]
    up_grad = adapter_scale * jnp.concatenate(
        [
            tn(low_ref[:rows, :], dq_ref[...])[0:RANK],
            tn(t_ref[:, :LOW], q_ref[...])[RANK : 2 * RANK],
            tn(t_ref[:, LOW:], do_ref[...])[2 * RANK : 3 * RANK],
        ],
        axis=0,
    )
    if which == 0:
        up_out[...] = up_grad
        return
    total = nn(acc_ref[:, :rows].astype(BF16), normed_ref[...])
    halo = jnp.zeros((2 * RANK, width), F32)
    for members, start in segments[1:]:
        halo += nn(acc_ref[RANK:, pl.ds(start, half)].astype(BF16), rows_of(members))
    sum_ref = scratch[10]
    sum_ref[:RANK, :] = total[:RANK]
    sum_ref[RANK:, :] = total[RANK:] + halo
    keep_ref[...] = sum_ref[:, half_lanes(core, width)].astype(BF16)
    send_ref[...] = sum_ref[:, half_lanes(1 - core, width)].astype(BF16)
    up_out[:, lanes_at(head)] = up_grad.astype(BF16)
    up_out[:, lanes_at(1 - head)] = up_in[...].astype(BF16)


def half_lanes(side, width):
    return pl.ds(pl.multiple_of(side * (width // 2), width // 2), width // 2)


def merge_kernel(down_ref, sibling_ref, up_ref, out_ref):
    width = down_ref.shape[1]
    out_ref[:, :width] = (down_ref[...].astype(F32) + sibling_ref[...].astype(F32)).astype(BF16)
    out_ref[:, width:] = up_ref[...]


def total_kernel(*refs):
    terms, (down_ref, up_ref) = [r[...].astype(F32) for r in refs[:-2]], refs[-2:]
    while len(terms) > 1:
        terms = [a + b for a, b in zip(terms[::2], terms[1::2])]
    width = down_ref.shape[1]
    down_ref[...] = terms[0][:, :width]
    up_ref[...] = terms[0][:, width:]


def final_kernel(own_ref, recv_ref, up_ref, out_ref, up_out):
    core, width = lax.axis_index("head"), out_ref.shape[1]
    up_out[...] = up_ref[...]
    out_ref[:, half_lanes(core, width)] = own_ref[...]
    out_ref[:, half_lanes(1 - core, width)] = recv_ref[...]


def out_kernel(order_ref, x_ref, att1_ref, att2_ref, wo1_ref, wo2_ref, base_ref, other_ref):
    rows, cols = x_ref.shape
    core = lax.axis_index("head")
    place = scatter_matrix(order_ref, rows)

    def part(side):
        span = pl.ds(pl.multiple_of(side * cols, cols), cols)
        terms = nt(att1_ref[...], wo1_ref[span, :]) + nt(att2_ref[...], wo2_ref[span, :])
        return nn(place, terms.astype(BF16))

    other_ref[...] = part(1 - core).astype(BF16)
    base_ref[...] = x_ref[...].astype(F32) + part(core)


HBM = pl.BlockSpec(memory_space=pltpu.HBM)
VMEM = pl.BlockSpec(memory_space=pltpu.VMEM)


def shape(dims, dtype=BF16):
    return jax.ShapeDtypeStruct(dims, dtype)


def call(kernel, outs, ins, scratch=(), hbm=0, flops=0, limit=None, pin=False):
    if hbm:
        ins = tuple(pltpu.with_memory_space_constraint(x, pltpu.HBM) for x in ins)
    if hbm or pin:
        outs = tuple(pltpu.VMEM(x.shape, x.dtype) for x in outs)
    return pl.pallas_call(
        kernel,
        out_shape=outs,
        in_specs=[HBM] * hbm + [VMEM] * (len(ins) - hbm),
        out_specs=(VMEM,) * len(outs),
        scratch_shapes=list(scratch),
        cost_estimate=pl.CostEstimate(flops=flops, bytes_accessed=1 << 20, transcendentals=0),
        compiler_params=pltpu.CompilerParams(vmem_limit_bytes=limit and limit * 2**20),
    )(*ins)


def swap(value, axis, step=1):
    size = lax.axis_size(axis)
    return lax.ppermute(value, axis, [(i, i ^ step) for i in range(size)])


def chain_pairs(size):
    pairs = {0: 0, size - 1: size - 1}
    for i in range(1, size - 1, 2):
        pairs[i], pairs[i + 1] = i + 1, i
    return sorted(pairs.items())


def split_kernel(a_ref, b_ref, *outs):
    rows = outs[0].shape[0]
    for out, (ref, start) in zip(outs, ((a_ref, 0), (a_ref, rows), (b_ref, 0), (b_ref, rows))):
        out[...] = ref[start : start + rows, :]


def pair_kernel(one_ref, two_ref, out_ref):
    depth = one_ref.shape[0]
    out_ref[:depth, :] = one_ref[...]
    out_ref[depth:, :] = two_ref[...]


def gather_weights(first, second, half):
    count, depth = lax.axis_size("node"), first.shape[0]
    if not split_weights():
        whole = [lax.all_gather(m, "node", axis=0, tiled=True) for m in (first, second)]
        return [whole[:1], whole[1:]], lambda node: [0], whole
    far_pairs = [(g * 4 + n, g * 4 + (n ^ (2 + g))) for g in range(2) for n in range(4)]
    far = lax.ppermute(first, ("group", "node"), far_pairs)
    near = swap(first, "node")
    far, near, _ = lax.optimization_barrier((far, near, half))
    other_far = swap(far, "group")
    pair = call(pair_kernel, (shape((2 * depth, 4 * DH)),), (near, far), limit=16)[0]
    pair = swap(pair, "sample")
    theirs = [second, pair, swap(other_far, "sample")]

    def piece_rows(node):
        group = lax.axis_index("group")
        return [jnp.bitwise_xor(node, k) * depth for k in (0, 1, 2 + group, 3 - group)]

    return [[first, near, far, other_far], theirs], piece_rows, other_far


def split_weights():
    return lax.axis_size("node") == 4 and lax.axis_size("group") == 2 and lax.axis_size("sample") == 2


def shards(
    mesh_node_state,
    cotangent,
    query_weight,
    key_weight,
    value_weight,
    output_weight,
    adapter_down_weight,
    adapter_up_weight,
    neighbour_key_blocks,
    block_node_order,
):
    _, rows, width = mesh_node_state.shape
    cols = query_weight.shape[1]
    depth = query_weight.shape[0]
    state = mesh_node_state[0]
    order = block_node_order.reshape(1, rows)
    split = split_weights()

    packed = call(
        functools.partial(pack_kernel, split),
        (shape((depth, 4 * DH)),) * 2,
        (query_weight, key_weight, value_weight, output_weight),
        [pltpu.VMEM((depth, cols), BF16)] * 3
        + [pltpu.VMEM((cols, depth), BF16), pltpu.SemaphoreType.DMA((4,))],
        hbm=4,
        limit=16,
    )
    order, _ = lax.optimization_barrier((order, packed[0]))
    order, table, down, up, x_own, normed, half, cot_own = call(
        prep_kernel,
        (
            shape((1, rows), jnp.int32),
            shape(neighbour_key_blocks.shape[::-1], jnp.int32),
            shape((3 * RANK, width)),
            shape((3 * RANK, cols)),
            shape((rows, cols)),
            shape((rows, width)),
            shape((rows // 2, width)),
            shape((rows, cols)),
        ),
        (
            order,
            state,
            cotangent[0],
            adapter_down_weight.transpose(0, 2, 1).reshape(3 * RANK, width),
            adapter_up_weight.reshape(3 * RANK, cols),
            neighbour_key_blocks.T,
        ),
        [
            pltpu.VMEM((rows, width), BF16),
            pltpu.VMEM((rows, cols), BF16),
            pltpu.SemaphoreType.DMA((6,)),
        ],
        hbm=6,
        flops=2 * rows * rows * (width + cols),
        limit=16,
    )
    pieces, piece_rows, late = gather_weights(*packed, half)
    a_own = swap(half, "node", 1)
    b_own = lax.ppermute(half, "node", chain_pairs(lax.axis_size("node")))
    cot_sib = swap(cot_own, "head")
    a_half, b_half, _ = lax.optimization_barrier((a_own, b_own, late))
    quarters = call(split_kernel, (shape((rows // 4, width)),) * 4, (a_half, b_half), limit=16)
    a_sib, a_sib2, b_sib, b_sib2 = [swap(q, "head") for q in quarters]

    shared = (
        table,
        normed,
        a_own,
        a_sib,
        a_sib2,
        b_own,
        b_sib,
        b_sib2,
        cot_own,
        cot_sib,
        down,
        up,
    )
    entries = neighbour_key_blocks.shape[1]
    scratch = [
        pltpu.VMEM((width + LOW, 4 * DH), BF16),
        pltpu.VMEM((3 * rows, 2 * DH), BF16),
        pltpu.VMEM((rows, DH), BF16),
        pltpu.VMEM((rows, DH), BF16),
        pltpu.VMEM((rows, DH), BF16),
        pltpu.VMEM((rows, 2 * LOW), BF16),
        pltpu.VMEM((rows // BLK, 2 * RANK, entries * BLK), F32),
        pltpu.VMEM((3 * RANK, 3 * rows), F32),
        pltpu.SMEM(table.shape, jnp.int32),
        pltpu.SemaphoreType.DMA,
        pltpu.VMEM((3 * RANK, width), F32),
    ]
    att1, wo1, low, acc, up1 = call(
        functools.partial(head_kernel, split, 0, piece_rows),
        (
            shape((rows, DH)),
            shape((width, DH)),
            shape((3 * rows, LOW)),
            shape((3 * RANK, 3 * rows), F32),
            shape((3 * RANK, DH), F32),
        ),
        shared + tuple(pieces[0]),
        scratch,
        limit=32,
    )
    att2, wo2, keep, send, up2 = call(
        functools.partial(head_kernel, split, 1, piece_rows),
        (
            shape((rows, DH)),
            shape((width, DH)),
            shape((3 * RANK, width // 2)),
            shape((3 * RANK, width // 2)),
            shape((3 * RANK, cols)),
        ),
        shared + (low, acc, up1) + tuple(pieces[1]),
        scratch,
        limit=32,
        flops=4 * 10**9,
    )
    received = swap(send, "head")
    base, other = call(
        out_kernel,
        (shape((rows, cols), F32), shape((rows, cols))),
        (order, x_own, att1, att2, wo1, wo2),
        flops=10**9,
        limit=16,
    )
    mesh_out = (base + swap(other, "head").astype(F32)).astype(BF16)[None]
    size = (3 * RANK, width // 2 + cols)
    lora = call(merge_kernel, (shape(size),), (keep, received, up2), limit=16)[0]
    hops = [("sample", 1 << i) for i in range(lax.axis_size("sample").bit_length() - 1)]
    count = lax.axis_size("node")
    if count != 4:
        hops += [("node", 1 << i) for i in range(count.bit_length() - 2)]
    for axis, step in hops:
        lora = (lora.astype(F32) + swap(lora, axis, step).astype(F32)).astype(BF16)
    steps = (3, 2, 1) if count == 4 else (count // 2,)
    terms = (lora, *[swap(lora, "node", k) for k in steps])
    terms, mesh_out = lax.optimization_barrier((terms, mesh_out))
    down_half, up_total = call(
        total_kernel,
        (shape((3 * RANK, width // 2), F32), shape((3 * RANK, cols), F32)),
        terms,
        limit=16,
        pin=True,
    )
    down_total, up_total = call(
        final_kernel,
        (shape((3 * RANK, width), F32), shape((3 * RANK, cols), F32)),
        (down_half, swap(down_half, "head"), up_total),
        limit=16,
    )
    down_total = down_total.reshape(3, RANK, width).transpose(0, 2, 1)
    up_total = up_total.reshape(3, RANK, cols)
    return (mesh_out, down_total, up_total)


def solution(mesh):
    in_specs = (
        P(("group", "sample"), "node", None),
        P(("group", "sample"), "node", "head"),
        P("node", "head"),
        P("node", "head"),
        P("node", "head"),
        P("head", "node"),
        P(),
        P(None, None, "head"),
        P(),
        P("node"),
    )
    out_specs = (
        P(("group", "sample"), "node", "head"),
        P("group", None, None),
        P("group", None, "head"),
    )
    return jax.shard_map(shards, mesh=mesh, in_specs=in_specs, out_specs=out_specs, check_vma=False)
```

```python
import functools
import math

import jax
import jax.numpy as jnp
from jax import lax
from jax.experimental import pallas as pl
from jax.experimental.pallas import tpu as pltpu
from jax.sharding import PartitionSpec as P

DH = 128
BLK = 128
RANK = 16
LOW = 128

adapter_scale = 0.5
masked_value = -1e30
F32 = jnp.float32
BF16 = jnp.bfloat16


def nn(a, b):
    return lax.dot_general(a, b, (((1,), (0,)), ((), ())), preferred_element_type=F32)


def nt(a, b):
    return lax.dot_general(a, b, (((1,), (1,)), ((), ())), preferred_element_type=F32)


def tn(a, b):
    return lax.dot_general(a, b, (((0,), (0,)), ((), ())), preferred_element_type=F32)


def scatter_matrix(order_ref, rows):
    local = order_ref[...] - lax.axis_index("node") * rows
    nodes = lax.broadcasted_iota(jnp.int32, (rows, rows), 0)
    return jnp.where(nodes == local, 1.0, 0.0).astype(BF16)


def head_at(split, which):
    if not split:
        return which
    return jnp.bitwise_xor(lax.rem(lax.axis_index("sample"), 2), which)


def lanes_at(index):
    if isinstance(index, int):
        return pl.ds(index * DH, DH)
    return pl.ds(pl.multiple_of(index * DH, DH), DH)


def load_all(sources, buffers, sems):
    copies = [pltpu.make_async_copy(a, b, sems.at[i]) for i, (a, b) in enumerate(zip(sources, buffers))]
    for copy in copies:
        copy.start()
    return copies


def pack_kernel(split, *refs):
    sources, outs, buffers, sems = refs[:4], refs[4:6], refs[6:-1], refs[-1]
    for copy in load_all(sources, buffers, sems):
        copy.wait()
    for which, out in enumerate(outs):
        lanes = lanes_at(head_at(split, which))
        for j, member in enumerate(buffers[:3]):
            out[:, j * DH : (j + 1) * DH] = member[:, lanes]
        out[:, 3 * DH :] = buffers[3][lanes, :].T


def prep_kernel(*refs):
    sources, outs, buffers, sems = refs[:6], refs[6:-3], refs[-3:-1], refs[-1]
    order_ref, table_ref, down_ref, up_ref, x_own_ref, normed_ref, half_ref, cot_out_ref = outs
    x_ref, cot_ref = buffers
    copies = load_all(sources, (order_ref, x_ref, cot_ref, down_ref, up_ref, table_ref), sems)
    rows = x_ref.shape[0]
    copies[0].wait()
    place = scatter_matrix(order_ref, rows)
    copies[1].wait()
    ordered = tn(place, x_ref[...])
    center = ordered - jnp.mean(ordered, axis=-1, keepdims=True)
    spread = jnp.mean(center * center, axis=-1, keepdims=True)
    normed_ref[...] = (center * lax.rsqrt(spread + 1e-05)).astype(BF16)
    start = pl.multiple_of(lax.axis_index("head") * (rows // 2), rows // 2)
    half_ref[...] = normed_ref[pl.ds(start, rows // 2), :]
    for copy in copies[2:]:
        copy.wait()
    cot_out_ref[...] = tn(place, cot_ref[...]).astype(BF16)
    cols = x_own_ref.shape[1]
    x_own_ref[...] = x_ref[:, pl.ds(pl.multiple_of(lax.axis_index("head") * cols, cols), cols)]


def head_kernel(split, which, piece_rows, *refs):
    table_vmem, normed_ref, a_own_ref, a_sib_ref, a_sib2_ref = refs[:5]
    b_own_ref, b_sib_ref, b_sib2_ref, cot_own_ref, cot_sib_ref, down_ref, up_ref = refs[5:12]
    rest, scratch = refs[12:-11], refs[-11:]
    if which == 0:
        pieces, (att_ref, wo_ref, low_ref, acc_ref, up_out) = rest[:-5], rest[-5:]
    else:
        low_ref, acc_in, up_in = rest[:3]
        pieces, (att_ref, wo_ref, keep_ref, send_ref, up_out) = rest[3:-5], rest[-5:]
    w_ref, kv_ref, q_ref, do_ref, dq_ref, t_ref, back_ref = scratch[:7]
    table_ref, table_sem = scratch[8:10]
    if which:
        acc_ref = scratch[7]
    table_copy = pltpu.make_async_copy(table_vmem, table_ref, table_sem)
    table_copy.start()
    rows, width = normed_ref.shape
    blocks, half = rows // BLK, rows // 2
    node, core = lax.axis_index("node"), lax.axis_index("head")
    head = head_at(split, which)
    first = node * blocks
    inverse_root = 1.0 / math.sqrt(DH)

    places = piece_rows(node)
    step = width // len(places)
    for piece in pieces:
        for j in range(0, piece.shape[0], step):
            row, *places = places
            start = row if isinstance(row, int) else pl.multiple_of(row, step)
            w_ref[pl.ds(start, step), :] = piece[j : j + step, :]
    wo_ref[...] = w_ref[:width, 3 * DH :]
    w_ref[width:, :] = jnp.zeros((LOW, 4 * DH), BF16)
    for j in range(3):
        span = slice(j * RANK, (j + 1) * RANK)
        w_ref[width + j * RANK : width + (j + 1) * RANK, j * DH : (j + 1) * DH] = (
            adapter_scale * up_ref[span, lanes_at(head)]
        )

    segments = [
        ((normed_ref,), 0),
        ((a_own_ref,), pl.multiple_of(rows + core * half, half)),
        ((a_sib_ref, a_sib2_ref), pl.multiple_of(rows + (1 - core) * half, half)),
        ((b_own_ref,), pl.multiple_of(2 * rows + core * half, half)),
        ((b_sib_ref, b_sib2_ref), pl.multiple_of(2 * rows + (1 - core) * half, half)),
    ]
    def rows_of(members):
        return jnp.concatenate([m[...] for m in members], axis=0)

    if which == 0:
        for members, start in segments:
            low = nt(rows_of(members), down_ref[...]).astype(BF16)
            blank = jnp.zeros((low.shape[0], LOW - 3 * RANK), BF16)
            low_ref[pl.ds(start, low.shape[0]), :] = jnp.concatenate([low, blank], axis=1)
    for j, (members, start) in enumerate(segments):
        span = pl.ds(start, half if j else rows)
        value = jnp.concatenate([rows_of(members), low_ref[span, :]], axis=1)
        projected = nn(value, w_ref[:, (DH if j else 0) : 3 * DH]).astype(BF16)
        if j == 0:
            q_ref[...] = projected[:, :DH]
        kv_ref[span, :] = projected[:, -2 * DH :]

    def out_rows(side):
        return w_ref[pl.ds(pl.multiple_of(side * (width // 2), width // 2), width // 2), 3 * DH :]

    do_ref[...] = (
        nn(cot_own_ref[...], out_rows(core)) + nn(cot_sib_ref[...], out_rows(1 - core))
    ).astype(BF16)
    up_q = w_ref[width : width + RANK, :DH]
    up_k = w_ref[width + RANK : width + 2 * RANK, DH : 2 * DH]
    up_v = w_ref[width + 2 * RANK : width + 3 * RANK, 2 * DH : 3 * DH]
    query_up = nt(up_k, q_ref[...]).astype(BF16)
    grad_up = nt(up_v, do_ref[...]).astype(BF16)

    table_copy.wait()
    odd = lax.rem(node, 2)
    left, right = 2 - odd, 1 + odd
    all_starts, all_valid = [], []
    for i in range(blocks):
        named = [table_ref[e, first + i] for e in range(table_ref.shape[0])]
        starts, valid = [], []
        for e, c in enumerate(named):
            rel = c - first
            block = jnp.where(
                rel < 0,
                left * blocks + rel + blocks,
                jnp.where(rel >= blocks, (right - 1) * blocks + rel, rel),
            )
            starts.append(pl.multiple_of(block * BLK, BLK))
            fresh = c >= 0
            for before in named[:e]:
                fresh = jnp.logical_and(fresh, c != before)
            valid.append(fresh)
        all_starts.append(starts)
        all_valid.append(valid)

    def chosen(ref, i, lanes=slice(None)):
        return jnp.concatenate([ref[pl.ds(s, BLK), lanes] for s in all_starts[i]], axis=0)

    def masked(scores, i):
        return jnp.concatenate(
            [
                jnp.where(ok, scores[:, e * BLK : (e + 1) * BLK], masked_value)
                for e, ok in enumerate(all_valid[i])
            ],
            axis=1,
        )

    units = range(blocks)
    own = [slice(i * BLK, (i + 1) * BLK) for i in units]
    key_lanes, value_lanes = slice(0, DH), slice(DH, 2 * DH)
    for base in range(0, blocks, 4):
        some = range(base, base + 4)
        scores = [
            masked(nt(q_ref[own[i], :], chosen(kv_ref, i, key_lanes)) * inverse_root, i) for i in some
        ]
        prob_grads = [nt(do_ref[own[i], :], chosen(kv_ref, i, value_lanes)) for i in some]
        probs, probs_b, score_grads = [], [], []
        for score in scores:
            weights = jnp.exp(score - jnp.max(score, axis=-1, keepdims=True))
            prob = weights * (1.0 / jnp.sum(weights, axis=-1, keepdims=True))
            probs.append(prob)
            probs_b.append(prob.astype(BF16))
        for i, prob, prob_b, prob_grad in zip(some, probs, probs_b, prob_grads):
            rhs = jnp.concatenate([chosen(kv_ref, i, value_lanes), chosen(low_ref, i)], axis=1)
            mixed = nn(prob_b, rhs)
            attended = mixed[:, :DH].astype(BF16)
            att_ref[own[i], :] = attended
            t_ref[own[i], LOW:] = mixed[:, DH:].astype(BF16)
            terms = do_ref[own[i], :].astype(F32) * attended.astype(F32)
            delta = jnp.sum(terms, axis=-1, keepdims=True)
            score_grads.append((prob * (prob_grad - delta) * inverse_root).astype(BF16))
        for i, prob_b, score_grad in zip(some, probs_b, score_grads):
            rhs = jnp.concatenate([chosen(kv_ref, i, key_lanes), chosen(low_ref, i)], axis=1)
            mixed = nn(score_grad, rhs)
            dq_ref[own[i], :] = mixed[:, :DH].astype(BF16)
            t_ref[own[i], :LOW] = mixed[:, DH:].astype(BF16)
            back_ref[i, :RANK, :] = nn(query_up[:, own[i]], score_grad)
            back_ref[i, RANK:, :] = nn(grad_up[:, own[i]], prob_b)

    acc_ref[...] = acc_in[...] if which else jnp.zeros_like(acc_ref)
    acc_ref[:RANK, :rows] += nt(up_q, dq_ref[...])
    for i, starts in enumerate(all_starts):
        for e, s in enumerate(starts):
            acc_ref[RANK:, pl.ds(s, BLK)] += back_ref[i, :, e * BLK : (e + 1) * BLK]
    up_grad = adapter_scale * jnp.concatenate(
        [
            tn(low_ref[:rows, :], dq_ref[...])[0:RANK],
            tn(t_ref[:, :LOW], q_ref[...])[RANK : 2 * RANK],
            tn(t_ref[:, LOW:], do_ref[...])[2 * RANK : 3 * RANK],
        ],
        axis=0,
    )
    if which == 0:
        up_out[...] = up_grad
        return
    total = nn(acc_ref[:, :rows].astype(BF16), normed_ref[...])
    halo = jnp.zeros((2 * RANK, width), F32)
    for members, start in segments[1:]:
        halo += nn(acc_ref[RANK:, pl.ds(start, half)].astype(BF16), rows_of(members))
    sum_ref = scratch[10]
    sum_ref[:RANK, :] = total[:RANK]
    sum_ref[RANK:, :] = total[RANK:] + halo
    keep_ref[...] = sum_ref[:, half_lanes(core, width)].astype(BF16)
    send_ref[...] = sum_ref[:, half_lanes(1 - core, width)].astype(BF16)
    up_out[:, lanes_at(head)] = up_grad.astype(BF16)
    up_out[:, lanes_at(1 - head)] = up_in[...].astype(BF16)


def half_lanes(side, width):
    return pl.ds(pl.multiple_of(side * (width // 2), width // 2), width // 2)


def merge_kernel(down_ref, sibling_ref, up_ref, out_ref):
    width = down_ref.shape[1]
    out_ref[:, :width] = (down_ref[...].astype(F32) + sibling_ref[...].astype(F32)).astype(BF16)
    out_ref[:, width:] = up_ref[...]


def total_kernel(*refs):
    terms, (down_ref, up_ref) = [r[...].astype(F32) for r in refs[:-2]], refs[-2:]
    while len(terms) > 1:
        terms = [a + b for a, b in zip(terms[::2], terms[1::2])]
    width = down_ref.shape[1]
    down_ref[...] = terms[0][:, :width]
    up_ref[...] = terms[0][:, width:]


def final_kernel(own_ref, recv_ref, up_ref, out_ref, up_out):
    core, width = lax.axis_index("head"), out_ref.shape[1]
    up_out[...] = up_ref[...]
    out_ref[:, half_lanes(core, width)] = own_ref[...]
    out_ref[:, half_lanes(1 - core, width)] = recv_ref[...]


def out_kernel(order_ref, x_ref, att1_ref, att2_ref, wo1_ref, wo2_ref, base_ref, other_ref):
    rows, cols = x_ref.shape
    core = lax.axis_index("head")
    place = scatter_matrix(order_ref, rows)

    def part(side):
        span = pl.ds(pl.multiple_of(side * cols, cols), cols)
        terms = nt(att1_ref[...], wo1_ref[span, :]) + nt(att2_ref[...], wo2_ref[span, :])
        return nn(place, terms.astype(BF16))

    other_ref[...] = part(1 - core).astype(BF16)
    base_ref[...] = x_ref[...].astype(F32) + part(core)


HBM = pl.BlockSpec(memory_space=pltpu.HBM)
VMEM = pl.BlockSpec(memory_space=pltpu.VMEM)


def shape(dims, dtype=BF16):
    return jax.ShapeDtypeStruct(dims, dtype)


def call(kernel, outs, ins, scratch=(), hbm=0, flops=0, limit=None, pin=False):
    if hbm:
        ins = tuple(pltpu.with_memory_space_constraint(x, pltpu.HBM) for x in ins)
    if hbm or pin:
        outs = tuple(pltpu.VMEM(x.shape, x.dtype) for x in outs)
    return pl.pallas_call(
        kernel,
        out_shape=outs,
        in_specs=[HBM] * hbm + [VMEM] * (len(ins) - hbm),
        out_specs=(VMEM,) * len(outs),
        scratch_shapes=list(scratch),
        cost_estimate=pl.CostEstimate(flops=flops, bytes_accessed=1 << 20, transcendentals=0),
        compiler_params=pltpu.CompilerParams(vmem_limit_bytes=limit and limit * 2**20),
    )(*ins)


def swap(value, axis, step=1):
    size = lax.axis_size(axis)
    return lax.ppermute(value, axis, [(i, i ^ step) for i in range(size)])


def chain_pairs(size):
    pairs = {0: 0, size - 1: size - 1}
    for i in range(1, size - 1, 2):
        pairs[i], pairs[i + 1] = i + 1, i
    return sorted(pairs.items())


def split_kernel(a_ref, b_ref, *outs):
    rows = outs[0].shape[0]
    for out, (ref, start) in zip(outs, ((a_ref, 0), (a_ref, rows), (b_ref, 0), (b_ref, rows))):
        out[...] = ref[start : start + rows, :]


def pair_kernel(one_ref, two_ref, out_ref):
    depth = one_ref.shape[0]
    out_ref[:depth, :] = one_ref[...]
    out_ref[depth:, :] = two_ref[...]


def gather_weights(first, second, half):
    count, depth = lax.axis_size("node"), first.shape[0]
    if not split_weights():
        whole = [lax.all_gather(m, "node", axis=0, tiled=True) for m in (first, second)]
        return [whole[:1], whole[1:]], lambda node: [0], whole
    far_pairs = [(g * 4 + n, g * 4 + (n ^ (2 + g))) for g in range(2) for n in range(4)]
    near = swap(first, "node")
    far = lax.ppermute(first, ("group", "node"), far_pairs)
    far, near, _ = lax.optimization_barrier((far, near, half))
    other_far = swap(far, "group")
    pair = call(pair_kernel, (shape((2 * depth, 4 * DH)),), (near, far), limit=16)[0]
    pair = swap(pair, "sample")
    theirs = [second, pair, swap(other_far, "sample")]

    def piece_rows(node):
        group = lax.axis_index("group")
        return [jnp.bitwise_xor(node, k) * depth for k in (0, 1, 2 + group, 3 - group)]

    return [[first, near, far, other_far], theirs], piece_rows, other_far


def split_weights():
    return lax.axis_size("node") == 4 and lax.axis_size("group") == 2 and lax.axis_size("sample") == 2


def shards(
    mesh_node_state,
    cotangent,
    query_weight,
    key_weight,
    value_weight,
    output_weight,
    adapter_down_weight,
    adapter_up_weight,
    neighbour_key_blocks,
    block_node_order,
):
    _, rows, width = mesh_node_state.shape
    cols = query_weight.shape[1]
    depth = query_weight.shape[0]
    state = mesh_node_state[0]
    order = block_node_order.reshape(1, rows)
    split = split_weights()

    packed = call(
        functools.partial(pack_kernel, split),
        (shape((depth, 4 * DH)),) * 2,
        (query_weight, key_weight, value_weight, output_weight),
        [pltpu.VMEM((depth, cols), BF16)] * 3
        + [pltpu.VMEM((cols, depth), BF16), pltpu.SemaphoreType.DMA((4,))],
        hbm=4,
        limit=16,
    )
    order, _ = lax.optimization_barrier((order, packed[0]))
    order, table, down, up, x_own, normed, half, cot_own = call(
        prep_kernel,
        (
            shape((1, rows), jnp.int32),
            shape(neighbour_key_blocks.shape[::-1], jnp.int32),
            shape((3 * RANK, width)),
            shape((3 * RANK, cols)),
            shape((rows, cols)),
            shape((rows, width)),
            shape((rows // 2, width)),
            shape((rows, cols)),
        ),
        (
            order,
            state,
            cotangent[0],
            adapter_down_weight.transpose(0, 2, 1).reshape(3 * RANK, width),
            adapter_up_weight.reshape(3 * RANK, cols),
            neighbour_key_blocks.T,
        ),
        [
            pltpu.VMEM((rows, width), BF16),
            pltpu.VMEM((rows, cols), BF16),
            pltpu.SemaphoreType.DMA((6,)),
        ],
        hbm=6,
        flops=2 * rows * rows * (width + cols),
        limit=16,
    )
    pieces, piece_rows, late = gather_weights(*packed, half)
    a_own = swap(half, "node", 1)
    b_own = lax.ppermute(half, "node", chain_pairs(lax.axis_size("node")))
    cot_sib = swap(cot_own, "head")
    a_half, b_half, _ = lax.optimization_barrier((a_own, b_own, late))
    quarters = call(split_kernel, (shape((rows // 4, width)),) * 4, (a_half, b_half), limit=16)
    a_sib, a_sib2, b_sib, b_sib2 = [swap(q, "head") for q in quarters]

    shared = (
        table,
        normed,
        a_own,
        a_sib,
        a_sib2,
        b_own,
        b_sib,
        b_sib2,
        cot_own,
        cot_sib,
        down,
        up,
    )
    entries = neighbour_key_blocks.shape[1]
    scratch = [
        pltpu.VMEM((width + LOW, 4 * DH), BF16),
        pltpu.VMEM((3 * rows, 2 * DH), BF16),
        pltpu.VMEM((rows, DH), BF16),
        pltpu.VMEM((rows, DH), BF16),
        pltpu.VMEM((rows, DH), BF16),
        pltpu.VMEM((rows, 2 * LOW), BF16),
        pltpu.VMEM((rows // BLK, 2 * RANK, entries * BLK), F32),
        pltpu.VMEM((3 * RANK, 3 * rows), F32),
        pltpu.SMEM(table.shape, jnp.int32),
        pltpu.SemaphoreType.DMA,
        pltpu.VMEM((3 * RANK, width), F32),
    ]
    att1, wo1, low, acc, up1 = call(
        functools.partial(head_kernel, split, 0, piece_rows),
        (
            shape((rows, DH)),
            shape((width, DH)),
            shape((3 * rows, LOW)),
            shape((3 * RANK, 3 * rows), F32),
            shape((3 * RANK, DH), F32),
        ),
        shared + tuple(pieces[0]),
        scratch,
        limit=32,
    )
    att2, wo2, keep, send, up2 = call(
        functools.partial(head_kernel, split, 1, piece_rows),
        (
            shape((rows, DH)),
            shape((width, DH)),
            shape((3 * RANK, width // 2)),
            shape((3 * RANK, width // 2)),
            shape((3 * RANK, cols)),
        ),
        shared + (low, acc, up1) + tuple(pieces[1]),
        scratch,
        limit=32,
        flops=4 * 10**9,
    )
    received = swap(send, "head")
    base, other = call(
        out_kernel,
        (shape((rows, cols), F32), shape((rows, cols))),
        (order, x_own, att1, att2, wo1, wo2),
        flops=10**9,
        limit=16,
    )
    mesh_out = (base + swap(other, "head").astype(F32)).astype(BF16)[None]
    size = (3 * RANK, width // 2 + cols)
    lora = call(merge_kernel, (shape(size),), (keep, received, up2), limit=16)[0]
    hops = [("sample", 1 << i) for i in range(lax.axis_size("sample").bit_length() - 1)]
    count = lax.axis_size("node")
    if count != 4:
        hops += [("node", 1 << i) for i in range(count.bit_length() - 2)]
    for axis, step in hops:
        lora = (lora.astype(F32) + swap(lora, axis, step).astype(F32)).astype(BF16)
    steps = (2, 1, 3) if count == 4 else (count // 2,)
    terms = (lora, *[lax.ppermute(lora, "node", [(i, (i + k) % count) for i in range(count)]) for k in steps])
    terms, mesh_out = lax.optimization_barrier((terms, mesh_out))
    down_half, up_total = call(
        total_kernel,
        (shape((3 * RANK, width // 2), F32), shape((3 * RANK, cols), F32)),
        terms,
        limit=16,
        pin=True,
    )
    down_total, up_total = call(
        final_kernel,
        (shape((3 * RANK, width), F32), shape((3 * RANK, cols), F32)),
        (down_half, swap(down_half, "head"), up_total),
        limit=16,
    )
    down_total = down_total.reshape(3, RANK, width).transpose(0, 2, 1)
    up_total = up_total.reshape(3, RANK, cols)
    return (mesh_out, down_total, up_total)


def solution(mesh):
    in_specs = (
        P(("group", "sample"), "node", None),
        P(("group", "sample"), "node", "head"),
        P("node", "head"),
        P("node", "head"),
        P("node", "head"),
        P("head", "node"),
        P(),
        P(None, None, "head"),
        P(),
        P("node"),
    )
    out_specs = (
        P(("group", "sample"), "node", "head"),
        P("group", None, None),
        P("group", None, "head"),
    )
    return jax.shard_map(shards, mesh=mesh, in_specs=in_specs, out_specs=out_specs, check_vma=False)
```

```python
import functools
import math

import jax
import jax.numpy as jnp
from jax import lax
from jax.experimental import pallas as pl
from jax.experimental.pallas import tpu as pltpu
from jax.sharding import PartitionSpec as P

DH = 128
BLK = 128
RANK = 16
LOW = 128

adapter_scale = 0.5
masked_value = -1e30
F32 = jnp.float32
BF16 = jnp.bfloat16


def nn(a, b):
    return lax.dot_general(a, b, (((1,), (0,)), ((), ())), preferred_element_type=F32)


def nt(a, b):
    return lax.dot_general(a, b, (((1,), (1,)), ((), ())), preferred_element_type=F32)


def tn(a, b):
    return lax.dot_general(a, b, (((0,), (0,)), ((), ())), preferred_element_type=F32)


def scatter_matrix(order_ref, rows):
    local = order_ref[...] - lax.axis_index("node") * rows
    nodes = lax.broadcasted_iota(jnp.int32, (rows, rows), 0)
    return jnp.where(nodes == local, 1.0, 0.0).astype(BF16)


def head_at(split, which):
    if not split:
        return which
    return jnp.bitwise_xor(lax.rem(lax.axis_index("sample"), 2), which)


def lanes_at(index):
    if isinstance(index, int):
        return pl.ds(index * DH, DH)
    return pl.ds(pl.multiple_of(index * DH, DH), DH)


def load_all(sources, buffers, sems):
    copies = [pltpu.make_async_copy(a, b, sems.at[i]) for i, (a, b) in enumerate(zip(sources, buffers))]
    for copy in copies:
        copy.start()
    return copies


def pack_kernel(split, *refs):
    sources, outs, buffers, sems = refs[:4], refs[4:6], refs[6:-1], refs[-1]
    for copy in load_all(sources, buffers, sems):
        copy.wait()
    for which, out in enumerate(outs):
        lanes = lanes_at(head_at(split, which))
        for j, member in enumerate(buffers[:3]):
            out[:, j * DH : (j + 1) * DH] = member[:, lanes]
        out[:, 3 * DH :] = buffers[3][lanes, :].T


def prep_kernel(*refs):
    sources, outs, buffers, sems = refs[:6], refs[6:-3], refs[-3:-1], refs[-1]
    order_ref, table_ref, down_ref, up_ref, x_own_ref, normed_ref, half_ref, cot_out_ref = outs
    x_ref, cot_ref = buffers
    copies = load_all(sources, (order_ref, x_ref, cot_ref, down_ref, up_ref, table_ref), sems)
    rows = x_ref.shape[0]
    copies[0].wait()
    place = scatter_matrix(order_ref, rows)
    copies[1].wait()
    ordered = tn(place, x_ref[...])
    center = ordered - jnp.mean(ordered, axis=-1, keepdims=True)
    spread = jnp.mean(center * center, axis=-1, keepdims=True)
    normed_ref[...] = (center * lax.rsqrt(spread + 1e-05)).astype(BF16)
    start = pl.multiple_of(lax.axis_index("head") * (rows // 2), rows // 2)
    half_ref[...] = normed_ref[pl.ds(start, rows // 2), :]
    for copy in copies[2:]:
        copy.wait()
    cot_out_ref[...] = tn(place, cot_ref[...]).astype(BF16)
    cols = x_own_ref.shape[1]
    x_own_ref[...] = x_ref[:, pl.ds(pl.multiple_of(lax.axis_index("head") * cols, cols), cols)]


def head_kernel(split, which, piece_rows, *refs):
    table_vmem, normed_ref, a_own_ref, a_sib_ref, a_sib2_ref = refs[:5]
    b_own_ref, b_sib_ref, b_sib2_ref, cot_own_ref, cot_sib_ref, down_ref, up_ref = refs[5:12]
    rest, scratch = refs[12:-12], refs[-12:]
    if which == 0:
        pieces, (att_ref, wo_ref, low_ref, acc_ref, up_out) = rest[:-5], rest[-5:]
    else:
        low_ref, acc_in, up_in = rest[:3]
        pieces, (att_ref, wo_ref, keep_ref, send_ref, up_out) = rest[3:-5], rest[-5:]
    w_ref, kv_ref, q_ref, do_ref, dq_ref, t_ref, back_ref = scratch[:7]
    table_ref, table_sem = scratch[8:10]
    more_ref = scratch[11]
    if which:
        acc_ref = scratch[7]
    table_copy = pltpu.make_async_copy(table_vmem, table_ref, table_sem)
    table_copy.start()
    rows, width = normed_ref.shape
    blocks, half = rows // BLK, rows // 2
    node, core = lax.axis_index("node"), lax.axis_index("head")
    head = head_at(split, which)
    first = node * blocks
    inverse_root = 1.0 / math.sqrt(DH)

    places = piece_rows(node)
    step = width // len(places)
    for piece in pieces:
        for j in range(0, piece.shape[0], step):
            row, *places = places
            start = row if isinstance(row, int) else pl.multiple_of(row, step)
            w_ref[pl.ds(start, step), :] = piece[j : j + step, :]
    wo_ref[...] = w_ref[:width, 3 * DH :]
    w_ref[width:, :] = jnp.zeros((LOW, 4 * DH), BF16)
    for j in range(3):
        span = slice(j * RANK, (j + 1) * RANK)
        w_ref[width + j * RANK : width + (j + 1) * RANK, j * DH : (j + 1) * DH] = (
            adapter_scale * up_ref[span, lanes_at(head)]
        )

    segments = [
        ((normed_ref,), 0),
        ((a_own_ref,), pl.multiple_of(rows + core * half, half)),
        ((a_sib_ref, a_sib2_ref), pl.multiple_of(rows + (1 - core) * half, half)),
        ((b_own_ref,), pl.multiple_of(2 * rows + core * half, half)),
        ((b_sib_ref, b_sib2_ref), pl.multiple_of(2 * rows + (1 - core) * half, half)),
    ]
    def rows_of(members):
        return jnp.concatenate([m[...] for m in members], axis=0)

    if which == 0:
        for members, start in segments:
            low = nt(rows_of(members), down_ref[...]).astype(BF16)
            blank = jnp.zeros((low.shape[0], LOW - 3 * RANK), BF16)
            low_ref[pl.ds(start, low.shape[0]), :] = jnp.concatenate([low, blank], axis=1)
    for j, (members, start) in enumerate(segments):
        span = pl.ds(start, half if j else rows)
        value = jnp.concatenate([rows_of(members), low_ref[span, :]], axis=1)
        projected = nn(value, w_ref[:, (DH if j else 0) : 3 * DH]).astype(BF16)
        if j == 0:
            q_ref[...] = projected[:, :DH]
        kv_ref[span, :] = projected[:, -2 * DH :]

    def out_rows(side):
        return w_ref[pl.ds(pl.multiple_of(side * (width // 2), width // 2), width // 2), 3 * DH :]

    do_ref[...] = (
        nn(cot_own_ref[...], out_rows(core)) + nn(cot_sib_ref[...], out_rows(1 - core))
    ).astype(BF16)
    up_q = w_ref[width : width + RANK, :DH]
    up_k = w_ref[width + RANK : width + 2 * RANK, DH : 2 * DH]
    up_v = w_ref[width + 2 * RANK : width + 3 * RANK, 2 * DH : 3 * DH]
    query_up = nt(up_k, q_ref[...]).astype(BF16)
    grad_up = nt(up_v, do_ref[...]).astype(BF16)

    table_copy.wait()
    odd = lax.rem(node, 2)
    left, right = 2 - odd, 1 + odd
    all_starts, all_valid = [], []
    for i in range(blocks):
        named = [table_ref[e, first + i] for e in range(table_ref.shape[0])]
        starts, valid = [], []
        for e, c in enumerate(named):
            rel = c - first
            block = jnp.where(
                rel < 0,
                left * blocks + rel + blocks,
                jnp.where(rel >= blocks, (right - 1) * blocks + rel, rel),
            )
            starts.append(pl.multiple_of(block * BLK, BLK))
            fresh = c >= 0
            for before in named[:e]:
                fresh = jnp.logical_and(fresh, c != before)
            valid.append(fresh)
        all_starts.append(starts)
        all_valid.append(valid)

    def chosen(ref, i, lanes=slice(None)):
        return jnp.concatenate([ref[pl.ds(s, BLK), lanes] for s in all_starts[i]], axis=0)

    def masked(scores, i):
        return jnp.concatenate(
            [
                jnp.where(ok, scores[:, e * BLK : (e + 1) * BLK], masked_value)
                for e, ok in enumerate(all_valid[i])
            ],
            axis=1,
        )

    units = range(blocks)
    own = [slice(i * BLK, (i + 1) * BLK) for i in units]
    key_lanes, value_lanes = slice(0, DH), slice(DH, 2 * DH)
    for base in range(0, blocks, 4):
        some = range(base, base + 4)
        scores = [
            masked(nt(q_ref[own[i], :], chosen(kv_ref, i, key_lanes)) * inverse_root, i) for i in some
        ]
        prob_grads = [nt(do_ref[own[i], :], chosen(kv_ref, i, value_lanes)) for i in some]
        probs, probs_b, score_grads = [], [], []
        for score in scores:
            weights = jnp.exp(score - jnp.max(score, axis=-1, keepdims=True))
            prob = weights * (1.0 / jnp.sum(weights, axis=-1, keepdims=True))
            probs.append(prob)
            probs_b.append(prob.astype(BF16))
        for i, prob, prob_b, prob_grad in zip(some, probs, probs_b, prob_grads):
            rhs = jnp.concatenate([chosen(kv_ref, i, value_lanes), chosen(low_ref, i)], axis=1)
            mixed = nn(prob_b, rhs)
            attended = mixed[:, :DH].astype(BF16)
            att_ref[own[i], :] = attended
            t_ref[own[i], LOW:] = mixed[:, DH:].astype(BF16)
            terms = do_ref[own[i], :].astype(F32) * attended.astype(F32)
            delta = jnp.sum(terms, axis=-1, keepdims=True)
            score_grads.append((prob * (prob_grad - delta) * inverse_root).astype(BF16))
        for i, prob_b, score_grad in zip(some, probs_b, score_grads):
            rhs = jnp.concatenate([chosen(kv_ref, i, key_lanes), chosen(low_ref, i)], axis=1)
            mixed = nn(score_grad, rhs)
            dq_ref[own[i], :] = mixed[:, :DH].astype(BF16)
            t_ref[own[i], :LOW] = mixed[:, DH:].astype(BF16)
            back_ref[i, :RANK, :] = nn(query_up[:, own[i]], score_grad)
            back_ref[i, RANK:, :] = nn(grad_up[:, own[i]], prob_b)

    acc_ref[...] = acc_in[...] if which else jnp.zeros_like(acc_ref)
    acc_ref[:RANK, :rows] += nt(up_q, dq_ref[...])
    half_acc = [acc_ref.at[RANK:, :], more_ref]
    more_ref[...] = jnp.zeros_like(more_ref)
    for e in range(len(all_starts[0])):
        for i, starts in enumerate(all_starts):
            half_acc[i % 2][:, pl.ds(starts[e], BLK)] += back_ref[i, :, e * BLK : (e + 1) * BLK]
    acc_ref[RANK:, :] += more_ref[...]
    up_grad = adapter_scale * jnp.concatenate(
        [
            tn(low_ref[:rows, :], dq_ref[...])[0:RANK],
            tn(t_ref[:, :LOW], q_ref[...])[RANK : 2 * RANK],
            tn(t_ref[:, LOW:], do_ref[...])[2 * RANK : 3 * RANK],
        ],
        axis=0,
    )
    if which == 0:
        up_out[...] = up_grad
        return
    total = nn(acc_ref[:, :rows].astype(BF16), normed_ref[...])
    halo = jnp.zeros((2 * RANK, width), F32)
    for members, start in segments[1:]:
        halo += nn(acc_ref[RANK:, pl.ds(start, half)].astype(BF16), rows_of(members))
    sum_ref = scratch[10]
    sum_ref[:RANK, :] = total[:RANK]
    sum_ref[RANK:, :] = total[RANK:] + halo
    keep_ref[...] = sum_ref[:, half_lanes(core, width)].astype(BF16)
    send_ref[...] = sum_ref[:, half_lanes(1 - core, width)].astype(BF16)
    up_out[:, lanes_at(head)] = up_grad.astype(BF16)
    up_out[:, lanes_at(1 - head)] = up_in[...].astype(BF16)


def half_lanes(side, width):
    return pl.ds(pl.multiple_of(side * (width // 2), width // 2), width // 2)


def merge_kernel(down_ref, sibling_ref, up_ref, out_ref):
    width = down_ref.shape[1]
    out_ref[:, :width] = (down_ref[...].astype(F32) + sibling_ref[...].astype(F32)).astype(BF16)
    out_ref[:, width:] = up_ref[...]


def total_kernel(*refs):
    terms, (down_ref, up_ref) = [r[...].astype(F32) for r in refs[:-2]], refs[-2:]
    while len(terms) > 1:
        terms = [a + b for a, b in zip(terms[::2], terms[1::2])]
    width = down_ref.shape[1]
    down_ref[...] = terms[0][:, :width]
    up_ref[...] = terms[0][:, width:]


def final_kernel(own_ref, recv_ref, up_ref, out_ref, up_out):
    core, width = lax.axis_index("head"), out_ref.shape[1]
    up_out[...] = up_ref[...]
    out_ref[:, half_lanes(core, width)] = own_ref[...]
    out_ref[:, half_lanes(1 - core, width)] = recv_ref[...]


def out_kernel(order_ref, x_ref, att1_ref, att2_ref, wo1_ref, wo2_ref, base_ref, other_ref):
    rows, cols = x_ref.shape
    core = lax.axis_index("head")
    place = scatter_matrix(order_ref, rows)

    def part(side):
        span = pl.ds(pl.multiple_of(side * cols, cols), cols)
        terms = nt(att1_ref[...], wo1_ref[span, :]) + nt(att2_ref[...], wo2_ref[span, :])
        return nn(place, terms.astype(BF16))

    other_ref[...] = part(1 - core).astype(BF16)
    base_ref[...] = x_ref[...].astype(F32) + part(core)


HBM = pl.BlockSpec(memory_space=pltpu.HBM)
VMEM = pl.BlockSpec(memory_space=pltpu.VMEM)


def shape(dims, dtype=BF16):
    return jax.ShapeDtypeStruct(dims, dtype)


def call(kernel, outs, ins, scratch=(), hbm=0, flops=0, limit=None, pin=False):
    if hbm:
        ins = tuple(pltpu.with_memory_space_constraint(x, pltpu.HBM) for x in ins)
    if hbm or pin:
        outs = tuple(pltpu.VMEM(x.shape, x.dtype) for x in outs)
    return pl.pallas_call(
        kernel,
        out_shape=outs,
        in_specs=[HBM] * hbm + [VMEM] * (len(ins) - hbm),
        out_specs=(VMEM,) * len(outs),
        scratch_shapes=list(scratch),
        cost_estimate=pl.CostEstimate(flops=flops, bytes_accessed=1 << 20, transcendentals=0),
        compiler_params=pltpu.CompilerParams(vmem_limit_bytes=limit and limit * 2**20),
    )(*ins)


def swap(value, axis, step=1):
    size = lax.axis_size(axis)
    return lax.ppermute(value, axis, [(i, i ^ step) for i in range(size)])


def chain_pairs(size):
    pairs = {0: 0, size - 1: size - 1}
    for i in range(1, size - 1, 2):
        pairs[i], pairs[i + 1] = i + 1, i
    return sorted(pairs.items())


def split_kernel(a_ref, b_ref, *outs):
    rows = outs[0].shape[0]
    for out, (ref, start) in zip(outs, ((a_ref, 0), (a_ref, rows), (b_ref, 0), (b_ref, rows))):
        out[...] = ref[start : start + rows, :]


def pair_kernel(one_ref, two_ref, out_ref):
    depth = one_ref.shape[0]
    out_ref[:depth, :] = one_ref[...]
    out_ref[depth:, :] = two_ref[...]


def gather_weights(first, second, half):
    count, depth = lax.axis_size("node"), first.shape[0]
    if not split_weights():
        whole = [lax.all_gather(m, "node", axis=0, tiled=True) for m in (first, second)]
        return [whole[:1], whole[1:]], lambda node: [0], whole
    far_pairs = [(g * 4 + n, g * 4 + (n ^ (3 - g))) for g in range(2) for n in range(4)]
    near = swap(first, "node")
    far = lax.ppermute(first, ("group", "node"), far_pairs)
    far, near, _ = lax.optimization_barrier((far, near, half))
    other_far = swap(far, "group")
    pair = call(pair_kernel, (shape((2 * depth, 4 * DH)),), (near, far), limit=16)[0]
    pair = swap(pair, "sample")
    theirs = [second, pair, swap(other_far, "sample")]

    def piece_rows(node):
        group = lax.axis_index("group")
        return [jnp.bitwise_xor(node, k) * depth for k in (0, 1, 3 - group, 2 + group)]

    return [[first, near, far, other_far], theirs], piece_rows, other_far


def split_weights():
    return lax.axis_size("node") == 4 and lax.axis_size("group") == 2 and lax.axis_size("sample") == 2


def shards(
    mesh_node_state,
    cotangent,
    query_weight,
    key_weight,
    value_weight,
    output_weight,
    adapter_down_weight,
    adapter_up_weight,
    neighbour_key_blocks,
    block_node_order,
):
    _, rows, width = mesh_node_state.shape
    cols = query_weight.shape[1]
    depth = query_weight.shape[0]
    state = mesh_node_state[0]
    order = block_node_order.reshape(1, rows)
    split = split_weights()

    packed = call(
        functools.partial(pack_kernel, split),
        (shape((depth, 4 * DH)),) * 2,
        (query_weight, key_weight, value_weight, output_weight),
        [pltpu.VMEM((depth, cols), BF16)] * 3
        + [pltpu.VMEM((cols, depth), BF16), pltpu.SemaphoreType.DMA((4,))],
        hbm=4,
        limit=16,
    )
    order, _ = lax.optimization_barrier((order, packed[0]))
    order, table, down, up, x_own, normed, half, cot_own = call(
        prep_kernel,
        (
            shape((1, rows), jnp.int32),
            shape(neighbour_key_blocks.shape[::-1], jnp.int32),
            shape((3 * RANK, width)),
            shape((3 * RANK, cols)),
            shape((rows, cols)),
            shape((rows, width)),
            shape((rows // 2, width)),
            shape((rows, cols)),
        ),
        (
            order,
            state,
            cotangent[0],
            adapter_down_weight.transpose(0, 2, 1).reshape(3 * RANK, width),
            adapter_up_weight.reshape(3 * RANK, cols),
            neighbour_key_blocks.T,
        ),
        [
            pltpu.VMEM((rows, width), BF16),
            pltpu.VMEM((rows, cols), BF16),
            pltpu.SemaphoreType.DMA((6,)),
        ],
        hbm=6,
        flops=2 * rows * rows * (width + cols),
        limit=16,
    )
    pieces, piece_rows, late = gather_weights(*packed, half)
    a_own = swap(half, "node", 1)
    b_own = lax.ppermute(half, "node", chain_pairs(lax.axis_size("node")))
    cot_sib = swap(cot_own, "head")
    a_half, b_half, _ = lax.optimization_barrier((a_own, b_own, late))
    quarters = call(split_kernel, (shape((rows // 4, width)),) * 4, (a_half, b_half), limit=16)
    a_sib, a_sib2, b_sib, b_sib2 = [swap(q, "head") for q in quarters]

    shared = (
        table,
        normed,
        a_own,
        a_sib,
        a_sib2,
        b_own,
        b_sib,
        b_sib2,
        cot_own,
        cot_sib,
        down,
        up,
    )
    entries = neighbour_key_blocks.shape[1]
    scratch = [
        pltpu.VMEM((width + LOW, 4 * DH), BF16),
        pltpu.VMEM((3 * rows, 2 * DH), BF16),
        pltpu.VMEM((rows, DH), BF16),
        pltpu.VMEM((rows, DH), BF16),
        pltpu.VMEM((rows, DH), BF16),
        pltpu.VMEM((rows, 2 * LOW), BF16),
        pltpu.VMEM((rows // BLK, 2 * RANK, entries * BLK), F32),
        pltpu.VMEM((3 * RANK, 3 * rows), F32),
        pltpu.SMEM(table.shape, jnp.int32),
        pltpu.SemaphoreType.DMA,
        pltpu.VMEM((3 * RANK, width), F32),
        pltpu.VMEM((2 * RANK, 3 * rows), F32),
    ]
    att1, wo1, low, acc, up1 = call(
        functools.partial(head_kernel, split, 0, piece_rows),
        (
            shape((rows, DH)),
            shape((width, DH)),
            shape((3 * rows, LOW)),
            shape((3 * RANK, 3 * rows), F32),
            shape((3 * RANK, DH), F32),
        ),
        shared + tuple(pieces[0]),
        scratch,
        limit=32,
    )
    att2, wo2, keep, send, up2 = call(
        functools.partial(head_kernel, split, 1, piece_rows),
        (
            shape((rows, DH)),
            shape((width, DH)),
            shape((3 * RANK, width // 2)),
            shape((3 * RANK, width // 2)),
            shape((3 * RANK, cols)),
        ),
        shared + (low, acc, up1) + tuple(pieces[1]),
        scratch,
        limit=32,
        flops=4 * 10**9,
    )
    received = swap(send, "head")
    base, other = call(
        out_kernel,
        (shape((rows, cols), F32), shape((rows, cols))),
        (order, x_own, att1, att2, wo1, wo2),
        flops=10**9,
        limit=16,
    )
    mesh_out = (base + swap(other, "head").astype(F32)).astype(BF16)[None]
    size = (3 * RANK, width // 2 + cols)
    lora = call(merge_kernel, (shape(size),), (keep, received, up2), limit=16)[0]
    hops = [("sample", 1 << i) for i in range(lax.axis_size("sample").bit_length() - 1)]
    count = lax.axis_size("node")
    if count != 4:
        hops += [("node", 1 << i) for i in range(count.bit_length() - 2)]
    for axis, step in hops:
        lora = (lora.astype(F32) + swap(lora, axis, step).astype(F32)).astype(BF16)
    steps = (1, 2, 3) if count == 4 else (count // 2,)
    terms = (lora, *[lax.ppermute(lora, "node", [(i, (i + k) % count) for i in range(count)]) for k in steps])
    terms, mesh_out = lax.optimization_barrier((terms, mesh_out))
    down_half, up_total = call(
        total_kernel,
        (shape((3 * RANK, width // 2), F32), shape((3 * RANK, cols), F32)),
        terms,
        limit=16,
        pin=True,
    )
    down_total, up_total = call(
        final_kernel,
        (shape((3 * RANK, width), F32), shape((3 * RANK, cols), F32)),
        (down_half, swap(down_half, "head"), up_total),
        limit=16,
    )
    down_total = down_total.reshape(3, RANK, width).transpose(0, 2, 1)
    up_total = up_total.reshape(3, RANK, cols)
    return (mesh_out, down_total, up_total)


def solution(mesh):
    in_specs = (
        P(("group", "sample"), "node", None),
        P(("group", "sample"), "node", "head"),
        P("node", "head"),
        P("node", "head"),
        P("node", "head"),
        P("head", "node"),
        P(),
        P(None, None, "head"),
        P(),
        P("node"),
    )
    out_specs = (
        P(("group", "sample"), "node", "head"),
        P("group", None, None),
        P("group", None, "head"),
    )
    return jax.shard_map(shards, mesh=mesh, in_specs=in_specs, out_specs=out_specs, check_vma=False)
```

```python
import functools
import math

import jax
import jax.numpy as jnp
from jax import lax
from jax.experimental import pallas as pl
from jax.experimental.pallas import tpu as pltpu
from jax.sharding import PartitionSpec as P

DH = 128
BLK = 128
RANK = 16
LOW = 128

adapter_scale = 0.5
masked_value = -1e30
F32 = jnp.float32
BF16 = jnp.bfloat16


def nn(a, b):
    return lax.dot_general(a, b, (((1,), (0,)), ((), ())), preferred_element_type=F32)


def nt(a, b):
    return lax.dot_general(a, b, (((1,), (1,)), ((), ())), preferred_element_type=F32)


def tn(a, b):
    return lax.dot_general(a, b, (((0,), (0,)), ((), ())), preferred_element_type=F32)


def scatter_matrix(order_ref, rows):
    local = order_ref[...] - lax.axis_index("node") * rows
    nodes = lax.broadcasted_iota(jnp.int32, (rows, rows), 0)
    return jnp.where(nodes == local, 1.0, 0.0).astype(BF16)


def head_at(split, which):
    if not split:
        return which
    return jnp.bitwise_xor(lax.rem(lax.axis_index("sample"), 2), which)


def lanes_at(index):
    if isinstance(index, int):
        return pl.ds(index * DH, DH)
    return pl.ds(pl.multiple_of(index * DH, DH), DH)


def load_all(sources, buffers, sems):
    copies = [pltpu.make_async_copy(a, b, sems.at[i]) for i, (a, b) in enumerate(zip(sources, buffers))]
    for copy in copies:
        copy.start()
    return copies


def pack_kernel(split, *refs):
    sources, outs, buffers, sems = refs[:4], refs[4:6], refs[6:-1], refs[-1]
    for copy in load_all(sources, buffers, sems):
        copy.wait()
    for which, out in enumerate(outs):
        lanes = lanes_at(head_at(split, which))
        for j, member in enumerate(buffers[:3]):
            out[:, j * DH : (j + 1) * DH] = member[:, lanes]
        out[:, 3 * DH :] = buffers[3][lanes, :].T


def prep_kernel(*refs):
    sources, outs, buffers, sems = refs[:6], refs[6:-3], refs[-3:-1], refs[-1]
    order_ref, table_ref, down_ref, up_ref, x_own_ref, normed_ref, half_ref, cot_out_ref = outs
    x_ref, cot_ref = buffers
    copies = load_all(sources, (order_ref, x_ref, cot_ref, down_ref, up_ref, table_ref), sems)
    rows = x_ref.shape[0]
    copies[0].wait()
    place = scatter_matrix(order_ref, rows)
    copies[1].wait()
    ordered = tn(place, x_ref[...])
    center = ordered - jnp.mean(ordered, axis=-1, keepdims=True)
    spread = jnp.mean(center * center, axis=-1, keepdims=True)
    normed_ref[...] = (center * lax.rsqrt(spread + 1e-05)).astype(BF16)
    start = pl.multiple_of(lax.axis_index("head") * (rows // 2), rows // 2)
    half_ref[...] = normed_ref[pl.ds(start, rows // 2), :]
    for copy in copies[2:]:
        copy.wait()
    cot_out_ref[...] = tn(place, cot_ref[...]).astype(BF16)
    cols = x_own_ref.shape[1]
    x_own_ref[...] = x_ref[:, pl.ds(pl.multiple_of(lax.axis_index("head") * cols, cols), cols)]


def head_kernel(split, which, piece_rows, *refs):
    table_vmem, normed_ref, a_own_ref, a_sib_ref, a_sib2_ref = refs[:5]
    b_own_ref, b_sib_ref, b_sib2_ref, cot_own_ref, cot_sib_ref, down_ref, up_ref = refs[5:12]
    rest, scratch = refs[12:-12], refs[-12:]
    if which == 0:
        pieces, (att_ref, wo_ref, low_ref, acc_ref, up_out) = rest[:-5], rest[-5:]
    else:
        low_ref, acc_in, up_in = rest[:3]
        pieces, (att_ref, wo_ref, keep_ref, send_ref, up_out) = rest[3:-5], rest[-5:]
    w_ref, kv_ref, q_ref, do_ref, dq_ref, t_ref, back_ref = scratch[:7]
    table_ref, table_sem = scratch[8:10]
    more_ref = scratch[11]
    if which:
        acc_ref = scratch[7]
    table_copy = pltpu.make_async_copy(table_vmem, table_ref, table_sem)
    table_copy.start()
    rows, width = normed_ref.shape
    blocks, half = rows // BLK, rows // 2
    node, core = lax.axis_index("node"), lax.axis_index("head")
    head = head_at(split, which)
    first = node * blocks
    inverse_root = 1.0 / math.sqrt(DH)

    places = piece_rows(node)
    step = width // len(places)
    for piece in pieces:
        for j in range(0, piece.shape[0], step):
            row, *places = places
            start = row if isinstance(row, int) else pl.multiple_of(row, step)
            w_ref[pl.ds(start, step), :] = piece[j : j + step, :]
    wo_ref[...] = w_ref[:width, 3 * DH :]
    w_ref[width:, :] = jnp.zeros((LOW, 4 * DH), BF16)
    for j in range(3):
        span = slice(j * RANK, (j + 1) * RANK)
        w_ref[width + j * RANK : width + (j + 1) * RANK, j * DH : (j + 1) * DH] = (
            adapter_scale * up_ref[span, lanes_at(head)]
        )

    segments = [
        ((normed_ref,), 0),
        ((a_own_ref,), pl.multiple_of(rows + core * half, half)),
        ((a_sib_ref, a_sib2_ref), pl.multiple_of(rows + (1 - core) * half, half)),
        ((b_own_ref,), pl.multiple_of(2 * rows + core * half, half)),
        ((b_sib_ref, b_sib2_ref), pl.multiple_of(2 * rows + (1 - core) * half, half)),
    ]
    def rows_of(members):
        return jnp.concatenate([m[...] for m in members], axis=0)

    if which == 0:
        for members, start in segments:
            low = nt(rows_of(members), down_ref[...]).astype(BF16)
            blank = jnp.zeros((low.shape[0], LOW - 3 * RANK), BF16)
            low_ref[pl.ds(start, low.shape[0]), :] = jnp.concatenate([low, blank], axis=1)
    for j, (members, start) in enumerate(segments):
        span = pl.ds(start, half if j else rows)
        value = jnp.concatenate([rows_of(members), low_ref[span, :]], axis=1)
        projected = nn(value, w_ref[:, (DH if j else 0) : 3 * DH]).astype(BF16)
        if j == 0:
            q_ref[...] = projected[:, :DH]
        kv_ref[span, :] = projected[:, -2 * DH :]

    def out_rows(side):
        return w_ref[pl.ds(pl.multiple_of(side * (width // 2), width // 2), width // 2), 3 * DH :]

    do_ref[...] = (
        nn(cot_own_ref[...], out_rows(core)) + nn(cot_sib_ref[...], out_rows(1 - core))
    ).astype(BF16)
    up_q = w_ref[width : width + RANK, :DH]
    up_k = w_ref[width + RANK : width + 2 * RANK, DH : 2 * DH]
    up_v = w_ref[width + 2 * RANK : width + 3 * RANK, 2 * DH : 3 * DH]
    query_up = nt(up_k, q_ref[...]).astype(BF16)
    grad_up = nt(up_v, do_ref[...]).astype(BF16)

    table_copy.wait()
    odd = lax.rem(node, 2)
    left, right = 2 - odd, 1 + odd
    all_starts, all_valid = [], []
    for i in range(blocks):
        named = [table_ref[e, first + i] for e in range(table_ref.shape[0])]
        starts, valid = [], []
        for e, c in enumerate(named):
            rel = c - first
            block = jnp.where(
                rel < 0,
                left * blocks + rel + blocks,
                jnp.where(rel >= blocks, (right - 1) * blocks + rel, rel),
            )
            starts.append(pl.multiple_of(block * BLK, BLK))
            fresh = c >= 0
            for before in named[:e]:
                fresh = jnp.logical_and(fresh, c != before)
            valid.append(fresh)
        all_starts.append(starts)
        all_valid.append(valid)

    def chosen(ref, i, lanes=slice(None)):
        return jnp.concatenate([ref[pl.ds(s, BLK), lanes] for s in all_starts[i]], axis=0)

    def masked(scores, i):
        return jnp.concatenate(
            [
                jnp.where(ok, scores[:, e * BLK : (e + 1) * BLK], masked_value)
                for e, ok in enumerate(all_valid[i])
            ],
            axis=1,
        )

    units = range(blocks)
    own = [slice(i * BLK, (i + 1) * BLK) for i in units]
    key_lanes, value_lanes = slice(0, DH), slice(DH, 2 * DH)
    for base in range(0, blocks, 4):
        some = range(base, base + 4)
        scores = [
            masked(nt(q_ref[own[i], :], chosen(kv_ref, i, key_lanes)) * inverse_root, i) for i in some
        ]
        prob_grads = [nt(do_ref[own[i], :], chosen(kv_ref, i, value_lanes)) for i in some]
        probs, probs_b, score_grads = [], [], []
        for score in scores:
            weights = jnp.exp(score - jnp.max(score, axis=-1, keepdims=True))
            prob = weights * (1.0 / jnp.sum(weights, axis=-1, keepdims=True))
            probs.append(prob)
            probs_b.append(prob.astype(BF16))
        for i, prob, prob_b, prob_grad in zip(some, probs, probs_b, prob_grads):
            rhs = jnp.concatenate([chosen(kv_ref, i, value_lanes), chosen(low_ref, i)], axis=1)
            mixed = nn(prob_b, rhs)
            attended = mixed[:, :DH].astype(BF16)
            att_ref[own[i], :] = attended
            t_ref[own[i], LOW:] = mixed[:, DH:].astype(BF16)
            terms = do_ref[own[i], :].astype(F32) * attended.astype(F32)
            delta = jnp.sum(terms, axis=-1, keepdims=True)
            score_grads.append((prob * (prob_grad - delta) * inverse_root).astype(BF16))
        for i, prob_b, score_grad in zip(some, probs_b, score_grads):
            rhs = jnp.concatenate([chosen(kv_ref, i, key_lanes), chosen(low_ref, i)], axis=1)
            mixed = nn(score_grad, rhs)
            dq_ref[own[i], :] = mixed[:, :DH].astype(BF16)
            t_ref[own[i], :LOW] = mixed[:, DH:].astype(BF16)
            back_ref[i, :RANK, :] = nn(query_up[:, own[i]], score_grad)
            back_ref[i, RANK:, :] = nn(grad_up[:, own[i]], prob_b)

    acc_ref[...] = acc_in[...] if which else jnp.zeros_like(acc_ref)
    acc_ref[:RANK, :rows] += nt(up_q, dq_ref[...])
    half_acc = [acc_ref.at[RANK:, :], more_ref]
    more_ref[...] = jnp.zeros_like(more_ref)
    for e in range(len(all_starts[0])):
        for i, starts in enumerate(all_starts):
            half_acc[i % 2][:, pl.ds(starts[e], BLK)] += back_ref[i, :, e * BLK : (e + 1) * BLK]
    acc_ref[RANK:, :] += more_ref[...]
    up_grad = adapter_scale * jnp.concatenate(
        [
            tn(low_ref[:rows, :], dq_ref[...])[0:RANK],
            tn(t_ref[:, :LOW], q_ref[...])[RANK : 2 * RANK],
            tn(t_ref[:, LOW:], do_ref[...])[2 * RANK : 3 * RANK],
        ],
        axis=0,
    )
    if which == 0:
        up_out[...] = up_grad
        return
    total = nn(acc_ref[:, :rows].astype(BF16), normed_ref[...])
    halo = jnp.zeros((2 * RANK, width), F32)
    for members, start in segments[1:]:
        halo += nn(acc_ref[RANK:, pl.ds(start, half)].astype(BF16), rows_of(members))
    sum_ref = scratch[10]
    sum_ref[:RANK, :] = total[:RANK]
    sum_ref[RANK:, :] = total[RANK:] + halo
    keep_ref[...] = sum_ref[:, half_lanes(core, width)].astype(BF16)
    send_ref[...] = sum_ref[:, half_lanes(1 - core, width)].astype(BF16)
    up_out[:, lanes_at(head)] = up_grad.astype(BF16)
    up_out[:, lanes_at(1 - head)] = up_in[...].astype(BF16)


def half_lanes(side, width):
    return pl.ds(pl.multiple_of(side * (width // 2), width // 2), width // 2)


def merge_kernel(down_ref, sibling_ref, up_ref, out_ref):
    width = down_ref.shape[1]
    out_ref[:, :width] = (down_ref[...].astype(F32) + sibling_ref[...].astype(F32)).astype(BF16)
    out_ref[:, width:] = up_ref[...]


def total_kernel(*refs):
    terms, (down_ref, up_ref) = [r[...].astype(F32) for r in refs[:-2]], refs[-2:]
    while len(terms) > 1:
        terms = [a + b for a, b in zip(terms, terms[len(terms) // 2 :])]
    width = down_ref.shape[1]
    down_ref[...] = terms[0][:, :width]
    up_ref[...] = terms[0][:, width:]


def final_kernel(own_ref, recv_ref, up_ref, out_ref, up_out):
    core, width = lax.axis_index("head"), out_ref.shape[1]
    up_out[...] = up_ref[...]
    out_ref[:, half_lanes(core, width)] = own_ref[...]
    out_ref[:, half_lanes(1 - core, width)] = recv_ref[...]


def out_kernel(order_ref, x_ref, att1_ref, att2_ref, wo1_ref, wo2_ref, base_ref, other_ref):
    rows, cols = x_ref.shape
    core = lax.axis_index("head")
    place = scatter_matrix(order_ref, rows)

    def part(side):
        span = pl.ds(pl.multiple_of(side * cols, cols), cols)
        terms = nt(att1_ref[...], wo1_ref[span, :]) + nt(att2_ref[...], wo2_ref[span, :])
        return nn(place, terms.astype(BF16))

    other_ref[...] = part(1 - core).astype(BF16)
    base_ref[...] = x_ref[...].astype(F32) + part(core)


HBM = pl.BlockSpec(memory_space=pltpu.HBM)
VMEM = pl.BlockSpec(memory_space=pltpu.VMEM)


def shape(dims, dtype=BF16):
    return jax.ShapeDtypeStruct(dims, dtype)


def call(kernel, outs, ins, scratch=(), hbm=0, flops=0, limit=None, pin=False):
    if hbm:
        ins = tuple(pltpu.with_memory_space_constraint(x, pltpu.HBM) for x in ins)
    if hbm or pin:
        outs = tuple(pltpu.VMEM(x.shape, x.dtype) for x in outs)
    return pl.pallas_call(
        kernel,
        out_shape=outs,
        in_specs=[HBM] * hbm + [VMEM] * (len(ins) - hbm),
        out_specs=(VMEM,) * len(outs),
        scratch_shapes=list(scratch),
        cost_estimate=pl.CostEstimate(flops=flops, bytes_accessed=1 << 20, transcendentals=0),
        compiler_params=pltpu.CompilerParams(vmem_limit_bytes=limit and limit * 2**20),
    )(*ins)


def swap(value, axis, step=1):
    size = lax.axis_size(axis)
    return lax.ppermute(value, axis, [(i, i ^ step) for i in range(size)])


def chain_pairs(size):
    pairs = {0: 0, size - 1: size - 1}
    for i in range(1, size - 1, 2):
        pairs[i], pairs[i + 1] = i + 1, i
    return sorted(pairs.items())


def split_kernel(a_ref, b_ref, *outs):
    rows = outs[0].shape[0]
    for out, (ref, start) in zip(outs, ((a_ref, 0), (a_ref, rows), (b_ref, 0), (b_ref, rows))):
        out[...] = ref[start : start + rows, :]


def pair_kernel(one_ref, two_ref, out_ref):
    depth = one_ref.shape[0]
    out_ref[:depth, :] = one_ref[...]
    out_ref[depth:, :] = two_ref[...]


def gather_weights(first, second, half):
    count, depth = lax.axis_size("node"), first.shape[0]
    if not split_weights():
        whole = [lax.all_gather(m, "node", axis=0, tiled=True) for m in (first, second)]
        return [whole[:1], whole[1:]], lambda node: [0], whole
    far_pairs = [(g * 4 + n, g * 4 + (n ^ (3 - g))) for g in range(2) for n in range(4)]
    near = swap(first, "node")
    far = lax.ppermute(first, ("group", "node"), far_pairs)
    far, near, _ = lax.optimization_barrier((far, near, half))
    other_far = swap(far, "group")
    pair = call(pair_kernel, (shape((2 * depth, 4 * DH)),), (near, far), limit=16)[0]
    pair = swap(pair, "sample")
    theirs = [second, pair, swap(other_far, "sample")]

    def piece_rows(node):
        group = lax.axis_index("group")
        return [jnp.bitwise_xor(node, k) * depth for k in (0, 1, 3 - group, 2 + group)]

    return [[first, near, far, other_far], theirs], piece_rows, other_far


def split_weights():
    return lax.axis_size("node") == 4 and lax.axis_size("group") == 2 and lax.axis_size("sample") == 2


def shards(
    mesh_node_state,
    cotangent,
    query_weight,
    key_weight,
    value_weight,
    output_weight,
    adapter_down_weight,
    adapter_up_weight,
    neighbour_key_blocks,
    block_node_order,
):
    _, rows, width = mesh_node_state.shape
    cols = query_weight.shape[1]
    depth = query_weight.shape[0]
    state = mesh_node_state[0]
    order = block_node_order.reshape(1, rows)
    split = split_weights()

    packed = call(
        functools.partial(pack_kernel, split),
        (shape((depth, 4 * DH)),) * 2,
        (query_weight, key_weight, value_weight, output_weight),
        [pltpu.VMEM((depth, cols), BF16)] * 3
        + [pltpu.VMEM((cols, depth), BF16), pltpu.SemaphoreType.DMA((4,))],
        hbm=4,
        limit=16,
    )
    order, _ = lax.optimization_barrier((order, packed[0]))
    order, table, down, up, x_own, normed, half, cot_own = call(
        prep_kernel,
        (
            shape((1, rows), jnp.int32),
            shape(neighbour_key_blocks.shape[::-1], jnp.int32),
            shape((3 * RANK, width)),
            shape((3 * RANK, cols)),
            shape((rows, cols)),
            shape((rows, width)),
            shape((rows // 2, width)),
            shape((rows, cols)),
        ),
        (
            order,
            state,
            cotangent[0],
            adapter_down_weight.transpose(0, 2, 1).reshape(3 * RANK, width),
            adapter_up_weight.reshape(3 * RANK, cols),
            neighbour_key_blocks.T,
        ),
        [
            pltpu.VMEM((rows, width), BF16),
            pltpu.VMEM((rows, cols), BF16),
            pltpu.SemaphoreType.DMA((6,)),
        ],
        hbm=6,
        flops=2 * rows * rows * (width + cols),
        limit=16,
    )
    pieces, piece_rows, late = gather_weights(*packed, half)
    a_own = swap(half, "node", 1)
    b_own = lax.ppermute(half, "node", chain_pairs(lax.axis_size("node")))
    cot_sib = swap(cot_own, "head")
    a_half, b_half, _ = lax.optimization_barrier((a_own, b_own, late))
    quarters = call(split_kernel, (shape((rows // 4, width)),) * 4, (a_half, b_half), limit=16)
    a_sib, a_sib2, b_sib, b_sib2 = [swap(q, "head") for q in quarters]

    shared = (
        table,
        normed,
        a_own,
        a_sib,
        a_sib2,
        b_own,
        b_sib,
        b_sib2,
        cot_own,
        cot_sib,
        down,
        up,
    )
    entries = neighbour_key_blocks.shape[1]
    scratch = [
        pltpu.VMEM((width + LOW, 4 * DH), BF16),
        pltpu.VMEM((3 * rows, 2 * DH), BF16),
        pltpu.VMEM((rows, DH), BF16),
        pltpu.VMEM((rows, DH), BF16),
        pltpu.VMEM((rows, DH), BF16),
        pltpu.VMEM((rows, 2 * LOW), BF16),
        pltpu.VMEM((rows // BLK, 2 * RANK, entries * BLK), F32),
        pltpu.VMEM((3 * RANK, 3 * rows), F32),
        pltpu.SMEM(table.shape, jnp.int32),
        pltpu.SemaphoreType.DMA,
        pltpu.VMEM((3 * RANK, width), F32),
        pltpu.VMEM((2 * RANK, 3 * rows), F32),
    ]
    att1, wo1, low, acc, up1 = call(
        functools.partial(head_kernel, split, 0, piece_rows),
        (
            shape((rows, DH)),
            shape((width, DH)),
            shape((3 * rows, LOW)),
            shape((3 * RANK, 3 * rows), F32),
            shape((3 * RANK, DH), F32),
        ),
        shared + tuple(pieces[0]),
        scratch,
        limit=32,
    )
    att2, wo2, keep, send, up2 = call(
        functools.partial(head_kernel, split, 1, piece_rows),
        (
            shape((rows, DH)),
            shape((width, DH)),
            shape((3 * RANK, width // 2)),
            shape((3 * RANK, width // 2)),
            shape((3 * RANK, cols)),
        ),
        shared + (low, acc, up1) + tuple(pieces[1]),
        scratch,
        limit=32,
        flops=4 * 10**9,
    )
    received = swap(send, "head")
    base, other = call(
        out_kernel,
        (shape((rows, cols), F32), shape((rows, cols))),
        (order, x_own, att1, att2, wo1, wo2),
        flops=10**9,
        limit=16,
    )
    mesh_out = (base + swap(other, "head").astype(F32)).astype(BF16)[None]
    size = (3 * RANK, width // 2 + cols)
    lora = call(merge_kernel, (shape(size),), (keep, received, up2), limit=16)[0]
    hops = [("sample", 1 << i) for i in range(lax.axis_size("sample").bit_length() - 1)]
    count = lax.axis_size("node")
    if count != 4:
        hops += [("node", 1 << i) for i in range(count.bit_length() - 2)]
    for axis, step in hops:
        lora = (lora.astype(F32) + swap(lora, axis, step).astype(F32)).astype(BF16)
    steps = (1, 2, 3) if count == 4 else (count // 2,)
    terms = (lora, *[lax.ppermute(lora, "node", [(i, (i + k) % count) for i in range(count)]) for k in steps])
    terms, mesh_out = lax.optimization_barrier((terms, mesh_out))
    down_half, up_total = call(
        total_kernel,
        (shape((3 * RANK, width // 2), F32), shape((3 * RANK, cols), F32)),
        terms,
        limit=16,
        pin=True,
    )
    down_total, up_total = call(
        final_kernel,
        (shape((3 * RANK, width), F32), shape((3 * RANK, cols), F32)),
        (down_half, swap(down_half, "head"), up_total),
        limit=16,
    )
    down_total = down_total.reshape(3, RANK, width).transpose(0, 2, 1)
    up_total = up_total.reshape(3, RANK, cols)
    return (mesh_out, down_total, up_total)


def solution(mesh):
    in_specs = (
        P(("group", "sample"), "node", None),
        P(("group", "sample"), "node", "head"),
        P("node", "head"),
        P("node", "head"),
        P("node", "head"),
        P("head", "node"),
        P(),
        P(None, None, "head"),
        P(),
        P("node"),
    )
    out_specs = (
        P(("group", "sample"), "node", "head"),
        P("group", None, None),
        P("group", None, "head"),
    )
    return jax.shard_map(shards, mesh=mesh, in_specs=in_specs, out_specs=out_specs, check_vma=False)
```

```python
import functools
import math

import jax
import jax.numpy as jnp
from jax import lax
from jax.experimental import pallas as pl
from jax.experimental.pallas import tpu as pltpu
from jax.sharding import PartitionSpec as P

DH = 128
BLK = 128
RANK = 16
LOW = 128

adapter_scale = 0.5
masked_value = -1e30
F32 = jnp.float32
BF16 = jnp.bfloat16


def nn(a, b):
    return lax.dot_general(a, b, (((1,), (0,)), ((), ())), preferred_element_type=F32)


def nt(a, b):
    return lax.dot_general(a, b, (((1,), (1,)), ((), ())), preferred_element_type=F32)


def tn(a, b):
    return lax.dot_general(a, b, (((0,), (0,)), ((), ())), preferred_element_type=F32)


def scatter_matrix(order_ref, rows):
    local = order_ref[...] - lax.axis_index("node") * rows
    nodes = lax.broadcasted_iota(jnp.int32, (rows, rows), 0)
    return jnp.where(nodes == local, 1.0, 0.0).astype(BF16)


def head_at(split, which):
    if not split:
        return which
    return jnp.bitwise_xor(lax.rem(lax.axis_index("sample"), 2), which)


def lanes_at(index):
    if isinstance(index, int):
        return pl.ds(index * DH, DH)
    return pl.ds(pl.multiple_of(index * DH, DH), DH)


def load_all(sources, buffers, sems):
    copies = [pltpu.make_async_copy(a, b, sems.at[i]) for i, (a, b) in enumerate(zip(sources, buffers))]
    for copy in copies:
        copy.start()
    return copies


def pack_kernel(split, *refs):
    sources, outs, out_weight, sems = refs[:4], refs[4:6], refs[6], refs[7]
    last = pltpu.make_async_copy(sources[3], out_weight, sems.at[6])
    last.start()
    copies = []
    for which, out in enumerate(outs):
        lanes = lanes_at(head_at(split, which))
        for j, member in enumerate(sources[:3]):
            target = out.at[:, pl.ds(j * DH, DH)]
            copies.append(pltpu.make_async_copy(member.at[:, lanes], target, sems.at[which * 3 + j]))
            copies[-1].start()
    last.wait()
    for which, out in enumerate(outs):
        out[:, 3 * DH :] = out_weight[lanes_at(head_at(split, which)), :].T
    for copy in copies:
        copy.wait()


def prep_kernel(*refs):
    sources, outs, buffers, sems = refs[:6], refs[6:-3], refs[-3:-1], refs[-1]
    order_ref, table_ref, down_ref, up_ref, x_own_ref, normed_ref, half_ref, cot_out_ref = outs
    x_ref, cot_ref = buffers
    copies = load_all(sources, (order_ref, x_ref, cot_ref, down_ref, up_ref, table_ref), sems)
    rows = x_ref.shape[0]
    copies[0].wait()
    place = scatter_matrix(order_ref, rows)
    copies[1].wait()
    ordered = tn(place, x_ref[...])
    center = ordered - jnp.mean(ordered, axis=-1, keepdims=True)
    spread = jnp.mean(center * center, axis=-1, keepdims=True)
    normed_ref[...] = (center * lax.rsqrt(spread + 1e-05)).astype(BF16)
    start = pl.multiple_of(lax.axis_index("head") * (rows // 2), rows // 2)
    half_ref[...] = normed_ref[pl.ds(start, rows // 2), :]
    for copy in copies[2:]:
        copy.wait()
    cot_out_ref[...] = tn(place, cot_ref[...]).astype(BF16)
    cols = x_own_ref.shape[1]
    x_own_ref[...] = x_ref[:, pl.ds(pl.multiple_of(lax.axis_index("head") * cols, cols), cols)]


def head_kernel(split, which, piece_rows, *refs):
    table_vmem, normed_ref, a_own_ref, a_sib_ref, a_sib2_ref = refs[:5]
    b_own_ref, b_sib_ref, b_sib2_ref, cot_own_ref, cot_sib_ref, down_ref, up_ref = refs[5:12]
    rest, scratch = refs[12:-12], refs[-12:]
    if which == 0:
        pieces, (att_ref, wo_ref, low_ref, acc_ref, up_out) = rest[:-5], rest[-5:]
    else:
        low_ref, acc_in, up_in = rest[:3]
        pieces, (att_ref, wo_ref, keep_ref, send_ref, up_out) = rest[3:-5], rest[-5:]
    w_ref, kv_ref, q_ref, do_ref, dq_ref, t_ref, back_ref = scratch[:7]
    table_ref, table_sem = scratch[8:10]
    more_ref = scratch[11]
    if which:
        acc_ref = scratch[7]
    table_copy = pltpu.make_async_copy(table_vmem, table_ref, table_sem)
    table_copy.start()
    rows, width = normed_ref.shape
    blocks, half = rows // BLK, rows // 2
    node, core = lax.axis_index("node"), lax.axis_index("head")
    head = head_at(split, which)
    first = node * blocks
    inverse_root = 1.0 / math.sqrt(DH)

    places = piece_rows(node)
    step = width // len(places)
    for piece in pieces:
        for j in range(0, piece.shape[0], step):
            row, *places = places
            start = row if isinstance(row, int) else pl.multiple_of(row, step)
            w_ref[pl.ds(start, step), :] = piece[j : j + step, :]
    wo_ref[...] = w_ref[:width, 3 * DH :]
    w_ref[width:, :] = jnp.zeros((LOW, 4 * DH), BF16)
    for j in range(3):
        span = slice(j * RANK, (j + 1) * RANK)
        w_ref[width + j * RANK : width + (j + 1) * RANK, j * DH : (j + 1) * DH] = (
            adapter_scale * up_ref[span, lanes_at(head)]
        )

    segments = [
        ((normed_ref,), 0),
        ((a_own_ref,), pl.multiple_of(rows + core * half, half)),
        ((a_sib_ref, a_sib2_ref), pl.multiple_of(rows + (1 - core) * half, half)),
        ((b_own_ref,), pl.multiple_of(2 * rows + core * half, half)),
        ((b_sib_ref, b_sib2_ref), pl.multiple_of(2 * rows + (1 - core) * half, half)),
    ]
    def rows_of(members):
        return jnp.concatenate([m[...] for m in members], axis=0)

    if which == 0:
        for members, start in segments:
            low = nt(rows_of(members), down_ref[...]).astype(BF16)
            blank = jnp.zeros((low.shape[0], LOW - 3 * RANK), BF16)
            low_ref[pl.ds(start, low.shape[0]), :] = jnp.concatenate([low, blank], axis=1)
    for j, (members, start) in enumerate(segments):
        span = pl.ds(start, half if j else rows)
        value = jnp.concatenate([rows_of(members), low_ref[span, :]], axis=1)
        projected = nn(value, w_ref[:, (DH if j else 0) : 3 * DH]).astype(BF16)
        if j == 0:
            q_ref[...] = projected[:, :DH]
        kv_ref[span, :] = projected[:, -2 * DH :]

    def out_rows(side):
        return w_ref[pl.ds(pl.multiple_of(side * (width // 2), width // 2), width // 2), 3 * DH :]

    do_ref[...] = (
        nn(cot_own_ref[...], out_rows(core)) + nn(cot_sib_ref[...], out_rows(1 - core))
    ).astype(BF16)
    up_q = w_ref[width : width + RANK, :DH]
    up_k = w_ref[width + RANK : width + 2 * RANK, DH : 2 * DH]
    up_v = w_ref[width + 2 * RANK : width + 3 * RANK, 2 * DH : 3 * DH]
    query_up = nt(up_k, q_ref[...]).astype(BF16)
    grad_up = nt(up_v, do_ref[...]).astype(BF16)

    table_copy.wait()
    odd = lax.rem(node, 2)
    left, right = 2 - odd, 1 + odd
    all_starts, all_valid = [], []
    for i in range(blocks):
        named = [table_ref[e, first + i] for e in range(table_ref.shape[0])]
        starts, valid = [], []
        for e, c in enumerate(named):
            rel = c - first
            block = jnp.where(
                rel < 0,
                left * blocks + rel + blocks,
                jnp.where(rel >= blocks, (right - 1) * blocks + rel, rel),
            )
            starts.append(pl.multiple_of(block * BLK, BLK))
            fresh = c >= 0
            for before in named[:e]:
                fresh = jnp.logical_and(fresh, c != before)
            valid.append(fresh)
        all_starts.append(starts)
        all_valid.append(valid)

    def chosen(ref, i, lanes=slice(None)):
        return jnp.concatenate([ref[pl.ds(s, BLK), lanes] for s in all_starts[i]], axis=0)

    def masked(scores, i):
        return jnp.concatenate(
            [
                jnp.where(ok, scores[:, e * BLK : (e + 1) * BLK], masked_value)
                for e, ok in enumerate(all_valid[i])
            ],
            axis=1,
        )

    units = range(blocks)
    own = [slice(i * BLK, (i + 1) * BLK) for i in units]
    key_lanes, value_lanes = slice(0, DH), slice(DH, 2 * DH)
    for base in range(0, blocks, 4):
        some = range(base, base + 4)
        scores = [
            masked(nt(q_ref[own[i], :], chosen(kv_ref, i, key_lanes)) * inverse_root, i) for i in some
        ]
        prob_grads = [nt(do_ref[own[i], :], chosen(kv_ref, i, value_lanes)) for i in some]
        probs, probs_b, score_grads = [], [], []
        for score in scores:
            weights = jnp.exp(score - jnp.max(score, axis=-1, keepdims=True))
            prob = weights * (1.0 / jnp.sum(weights, axis=-1, keepdims=True))
            probs.append(prob)
            probs_b.append(prob.astype(BF16))
        for i, prob, prob_b, prob_grad in zip(some, probs, probs_b, prob_grads):
            rhs = jnp.concatenate([chosen(kv_ref, i, value_lanes), chosen(low_ref, i)], axis=1)
            mixed = nn(prob_b, rhs)
            attended = mixed[:, :DH].astype(BF16)
            att_ref[own[i], :] = attended
            t_ref[own[i], LOW:] = mixed[:, DH:].astype(BF16)
            terms = do_ref[own[i], :].astype(F32) * attended.astype(F32)
            delta = jnp.sum(terms, axis=-1, keepdims=True)
            score_grads.append((prob * (prob_grad - delta) * inverse_root).astype(BF16))
        for i, prob_b, score_grad in zip(some, probs_b, score_grads):
            rhs = jnp.concatenate([chosen(kv_ref, i, key_lanes), chosen(low_ref, i)], axis=1)
            mixed = nn(score_grad, rhs)
            dq_ref[own[i], :] = mixed[:, :DH].astype(BF16)
            t_ref[own[i], :LOW] = mixed[:, DH:].astype(BF16)
            back_ref[i, :RANK, :] = nn(query_up[:, own[i]], score_grad)
            back_ref[i, RANK:, :] = nn(grad_up[:, own[i]], prob_b)

    acc_ref[...] = acc_in[...] if which else jnp.zeros_like(acc_ref)
    acc_ref[:RANK, :rows] += nt(up_q, dq_ref[...])
    half_acc = [acc_ref.at[RANK:, :], more_ref]
    more_ref[...] = jnp.zeros_like(more_ref)
    for e in range(len(all_starts[0])):
        for i, starts in enumerate(all_starts):
            half_acc[i % 2][:, pl.ds(starts[e], BLK)] += back_ref[i, :, e * BLK : (e + 1) * BLK]
    acc_ref[RANK:, :] += more_ref[...]
    up_grad = adapter_scale * jnp.concatenate(
        [
            tn(low_ref[:rows, :], dq_ref[...])[0:RANK],
            tn(t_ref[:, :LOW], q_ref[...])[RANK : 2 * RANK],
            tn(t_ref[:, LOW:], do_ref[...])[2 * RANK : 3 * RANK],
        ],
        axis=0,
    )
    if which == 0:
        up_out[...] = up_grad
        return
    total = nn(acc_ref[:, :rows].astype(BF16), normed_ref[...])
    halo = jnp.zeros((2 * RANK, width), F32)
    for members, start in segments[1:]:
        halo += nn(acc_ref[RANK:, pl.ds(start, half)].astype(BF16), rows_of(members))
    sum_ref = scratch[10]
    sum_ref[:RANK, :] = total[:RANK]
    sum_ref[RANK:, :] = total[RANK:] + halo
    keep_ref[...] = sum_ref[:, half_lanes(core, width)].astype(BF16)
    send_ref[...] = sum_ref[:, half_lanes(1 - core, width)].astype(BF16)
    up_out[:, lanes_at(head)] = up_grad.astype(BF16)
    up_out[:, lanes_at(1 - head)] = up_in[...].astype(BF16)


def half_lanes(side, width):
    return pl.ds(pl.multiple_of(side * (width // 2), width // 2), width // 2)


def merge_kernel(down_ref, sibling_ref, up_ref, out_ref):
    width = down_ref.shape[1]
    out_ref[:, :width] = (down_ref[...].astype(F32) + sibling_ref[...].astype(F32)).astype(BF16)
    out_ref[:, width:] = up_ref[...]


def total_kernel(*refs):
    terms, (down_ref, up_ref) = [r[...].astype(F32) for r in refs[:-2]], refs[-2:]
    while len(terms) > 1:
        terms = [a + b for a, b in zip(terms, terms[len(terms) // 2 :])]
    width = down_ref.shape[1]
    down_ref[...] = terms[0][:, :width]
    up_ref[...] = terms[0][:, width:]


def final_kernel(own_ref, recv_ref, up_ref, out_ref, up_out):
    core, width = lax.axis_index("head"), out_ref.shape[1]
    up_out[...] = up_ref[...]
    out_ref[:, half_lanes(core, width)] = own_ref[...]
    out_ref[:, half_lanes(1 - core, width)] = recv_ref[...]


def out_kernel(order_ref, x_ref, att1_ref, att2_ref, wo1_ref, wo2_ref, base_ref, other_ref):
    rows, cols = x_ref.shape
    core = lax.axis_index("head")
    place = scatter_matrix(order_ref, rows)

    def part(side):
        span = pl.ds(pl.multiple_of(side * cols, cols), cols)
        terms = nt(att1_ref[...], wo1_ref[span, :]) + nt(att2_ref[...], wo2_ref[span, :])
        return nn(place, terms.astype(BF16))

    other_ref[...] = part(1 - core).astype(BF16)
    base_ref[...] = x_ref[...].astype(F32) + part(core)


HBM = pl.BlockSpec(memory_space=pltpu.HBM)
VMEM = pl.BlockSpec(memory_space=pltpu.VMEM)


def shape(dims, dtype=BF16):
    return jax.ShapeDtypeStruct(dims, dtype)


def call(kernel, outs, ins, scratch=(), hbm=0, flops=0, limit=None, pin=False):
    if hbm:
        ins = tuple(pltpu.with_memory_space_constraint(x, pltpu.HBM) for x in ins)
    if hbm or pin:
        outs = tuple(pltpu.VMEM(x.shape, x.dtype) for x in outs)
    return pl.pallas_call(
        kernel,
        out_shape=outs,
        in_specs=[HBM] * hbm + [VMEM] * (len(ins) - hbm),
        out_specs=(VMEM,) * len(outs),
        scratch_shapes=list(scratch),
        cost_estimate=pl.CostEstimate(flops=flops, bytes_accessed=1 << 20, transcendentals=0),
        compiler_params=pltpu.CompilerParams(vmem_limit_bytes=limit and limit * 2**20),
    )(*ins)


def swap(value, axis, step=1):
    size = lax.axis_size(axis)
    return lax.ppermute(value, axis, [(i, i ^ step) for i in range(size)])


def chain_pairs(size):
    pairs = {0: 0, size - 1: size - 1}
    for i in range(1, size - 1, 2):
        pairs[i], pairs[i + 1] = i + 1, i
    return sorted(pairs.items())


def split_kernel(a_ref, b_ref, *outs):
    rows = outs[0].shape[0]
    for out, (ref, start) in zip(outs, ((a_ref, 0), (a_ref, rows), (b_ref, 0), (b_ref, rows))):
        out[...] = ref[start : start + rows, :]


def pair_kernel(one_ref, two_ref, out_ref):
    depth = one_ref.shape[0]
    out_ref[:depth, :] = one_ref[...]
    out_ref[depth:, :] = two_ref[...]


def gather_weights(first, second, half):
    count, depth = lax.axis_size("node"), first.shape[0]
    if not split_weights():
        whole = [lax.all_gather(m, "node", axis=0, tiled=True) for m in (first, second)]
        return [whole[:1], whole[1:]], lambda node: [0], whole
    far_pairs = [(g * 4 + n, g * 4 + (n ^ (3 - g))) for g in range(2) for n in range(4)]
    near = swap(first, "node")
    far = lax.ppermute(first, ("group", "node"), far_pairs)
    far, near, _ = lax.optimization_barrier((far, near, half))
    other_far = swap(far, "group")
    pair = call(pair_kernel, (shape((2 * depth, 4 * DH)),), (near, far), limit=16)[0]
    pair = swap(pair, "sample")
    theirs = [second, pair, swap(other_far, "sample")]

    def piece_rows(node):
        group = lax.axis_index("group")
        return [jnp.bitwise_xor(node, k) * depth for k in (0, 1, 3 - group, 2 + group)]

    return [[first, near, far, other_far], theirs], piece_rows, other_far


def split_weights():
    return lax.axis_size("node") == 4 and lax.axis_size("group") == 2 and lax.axis_size("sample") == 2


def shards(
    mesh_node_state,
    cotangent,
    query_weight,
    key_weight,
    value_weight,
    output_weight,
    adapter_down_weight,
    adapter_up_weight,
    neighbour_key_blocks,
    block_node_order,
):
    _, rows, width = mesh_node_state.shape
    cols = query_weight.shape[1]
    depth = query_weight.shape[0]
    state = mesh_node_state[0]
    order = block_node_order.reshape(1, rows)
    split = split_weights()

    packed = call(
        functools.partial(pack_kernel, split),
        (shape((depth, 4 * DH)),) * 2,
        (query_weight, key_weight, value_weight, output_weight),
        [pltpu.VMEM((cols, depth), BF16), pltpu.SemaphoreType.DMA((7,))],
        hbm=4,
        limit=16,
    )
    order, _ = lax.optimization_barrier((order, packed[0]))
    order, table, down, up, x_own, normed, half, cot_own = call(
        prep_kernel,
        (
            shape((1, rows), jnp.int32),
            shape(neighbour_key_blocks.shape[::-1], jnp.int32),
            shape((3 * RANK, width)),
            shape((3 * RANK, cols)),
            shape((rows, cols)),
            shape((rows, width)),
            shape((rows // 2, width)),
            shape((rows, cols)),
        ),
        (
            order,
            state,
            cotangent[0],
            adapter_down_weight.transpose(0, 2, 1).reshape(3 * RANK, width),
            adapter_up_weight.reshape(3 * RANK, cols),
            neighbour_key_blocks.T,
        ),
        [
            pltpu.VMEM((rows, width), BF16),
            pltpu.VMEM((rows, cols), BF16),
            pltpu.SemaphoreType.DMA((6,)),
        ],
        hbm=6,
        flops=2 * rows * rows * (width + cols),
        limit=16,
    )
    pieces, piece_rows, late = gather_weights(*packed, half)
    a_own = swap(half, "node", 1)
    b_own = lax.ppermute(half, "node", chain_pairs(lax.axis_size("node")))
    cot_sib = swap(cot_own, "head")
    a_half, b_half, _ = lax.optimization_barrier((a_own, b_own, late))
    quarters = call(split_kernel, (shape((rows // 4, width)),) * 4, (a_half, b_half), limit=16)
    a_sib, a_sib2, b_sib, b_sib2 = [swap(q, "head") for q in quarters]

    shared = (
        table,
        normed,
        a_own,
        a_sib,
        a_sib2,
        b_own,
        b_sib,
        b_sib2,
        cot_own,
        cot_sib,
        down,
        up,
    )
    entries = neighbour_key_blocks.shape[1]
    scratch = [
        pltpu.VMEM((width + LOW, 4 * DH), BF16),
        pltpu.VMEM((3 * rows, 2 * DH), BF16),
        pltpu.VMEM((rows, DH), BF16),
        pltpu.VMEM((rows, DH), BF16),
        pltpu.VMEM((rows, DH), BF16),
        pltpu.VMEM((rows, 2 * LOW), BF16),
        pltpu.VMEM((rows // BLK, 2 * RANK, entries * BLK), F32),
        pltpu.VMEM((3 * RANK, 3 * rows), F32),
        pltpu.SMEM(table.shape, jnp.int32),
        pltpu.SemaphoreType.DMA,
        pltpu.VMEM((3 * RANK, width), F32),
        pltpu.VMEM((2 * RANK, 3 * rows), F32),
    ]
    att1, wo1, low, acc, up1 = call(
        functools.partial(head_kernel, split, 0, piece_rows),
        (
            shape((rows, DH)),
            shape((width, DH)),
            shape((3 * rows, LOW)),
            shape((3 * RANK, 3 * rows), F32),
            shape((3 * RANK, DH), F32),
        ),
        shared + tuple(pieces[0]),
        scratch,
        limit=32,
    )
    att2, wo2, keep, send, up2 = call(
        functools.partial(head_kernel, split, 1, piece_rows),
        (
            shape((rows, DH)),
            shape((width, DH)),
            shape((3 * RANK, width // 2)),
            shape((3 * RANK, width // 2)),
            shape((3 * RANK, cols)),
        ),
        shared + (low, acc, up1) + tuple(pieces[1]),
        scratch,
        limit=32,
        flops=4 * 10**9,
    )
    received = swap(send, "head")
    base, other = call(
        out_kernel,
        (shape((rows, cols), F32), shape((rows, cols))),
        (order, x_own, att1, att2, wo1, wo2),
        flops=10**9,
        limit=16,
    )
    mesh_out = (base + swap(other, "head").astype(F32)).astype(BF16)[None]
    size = (3 * RANK, width // 2 + cols)
    lora = call(merge_kernel, (shape(size),), (keep, received, up2), limit=16)[0]
    hops = [("sample", 1 << i) for i in range(lax.axis_size("sample").bit_length() - 1)]
    count = lax.axis_size("node")
    if count != 4:
        hops += [("node", 1 << i) for i in range(count.bit_length() - 2)]
    for axis, step in hops:
        lora = (lora.astype(F32) + swap(lora, axis, step).astype(F32)).astype(BF16)
    steps = (1, 2, 3) if count == 4 else (count // 2,)
    terms = (lora, *[lax.ppermute(lora, "node", [(i, (i + k) % count) for i in range(count)]) for k in steps])
    terms, mesh_out = lax.optimization_barrier((terms, mesh_out))
    down_half, up_total = call(
        total_kernel,
        (shape((3 * RANK, width // 2), F32), shape((3 * RANK, cols), F32)),
        terms,
        limit=16,
        pin=True,
    )
    down_total, up_total = call(
        final_kernel,
        (shape((3 * RANK, width), F32), shape((3 * RANK, cols), F32)),
        (down_half, swap(down_half, "head"), up_total),
        limit=16,
    )
    down_total = down_total.reshape(3, RANK, width).transpose(0, 2, 1)
    up_total = up_total.reshape(3, RANK, cols)
    return (mesh_out, down_total, up_total)


def solution(mesh):
    in_specs = (
        P(("group", "sample"), "node", None),
        P(("group", "sample"), "node", "head"),
        P("node", "head"),
        P("node", "head"),
        P("node", "head"),
        P("head", "node"),
        P(),
        P(None, None, "head"),
        P(),
        P("node"),
    )
    out_specs = (
        P(("group", "sample"), "node", "head"),
        P("group", None, None),
        P("group", None, "head"),
    )
    return jax.shard_map(shards, mesh=mesh, in_specs=in_specs, out_specs=out_specs, check_vma=False)
```
